32 devices in a mesh: shard: 2 (over x), ctx: 4 (over z), tp: 4 (over y, core).
Axes of the slice: x: 2, y: 2, z: 4, core: 2. Of those that a mesh axis runs over, the one named last changes fastest.
Arguments:
- tokens: bfloat16 [1536, 1536], P(('shard', 'ctx')), may hold values from -6 to 6
- cotangent: bfloat16 [1536, 1536], P(('shard', 'ctx')), may hold values from -6 to 6
- valid_mask: int32 [1536], P(('shard', 'ctx')), may hold values 0 or 1
- lengths: int32 [2, 3], P('shard'), may hold values from 1 to 576, 768 in all within a row
- deal: int32 [2, 8], P('shard'), may hold values from 0 to 7, as said below
- attn_gain: bfloat16 [1536], replicated, may hold values from 0.5 to 1.5
- w_query: bfloat16 [1536, 1536], P(('shard', 'ctx'), 'tp'), may hold values from -0.15625 to 0.15625
- w_key: bfloat16 [1536, 1536], P(('shard', 'ctx'), 'tp'), may hold values from -0.15625 to 0.15625
- w_value: bfloat16 [1536, 1536], P(('shard', 'ctx'), 'tp'), may hold values from -0.15625 to 0.15625
- w_house: bfloat16 [1536, 1536], P(('shard', 'ctx'), 'tp'), may hold values from -0.15625 to 0.15625
- w_beta: bfloat16 [1536, 12], P(('shard', 'ctx'), 'tp'), may hold values from -0.15625 to 0.15625
- conv_taps: bfloat16 [4, 1536], P(None, 'tp'), may hold values from -3 to 3
- w_out: bfloat16 [1536, 1536], P('tp', ('shard', 'ctx')), may hold values from -0.625 to 0.625
- mlp_gain: bfloat16 [1536], replicated, may hold values from 0.5 to 1.5
- w_gate: bfloat16 [1536, 4096], P(('shard', 'ctx'), 'tp'), may hold values from -0.15625 to 0.15625
- w_up: bfloat16 [1536, 4096], P(('shard', 'ctx'), 'tp'), may hold values from -0.15625 to 0.15625
- w_down: bfloat16 [4096, 1536], P('tp', ('shard', 'ctx')), may hold values from -0.09375 to 0.09375
Outputs:
- output: bfloat16 [1536, 1536], P(('shard', 'ctx'))
- d_tokens: bfloat16 [1536, 1536], P(('shard', 'ctx'))
- d_attn_gain: float32 [1536], replicated
- d_query: float32 [1536, 1536], P(('shard', 'ctx'), 'tp')
- d_key: float32 [1536, 1536], P(('shard', 'ctx'), 'tp')
- d_value: float32 [1536, 1536], P(('shard', 'ctx'), 'tp')
- d_house: float32 [1536, 1536], P(('shard', 'ctx'), 'tp')
- d_beta: float32 [1536, 12], P(('shard', 'ctx'), 'tp')
- d_taps: float32 [4, 1536], P(None, 'tp')
- d_out: float32 [1536, 1536], P('tp', ('shard', 'ctx'))
- d_mlp_gain: float32 [1536], replicated
- d_gate: float32 [1536, 4096], P(('shard', 'ctx'), 'tp')
- d_up: float32 [1536, 4096], P(('shard', 'ctx'), 'tp')
- d_down: float32 [4096, 1536], P('tp', ('shard', 'ctx'))
- rms_stats: float32 [4], replicated
The draws below stay inside these ranges and needn't reach their ends.
Inputs may be any that keep to these rules, and one draw needn't show every extreme that they name: `deal`: each row is a permutation of 0 .. 7; for every p, of the causal pieces p and 7 - p exactly one holds a given piece under 8 // 2. `lengths`: each row sums to 768.
All inputs are finite; a program needn't handle non-finite values. No bound on the sum of `valid_mask` on one device may be relied on, other than what follows from the above.
Results may differ from the reference program's by a relative error of at most 0.015.
Values may be sent and summed in bfloat16 or wider, within the bound.
No kernel may reach another device: no remote copies, remote signals or barrier semaphores. Data moves between devices by JAX's collectives and lax.ppermute only.
A program may use at most 256 MiB of HBM per device.

```python
import math
import jax
import jax.numpy as jnp
import numpy as np
from jax import lax

D = 1536
HEADS = 12
HD = 128
FF = 4096
CONV = 4
PIECE = 96
SEQS = 3
NPIECE = 8
ROW = 768
GROUPS = 2
TOKENS = 1536
N_CTX = 4


def draw_deal(key, part):
    group_keys = jax.random.split(key, GROUPS)

    def one_group(group_key):
        first_key, second_key, third_key = jax.random.split(group_key, 3)
        low_half = jax.random.permutation(first_key, N_CTX).astype(jnp.int32)
        high_half = N_CTX + jax.random.permutation(second_key, N_CTX).astype(jnp.int32)
        flips = jax.random.randint(third_key, (N_CTX,), 0, 2)
        early = jnp.where(flips == 1, high_half, low_half)
        later = jnp.where(flips == 1, low_half, high_half)
        return jnp.concatenate([early, jnp.flip(later, 0)])
    return jax.vmap(one_group)(group_keys).astype(jnp.int32)


def plant(values, key, smallest, top_value):
    longest = values.shape.index(max(values.shape))
    spots = []
    for shift in (0, 1):
        where = [jax.random.randint(jax.random.fold_in(key, axis), (), 0, length) for axis, length in enumerate(values.shape)]
        where[longest] = (where[longest] + shift) % values.shape[longest]
        spots.append(tuple(where))
    return values.at[spots[0]].set(smallest).at[spots[1]].set(top_value)


def level_of(own_key, extent, cuts, least, high):
    def one(axis_at, blocks):
        draws = jax.random.uniform(jax.random.fold_in(jax.random.fold_in(own_key, 6), axis_at), (blocks,), jnp.float32, least / len(cuts), high / len(cuts))
        return jnp.repeat(jnp.exp(draws), extent[axis_at] // blocks).reshape((-1,) + (1,) * (len(extent) - axis_at - 1))

    loudness = one(*cuts[0])
    for cut in cuts[1:]:
        loudness = loudness * one(*cut)
    return loudness


def profile(count, total, reach, skew):
    weights = [(1 << 20) // math.isqrt(rank ** skew) + 1 for rank in range(2, count + 1)]
    surplus, given = total - reach - (count - 1), [1] * (count - 1)
    while surplus > 0:
        candidates = [i for i in range(count - 1) if given[i] < reach]
        whole, left = sum([weights[i] for i in candidates]), surplus
        for i in candidates:
            addition = min(reach - given[i], max(1, left * weights[i] // whole), surplus)
            given[i] = given[i] + addition
            surplus = surplus - addition
    return np.array([reach] + given)


def uneven(own_key, count, total, reach, lean):
    if count == 2:
        one = jax.random.randint(own_key, (), max(1, total - reach), min(reach, total - 1) + 1)
        return jnp.stack([one, total - one])
    sizes = jnp.asarray(profile(count, total, reach, lean), jnp.int32)
    twos = (count - 1) // 2
    source_of, taker = sizes[1:1 + 2 * twos:2], sizes[2:2 + 2 * twos:2]
    room = jnp.minimum(source_of - 1, reach - taker)
    passed = jax.random.randint(jax.random.fold_in(own_key, 1), (twos,), 0, 1 << 20) % (room + 1)
    sizes = sizes.at[1:1 + 2 * twos:2].set(source_of - passed).at[2:2 + 2 * twos:2].set(taker + passed)
    return sizes[jax.random.permutation(jax.random.fold_in(own_key, 2), count)]


def normal_values(own_key, extent, deviation, reach, shards=(), kind=jnp.bfloat16):
    level = level_of(own_key, extent, shards, -0.22, 0.18) if shards else 1.0
    result = jax.random.normal(own_key, extent, jnp.float32) * deviation * level
    return jnp.minimum(jnp.maximum(result, -reach), reach).astype(kind)


def setup_inputs(seed: int = 0) -> dict:
    key_of = jax.random.split(jax.random.key(seed), 18)
    return {
        "tokens": normal_values(key_of[0], (TOKENS, D), 1.0, 6.0, ((0, 8),)),
        "cotangent": normal_values(key_of[1], (TOKENS, D), 1.0, 6.0, ((0, 8),)),
        "valid_mask": plant((jax.random.randint(key_of[2], (TOKENS,), 0, 4) < 3).astype(jnp.int32), jax.random.fold_in(key_of[2], 1), 0, 1),
        "lengths": jax.vmap(lambda own: uneven(own, SEQS, ROW, ROW - ROW // 4, 2))(jax.random.split(key_of[3], GROUPS)).reshape((GROUPS, SEQS)).astype(jnp.int32),
        "deal": draw_deal(jax.random.fold_in(key_of[17], 71), 0),
        "attn_gain": jnp.clip(1.0 + 0.1 * jax.random.normal(key_of[5], (D,), jnp.float32), 0.5, 1.5).astype(jnp.bfloat16),
        "w_query": normal_values(key_of[6], (D, HEADS * HD), D ** -0.5, 0.15625, ((0, 8), (1, 4))),
        "w_key": normal_values(key_of[7], (D, HEADS * HD), D ** -0.5, 0.15625, ((0, 8), (1, 4))),
        "w_value": normal_values(key_of[8], (D, HEADS * HD), D ** -0.5, 0.15625, ((0, 8), (1, 4))),
        "w_house": normal_values(key_of[9], (D, HEADS * HD), D ** -0.5, 0.15625, ((0, 8), (1, 4))),
        "w_beta": normal_values(key_of[10], (D, HEADS), D ** -0.5, 0.15625, ((0, 8), (1, 4))),
        "conv_taps": normal_values(key_of[11], (CONV, HEADS * HD), 0.5, 3.0, ((1, 4),)),
        "w_out": normal_values(key_of[12], (HEADS * HD, D), (HEADS * HD // 16) ** -0.5, 0.625, ((0, 4), (1, 8))),
        "mlp_gain": jnp.clip(1.0 + 0.1 * jax.random.normal(key_of[13], (D,), jnp.float32), 0.5, 1.5).astype(jnp.bfloat16),
        "w_gate": normal_values(key_of[14], (D, FF), D ** -0.5, 0.15625, ((0, 8), (1, 4))),
        "w_up": normal_values(key_of[15], (D, FF), D ** -0.5, 0.15625, ((0, 8), (1, 4))),
        "w_down": normal_values(key_of[16], (FF, D), FF ** -0.5, 0.09375, ((0, 4), (1, 8))),
    }


EPS = 1e-06
NEG = -1e+30

@jax.custom_vjp
def low(v):
    return lax.optimization_barrier(v.astype(jnp.bfloat16)).astype(jnp.float32)

@jax.custom_vjp
def low_back(v):
    return v

def low_keep(v):
    return (low(v), None)

def low_pass(kept, grad):
    return (grad,)

def back_keep(v):
    return (v, None)

def back_low(kept, grad):
    return (low(grad),)
low.defvjp(low_keep, low_pass)
low_back.defvjp(back_keep, back_low)

def matmul(left, right):
    return jnp.dot(left, right, precision=lax.Precision.HIGHEST)

def rms_norm(value, gain):
    return value * lax.rsqrt(lax.optimization_barrier(jnp.mean(value * value, axis=-1, keepdims=True)) + EPS) * gain

def segment_ids(seq_lengths, positions):
    seq_ends = jnp.cumsum(seq_lengths)[:-1]
    return lax.optimization_barrier(jnp.sum((positions[..., None] >= seq_ends).astype(jnp.int32), axis=-1))

def solve_lower(system, right):
    return lax.linalg.triangular_solve(system, right, left_side=True, lower=True, unit_diagonal=True)

def solve_upper(system, right):
    return lax.linalg.triangular_solve(system, right, left_side=True, lower=False, unit_diagonal=True)

def piece_parts(queries, key_rows, house_rows, beta_rows):
    length = queries.shape[0]
    row_ids = lax.broadcasted_iota(jnp.int32, (length, length), 0)
    col_ids = lax.broadcasted_iota(jnp.int32, (length, length), 1)
    identity = jnp.eye(length, dtype=queries.dtype)
    gram_rows = beta_rows[:, None] * matmul(house_rows, house_rows.T)
    lower_sys = identity + jnp.where(row_ids > col_ids, gram_rows, 0.0)
    upper_sys = identity + jnp.where(row_ids < col_ids, gram_rows, 0.0)
    key_coef = solve_lower(lower_sys, beta_rows[:, None] * jnp.where(row_ids > col_ids, matmul(house_rows, key_rows.T), 0.0))
    query_house = matmul(queries, house_rows.T)
    inner_scores = matmul(queries, key_rows.T) - matmul(jnp.where(row_ids >= col_ids, query_house, 0.0), key_coef)
    moved_keys = key_rows - matmul(key_coef.T, house_rows)
    query_coef = solve_upper(upper_sys, beta_rows[:, None] * jnp.where(row_ids <= col_ids, query_house.T, 0.0))
    moved_queries = queries - matmul(query_coef.T, house_rows)
    through = solve_lower(lower_sys, beta_rows[:, None] * house_rows)
    transfer = jnp.eye(house_rows.shape[1], dtype=queries.dtype) - matmul(house_rows.T, through)
    return (inner_scores, moved_queries, moved_keys, transfer)

def attend(inner_scores, moved_queries, values, seg_own, piece_id, all_keys, all_values, all_transfers, all_segs, rounder):
    length, width = moved_queries.shape
    piece_count = all_keys.shape[0]
    score_scale = width ** (-0.5)
    row_ids = lax.broadcasted_iota(jnp.int32, (length, length), 0)
    col_ids = lax.broadcasted_iota(jnp.int32, (length, length), 1)
    own_logits = jnp.where((row_ids >= col_ids) & (seg_own[:, None] == seg_own[None, :]), inner_scores * score_scale, NEG)

    def advance(current, key_piece):
        before = key_piece < piece_id
        scores = matmul(current, all_keys[key_piece].T)
        same_seq = seg_own[:, None] == all_segs[key_piece][None, :]
        logits = jnp.where(before & same_seq, scores * score_scale, NEG)
        current = jnp.where(before, matmul(current, all_transfers[key_piece]), current)
        return (current, logits)
    finished, cross = lax.scan(advance, moved_queries, jnp.arange(piece_count - 1, -1, -1, dtype=jnp.int32))
    cross = jnp.flip(cross, 0).transpose(1, 0, 2).reshape(length, piece_count * length)
    row_max = jnp.maximum(lax.optimization_barrier(jnp.max(own_logits, axis=1)), lax.optimization_barrier(jnp.max(cross, axis=1)))
    own_exp = jnp.exp(own_logits - row_max[:, None])
    cross_exp = jnp.exp(cross - row_max[:, None])
    row_total = lax.optimization_barrier(jnp.sum(own_exp, axis=1)) + lax.optimization_barrier(jnp.sum(cross_exp, axis=1))
    own_prob = rounder(own_exp / row_total[:, None])
    cross_prob = rounder(cross_exp / row_total[:, None])
    return matmul(own_prob, values) + matmul(cross_prob, all_values.reshape(piece_count * length, width))

def short_conv(raw_house, conv_taps, seg_ids):
    mixed = conv_taps[0] * raw_house
    for offset in range(1, conv_taps.shape[0]):
        earlier = jnp.concatenate([jnp.zeros((offset, raw_house.shape[1]), raw_house.dtype), raw_house[:-offset]], axis=0)
        earlier_seg = jnp.concatenate([jnp.full((offset,), -1, jnp.int32), seg_ids[:-offset]], axis=0)
        mixed = mixed + conv_taps[offset] * jnp.where((earlier_seg == seg_ids)[:, None], earlier, 0.0)
    return mixed

def layer(x_rows, seg_ids, attn_gain, w_query, w_key, w_value, w_house, w_beta, conv_taps, w_out, mlp_gain, w_gate, w_up, w_down):
    heads = w_beta.shape[1]
    width = w_query.shape[1] // heads
    normed_one = low(rms_norm(x_rows, attn_gain))
    queries = low(low_back(matmul(normed_one, w_query)))
    key_rows = low(low_back(matmul(normed_one, w_key)))
    value_rows = low(low_back(matmul(normed_one, w_value)))
    raw_house = low_back(matmul(normed_one, w_house))
    mixed = short_conv(raw_house, conv_taps, seg_ids).reshape(ROW, heads, width)
    house_rows = low(mixed * lax.rsqrt(lax.optimization_barrier(jnp.sum(mixed * mixed, axis=-1, keepdims=True)) + EPS)).reshape(ROW, heads * width)
    beta_rows = 2.0 * jax.nn.sigmoid(low_back(matmul(normed_one, w_beta)))

    def by_head(value):
        return value.reshape(NPIECE, PIECE, heads, width).transpose(2, 0, 1, 3)
    seg_pieces = seg_ids.reshape(NPIECE, PIECE)
    piece_ids = jnp.arange(NPIECE, dtype=jnp.int32)

    def one_head(head_item):
        q_head, k_head, v_head, w_head, b_head = head_item
        inner_scores, moved_q, moved_k, transfer = jax.vmap(piece_parts)(q_head, k_head, w_head, b_head)

        def one_piece(piece_item):
            inner_p, moved_p, value_p, seg_p, ident = piece_item
            return attend(inner_p, moved_p, value_p, seg_p, ident, moved_k, v_head, transfer, seg_pieces, low)
        return lax.map(jax.checkpoint(one_piece), (inner_scores, moved_q, v_head, seg_pieces, piece_ids))
    head_out = lax.map(jax.checkpoint(one_head), (by_head(queries), by_head(key_rows), by_head(value_rows), by_head(house_rows), beta_rows.reshape(NPIECE, PIECE, heads).transpose(2, 0, 1)))
    attended = low(low_back(head_out.transpose(1, 2, 0, 3).reshape(ROW, heads * width)))
    attn_rows = low_back(matmul(attended, w_out))
    middle = x_rows + attn_rows
    normed_two = low(rms_norm(middle, mlp_gain))
    gate_rows = low_back(matmul(normed_two, w_gate))
    up_rows = low_back(matmul(normed_two, w_up))
    act_rows = low(jax.nn.silu(gate_rows) * up_rows)
    mlp_rows = low_back(matmul(act_rows, w_down))
    return (middle + mlp_rows, (attn_rows, mlp_rows))

def reference(tokens, cotangent, valid_mask, lengths, deal, attn_gain, w_query, w_key, w_value, w_house, w_beta, conv_taps, w_out, mlp_gain, w_gate, w_up, w_down):
    weights = tuple((weight.astype(jnp.float32) for weight in (attn_gain, w_query, w_key, w_value, w_house, w_beta, conv_taps, w_out, mlp_gain, w_gate, w_up, w_down)))
    labels = jnp.arange(NPIECE, dtype=jnp.int32)

    def per_group(totals, group_item):
        rows_in, grads_in, mask_in, seq_lengths, deal_row = group_item
        back_order = lax.optimization_barrier(jnp.sum(jnp.where(deal_row[:, None] == labels[None, :], labels[:, None], 0), axis=0)).astype(jnp.int32)

        def causal(value):
            return jnp.take(value.reshape((NPIECE, PIECE) + value.shape[1:]), deal_row, axis=0).reshape(value.shape)

        def given(value):
            return jnp.take(value.reshape((NPIECE, PIECE) + value.shape[1:]), back_order, axis=0).reshape(value.shape)
        x_rows = causal(rows_in).astype(jnp.float32)
        dy_rows = causal(grads_in).astype(jnp.float32)
        mask_rows = causal(mask_in).astype(jnp.float32)
        seg_ids = segment_ids(seq_lengths, jnp.arange(ROW, dtype=jnp.int32))

        def run_layer(x_in, *params):
            return layer(x_in, seg_ids, *params)
        out_rows, pullback, branches = jax.vjp(run_layer, x_rows, *weights, has_aux=True)
        gradients = pullback(dy_rows)
        sums = jnp.stack([jnp.sum(mask_rows * lax.optimization_barrier(jnp.sum(branch * branch, axis=1))) for branch in (x_rows, branches[0], branches[1], out_rows)] + [jnp.sum(mask_rows)])
        totals = tuple((old + new for old, new in zip(totals, tuple(gradients[1:]) + (sums,))))
        return (totals, (given(out_rows).astype(jnp.bfloat16), given(gradients[0]).astype(jnp.bfloat16)))
    zeros_init = tuple((jnp.zeros(weight.shape, jnp.float32) for weight in weights)) + (jnp.zeros((5,), jnp.float32),)
    group_items = (tokens.reshape(GROUPS, ROW, D), cotangent.reshape(GROUPS, ROW, D), valid_mask.reshape(GROUPS, ROW), lengths, deal)
    totals, (out_all, dx_all) = lax.scan(per_group, zeros_init, group_items)
    sums = totals[12]
    rms_stats = jnp.sqrt(sums[:4] / (jnp.maximum(sums[4], 1.0) * D))
    return (out_all.reshape(TOKENS, D), dx_all.reshape(TOKENS, D), totals[0], totals[1], totals[2], totals[3], totals[4], totals[5], totals[6], totals[7], totals[8], totals[9], totals[10], totals[11], rms_stats)
```

```python
import functools

import jax
import jax.numpy as jnp
from jax import lax
from jax.experimental import pallas as pl
from jax.experimental.pallas import tpu as pltpu
from jax.sharding import PartitionSpec as P

EPS = 1e-06
NEG = -1e30
BF = jnp.bfloat16
F32 = jnp.float32
CHUNK = 128


def dg(left, right, cl, cr):
    return lax.dot_general(left, right, (((cl,), (cr,)), ((), ())), preferred_element_type=F32)


def halves(value):
    high = value.astype(BF)
    return high, (value - high.astype(F32)).astype(BF)


def joined(pairs, cl=1, cr=0):
    lefts, rights = [], []
    for left, right in pairs:
        if left.dtype == BF and right.dtype == BF:
            lefts += [left]
            rights += [right]
        elif left.dtype == BF:
            lefts += [left, left]
            rights += halves(right)
        elif right.dtype == BF:
            lefts += halves(left)
            rights += [right, right]
        else:
            lh, ll = halves(left)
            rh, rl = halves(right)
            lefts += [lh, lh, ll]
            rights += [rh, rl, rh]
    return dg(jnp.concatenate(lefts, axis=cl), jnp.concatenate(rights, axis=cr), cl, cr)


def mm(left, right, cl=1, cr=0):
    return joined([(left, right)], cl, cr)


def ml(left, right, cl=1, cr=0):
    return dg(left.astype(BF), right.astype(BF), cl, cr)


def seg_at(position, ends):
    seg = (position >= ends[0]).astype(jnp.int32)
    for end in ends[1:]:
        seg = seg + (position >= end).astype(jnp.int32)
    return seg


def seq_ends(len_ref):
    ends = [len_ref[0, 0]]
    for index in range(1, len_ref.shape[1] - 1):
        ends.append(ends[-1] + len_ref[0, index])
    return ends


def shifted_mask(rows, width, shift, ends):
    here = lax.broadcasted_iota(jnp.int32, (rows, width), 0)
    back = here - shift
    return (back >= 0) & (seg_at(here, ends) == seg_at(back, ends))


def tile_iota():
    row = lax.broadcasted_iota(jnp.int32, (CHUNK, CHUNK), 0)
    col = lax.broadcasted_iota(jnp.int32, (CHUNK, CHUNK), 1)
    return row, col


def forward_kernel(
    deal_ref, found_ref, len_ref, x_ref, gain_ref, w_ref, wb_ref, taps_ref,
    o_ref, h1_ref, q_ref, k_ref, v_ref, house_ref, raw_ref, logit_ref, prob_ref,
    u_ref, kt_ref, tr_ref, tinv_ref, xq_ref, yk_ref, z_ref,
    proj_ref, score_ref,
):
    rows = x_ref.shape[0]
    pieces = deal_ref.shape[1]
    piece = rows // pieces
    chunks = rows // CHUNK
    width = o_ref.shape[1]
    scale = width ** (-0.5)
    ends = seq_ends(len_ref)
    gain = gain_ref[...].astype(F32)

    def project(step, carry):
        base = pl.multiple_of(step * piece, piece)
        here = pl.multiple_of(found_ref[0, step] * piece, piece)
        x = x_ref[pl.ds(here, piece), :].astype(F32)
        inv = lax.rsqrt(jnp.mean(x * x, axis=1, keepdims=True) + EPS)
        h1 = (x * inv * gain).astype(BF)
        h1_ref[pl.ds(base, piece), :] = h1
        proj_ref[pl.ds(base, piece), :] = dg(h1, w_ref[...], 1, 0)
        logit_ref[pl.ds(base, piece), :] = dg(h1, wb_ref[...], 1, 0)
        return carry

    lax.fori_loop(0, pieces, project, 0)
    q_ref[...] = proj_ref[:, :width].astype(BF)
    k_ref[...] = proj_ref[:, width:2 * width].astype(BF)
    v_ref[...] = proj_ref[:, 2 * width:3 * width].astype(BF)
    raw = proj_ref[:, 3 * width:4 * width]
    raw_ref[...] = raw
    taps = taps_ref[...].astype(F32)
    mixed = taps[0:1, :] * raw
    for shift in range(1, taps.shape[0]):
        moved = pltpu.roll(raw, shift, 0)
        mixed = mixed + taps[shift:shift + 1, :] * jnp.where(
            shifted_mask(rows, width, shift, ends), moved, 0.0
        )
    unit = mixed * lax.rsqrt(jnp.sum(mixed * mixed, axis=1, keepdims=True) + EPS)
    house_ref[...] = unit.astype(BF)

    row, col = tile_iota()
    strict = row > col
    eye = jnp.where(row == col, 1.0, 0.0)
    spans = [slice(n * CHUNK, (n + 1) * CHUNK) for n in range(chunks)]
    strength = [2.0 * jax.nn.sigmoid(logit_ref[s, 0:1]) for s in spans]
    system = []
    for n, s in enumerate(spans):
        house = house_ref[s, :]
        system.append(jnp.where(strict, strength[n] * dg(house, house, 1, 1), 0.0))
    inverse = [eye - jnp.where((row ^ col) == 1, a, 0.0) for a in system]
    level = 1
    while (1 << level) < CHUNK:
        block = ((row ^ col) >> level) == 1
        inner = [mm(jnp.where(block, a, 0.0), t) for a, t in zip(system, inverse)]
        inverse = [t - mm(t, i) for t, i in zip(inverse, inner)]
        level += 1
    for n, s in enumerate(spans):
        query, key, house = q_ref[s, :], k_ref[s, :], house_ref[s, :]
        tinv = inverse[n]
        tinv_ref[s, :] = tinv
        across = jnp.transpose(jnp.broadcast_to(strength[n], (CHUNK, CHUNK)))
        merged = tinv * across
        a_qw = jnp.where(row >= col, dg(query, house, 1, 1), 0.0)
        a_wk = jnp.where(strict, dg(house, key, 1, 1), 0.0)
        xq = mm(a_qw, merged)
        yk = mm(merged, a_wk)
        zz = mm(merged, house)
        xq_ref[s, :] = xq
        yk_ref[s, :] = yk
        z_ref[s, :] = zz
        score_ref[s, s] = (dg(query, key, 1, 1) - mm(xq, a_wk)) * scale
        proj_ref[s, :width] = query.astype(F32) - mm(xq, house)
        kt_ref[s, :] = key.astype(F32) - mm(yk, house, 0, 0)
        tr_ref[s, :] = eye - mm(house, zz, 0, 0)
    offset = 0
    for n in range(chunks - 2, -1, -1):
        later = slice((n + 1) * CHUNK, rows)
        count = rows - (n + 1) * CHUNK
        carried = proj_ref[later, :width]
        u_ref[offset:offset + count, :] = carried
        offset += count
        score_ref[later, spans[n]] = mm(carried, kt_ref[spans[n], :], 1, 1) * scale
        if n > 0:
            proj_ref[later, :width] = mm(carried, tr_ref[spans[n], :])
    for m, s in enumerate(spans):
        reach = (m + 1) * CHUNK
        at_row = lax.broadcasted_iota(jnp.int32, (CHUNK, reach), 0) + m * CHUNK
        at_col = lax.broadcasted_iota(jnp.int32, (CHUNK, reach), 1)
        keep = (at_row >= at_col) & (seg_at(at_row, ends) == seg_at(at_col, ends))
        logits = jnp.where(keep, score_ref[s, :reach], NEG)
        top = jnp.max(logits, axis=1, keepdims=True)
        grown = jnp.exp(logits - top)
        prob = grown / jnp.sum(grown, axis=1, keepdims=True)
        prob_ref[s, :reach] = prob
        proj_ref[s, :width] = dg(prob.astype(BF), v_ref[:reach, :], 1, 0)

    def give(step, carry):
        base = pl.multiple_of(step * piece, piece)
        given = pl.multiple_of(deal_ref[0, step] * piece, piece)
        o_ref[pl.ds(given, piece), :] = proj_ref[pl.ds(base, piece), :width].astype(BF)
        return carry

    lax.fori_loop(0, pieces, give, 0)


def backward_kernel(
    deal_ref, place_ref, len_ref, live_ref, do_ref, h1_ref, w_ref, wb_ref, taps_ref,
    q_ref, k_ref, v_ref, house_ref, raw_ref, logit_ref, prob_ref,
    u_ref, kt_ref, tr_ref, tinv_ref, xq_ref, yk_ref, z_ref,
    dh1_ref, dw_ref, db_ref, dtaps_ref,
    ds_ref, dout_ref, du_ref, dkt_ref, dtr_ref, dhouse_ref, dproj_ref,
):
    rows = do_ref.shape[0]
    pieces = deal_ref.shape[1]
    piece = rows // pieces
    small = rows // place_ref.shape[1]
    chunks = rows // CHUNK
    width = do_ref.shape[1]
    scale = width ** (-0.5)
    ends = seq_ends(len_ref)
    spans = [slice(n * CHUNK, (n + 1) * CHUNK) for n in range(chunks)]
    row, col = tile_iota()
    strict = row > col

    def take(step, carry):
        base = pl.multiple_of(step * piece, piece)
        given = pl.multiple_of(deal_ref[0, step] * piece, piece)
        dout_ref[pl.ds(base, piece), :] = do_ref[pl.ds(given, piece), :]
        return carry

    lax.fori_loop(0, pieces, take, 0)
    for m, s in enumerate(spans):
        reach = (m + 1) * CHUNK
        prob = prob_ref[s, :reach]
        dprob = dg(dout_ref[s, :], v_ref[:reach, :], 1, 1)
        dot = jnp.sum(prob * dprob, axis=1, keepdims=True)
        ds_ref[s, :reach] = prob * (dprob - dot) * scale
    for n, s in enumerate(spans):
        dproj_ref[s, 2 * width:3 * width] = dg(
            prob_ref[n * CHUNK:, s].astype(BF), dout_ref[n * CHUNK:, :], 0, 0
        ).astype(BF)
    starts = {}
    offset = 0
    for n in range(chunks - 2, -1, -1):
        starts[n] = offset
        offset += rows - (n + 1) * CHUNK
    for n in range(chunks - 1):
        later = slice((n + 1) * CHUNK, rows)
        count = rows - (n + 1) * CHUNK
        grad = ds_ref[later, spans[n]]
        carried = u_ref[starts[n]:starts[n] + count, :]
        dkt_ref[spans[n], :] = mm(grad, carried, 0, 0)
        fresh = mm(grad, kt_ref[spans[n], :])
        if n > 0:
            before = du_ref[later, :]
            dtr_ref[spans[n], :] = mm(carried, before, 0, 0)
            fresh = fresh + mm(before, tr_ref[spans[n], :], 1, 1)
        du_ref[later, :] = fresh
    for n, s in enumerate(spans):
        query, key, house = q_ref[s, :], k_ref[s, :], house_ref[s, :]
        strength = 2.0 * jax.nn.sigmoid(logit_ref[s, 0:1])
        tinv = tinv_ref[s, :]
        merged = tinv * jnp.transpose(jnp.broadcast_to(strength, (CHUNK, CHUNK)))
        a_qw = jnp.where(row >= col, dg(query, house, 1, 1), 0.0)
        a_wk = jnp.where(strict, dg(house, key, 1, 1), 0.0)
        gram = jnp.where(strict, dg(house, house, 1, 1), 0.0)
        xq, yk, zz = xq_ref[s, :], yk_ref[s, :], z_ref[s, :]
        di = ds_ref[s, s]
        first, final = n == 0, n == chunks - 1
        if first:
            dxq = mm(di, a_wk, 1, 1)
            da_qw = mm(di, yk, 1, 1)
        else:
            dqt = du_ref[s, :]
            dxq = joined([(di, a_wk), (dqt, house)], 1, 1)
            da_qw = joined([(di, yk), (dqt, zz)], 1, 1)
        da_qw = jnp.where(row >= col, da_qw, 0.0)
        dm = mm(a_qw, dxq, 0, 0)
        cross = [(xq, di)]
        if not final:
            dkt = dkt_ref[s, :]
            dyk = mm(house, dkt, 1, 1)
            cross.append((merged, dyk))
            outer = [(dyk, a_wk)]
            if not first:
                dtr = dtr_ref[s, :]
                wd = mm(house, dtr)
                outer.append((wd, house))
            dm = dm + joined(outer, 1, 1)
        da_wk = jnp.where(strict, joined(cross, 0, 0), 0.0)
        ee = mm(tinv, dm, 0, 0)
        rest = jnp.where(row == col, 1.0, 0.0) - mm(gram, merged)
        dstrength = -jnp.sum(ee * rest, axis=1, keepdims=True)
        dgram = jnp.where(strict, mm(strength * ee, merged, 1, 1), 0.0)
        dq = joined([(di, key), (-da_qw, house)])
        dk = joined([(di, query), (-da_wk, house)], 0, 0)
        tall = [(da_qw, query), (-dgram, house)]
        wide = [(da_wk, key), (-dgram, house)]
        if not first:
            dq = dq + dqt
            tall.append((xq, dqt))
        if not final:
            dk = dk + dkt
            wide.append((yk, dkt))
            if not first:
                tall.append((merged, wd))
        dw = joined(tall, 0, 0) + joined(wide)
        if not first and not final:
            dw = dw + mm(zz, dtr, 1, 1)
        dw = -dw
        dproj_ref[s, :width] = dq.astype(BF)
        dproj_ref[s, width:2 * width] = dk.astype(BF)
        dhouse_ref[s, :] = dw
        gate = 0.5 * strength
        dlogit = dstrength * 2.0 * gate * (1.0 - gate)
        lane = lax.broadcasted_iota(jnp.int32, (CHUNK, width), 1)
        dproj_ref[s, 4 * width:] = jnp.where(lane == 0, dlogit, 0.0).astype(BF)
    raw = raw_ref[...]
    taps = taps_ref[...].astype(F32)
    count = taps.shape[0]
    mixed = taps[0:1, :] * raw
    earlier = [raw]
    masks = [None]
    for shift in range(1, count):
        masks.append(shifted_mask(rows, width, shift, ends))
        earlier.append(jnp.where(masks[shift], pltpu.roll(raw, shift, 0), 0.0))
        mixed = mixed + taps[shift:shift + 1, :] * earlier[shift]
    inv = lax.rsqrt(jnp.sum(mixed * mixed, axis=1, keepdims=True) + EPS)
    dunit = dhouse_ref[...]
    dmixed = inv * dunit - mixed * (
        inv * inv * inv * jnp.sum(dunit * mixed, axis=1, keepdims=True)
    )
    live = live_ref[0, 0].astype(F32)
    draw = taps[0:1, :] * dmixed
    dtaps_ref[0:1, :] = jnp.sum(dmixed * raw, axis=0, keepdims=True) * live
    for shift in range(1, count):
        dtaps_ref[shift:shift + 1, :] = (
            jnp.sum(dmixed * earlier[shift], axis=0, keepdims=True) * live
        )
        later = jnp.where(masks[shift], dmixed, 0.0)
        draw = draw + taps[shift:shift + 1, :] * pltpu.roll(later, rows - shift, 0)
    dproj_ref[:, 3 * width:4 * width] = draw.astype(BF)

    def send(step, carry):
        base = pl.multiple_of(step * piece, piece)
        grads = dproj_ref[pl.ds(base, piece), :]
        dh1 = dg(grads[:, :4 * width], w_ref[...], 1, 1) + dg(grads[:, 4 * width:], wb_ref[...], 1, 1)
        dh1 = (dh1 * live).astype(dh1_ref.dtype)
        for part in range(piece // small):
            there = place_ref[0, deal_ref[0, step] * (piece // small) + part]
            dh1_ref[pl.ds(pl.multiple_of(there * small, small), small), :] = dh1[
                part * small:(part + 1) * small
            ]
        return carry

    lax.fori_loop(0, pieces, send, 0)
    depth = h1_ref.shape[1]
    block = 256

    def weigh(step, carry):
        base = pl.multiple_of(step * block, block)
        got = dg(h1_ref[:, pl.ds(base, block)], dproj_ref[...], 0, 0) * live
        dw_ref[pl.ds(base, block), :] = got[:, :4 * width].astype(dw_ref.dtype)
        db_ref[pl.ds(base, block), :] = got[:, 4 * width:]
        return carry

    lax.fori_loop(0, depth // block, weigh, 0)


def saved_shapes(rows, depth, width):
    chunks = rows // CHUNK
    carried = CHUNK * chunks * (chunks - 1) // 2

    def of(shape, dtype):
        return jax.ShapeDtypeStruct(shape, dtype)

    tall = of((rows, width), F32)
    slim = of((rows, width), BF)
    return (
        of((rows, depth), BF), slim, slim, slim, slim, tall, tall, of((rows, rows), F32),
        of((carried, width), F32), tall, tall, tall, tall, tall, tall,
    )


VMEM = pl.BlockSpec(memory_space=pltpu.VMEM)
SMEM = pl.BlockSpec(memory_space=pltpu.SMEM)


def attend_forward(deal, found, lengths, x_all, gain, w_all, wb_all, taps):
    rows, depth = x_all.shape
    width = w_all.shape[1] // 4
    saved = saved_shapes(rows, depth, width)
    return pl.pallas_call(
        forward_kernel,
        out_shape=(jax.ShapeDtypeStruct((rows, width), BF),) + saved,
        in_specs=[SMEM, SMEM, SMEM] + [VMEM] * 5,
        out_specs=tuple([VMEM] * (1 + len(saved))),
        scratch_shapes=[pltpu.VMEM((rows, 4 * width), F32), pltpu.VMEM((rows, rows), F32)],
        compiler_params=pltpu.CompilerParams(vmem_limit_bytes=48 * 1024 * 1024),
        name="attend_forward",
    )(deal, found, lengths, x_all, gain, w_all, wb_all, taps)


def attend_backward(deal, place, lengths, live, d_out, h1, w_all, wb_all, taps, saved):
    rows, width = d_out.shape
    depth = h1.shape[1]
    return pl.pallas_call(
        backward_kernel,
        out_shape=(
            jax.ShapeDtypeStruct((rows, depth), BF),
            jax.ShapeDtypeStruct((depth, 4 * width), BF),
            jax.ShapeDtypeStruct((depth, width), F32),
            jax.ShapeDtypeStruct((taps.shape[0], width), F32),
        ),
        in_specs=[SMEM, SMEM, SMEM, SMEM] + [VMEM] * (5 + len(saved)),
        out_specs=(VMEM, VMEM, VMEM, VMEM),
        scratch_shapes=[
            pltpu.VMEM((rows, rows), F32),
            pltpu.VMEM((rows, width), BF),
            pltpu.VMEM((rows, width), F32),
            pltpu.VMEM((rows, width), F32),
            pltpu.VMEM((rows, width), F32),
            pltpu.VMEM((rows, width), F32),
            pltpu.VMEM((rows, 5 * width), BF),
        ],
        compiler_params=pltpu.CompilerParams(vmem_limit_bytes=56 * 1024 * 1024),
        name="attend_backward",
    )(deal, place, lengths, live, d_out, h1, w_all, wb_all, taps, *saved)


def steps_of(axis, descending):
    size = lax.axis_size(axis)
    bits = []
    bit = 1
    while bit < size:
        bits.append((axis, bit))
        bit *= 2
    return bits[::-1] if descending else bits


def swap(value, axis, bit):
    size = lax.axis_size(axis)
    return lax.ppermute(value, axis, [(i, i ^ bit) for i in range(size)])


def spread_rows(value, steps):
    for axis, bit in steps:
        value = jnp.concatenate([value, swap(value, axis, bit)], axis=0)
    return value


def gather_rows(value, steps):
    for axis, bit in steps[::-1]:
        half = value.shape[0] // 2
        value = value[:half] + swap(value[half:].astype(BF), axis, bit).astype(F32)
    return value


def over_shard(value):
    size = lax.axis_size("shard")
    if size == 2:
        other = swap(value, "shard", 1)
        mine = lax.axis_index("shard") == 0
        return jnp.stack([jnp.where(mine, value, other), jnp.where(mine, other, value)])
    return lax.all_gather(value, "shard", axis=0, tiled=False)


def deal_out(value, axis):
    return lax.all_to_all(value, axis, split_axis=0, concat_axis=0, tiled=True)


def norm_back(value, inverse, gain, grad):
    scaled = grad * gain
    return inverse * scaled - value * inverse**3 * jnp.mean(scaled * value, axis=1, keepdims=True)


def local(
    tokens, cotangent, valid_mask, lengths, deal, attn_gain,
    w_query, w_key, w_value, w_house, w_beta, conv_taps, w_out,
    mlp_gain, w_gate, w_up, w_down,
):
    shards, ranks, lanes = (lax.axis_size(a) for a in ("shard", "ctx", "tp"))
    shard, rank, lane = (lax.axis_index(a) for a in ("shard", "ctx", "tp"))
    span, depth = tokens.shape
    share, columns = w_query.shape
    heads = w_beta.shape[1]
    width = columns // heads
    piece = span // 2
    group = ranks * span
    small = span // lanes
    part = w_gate.shape[1] // shards
    spare = ranks - heads
    tp_steps = steps_of("tp", True)
    plane_steps = steps_of("shard", False) + tp_steps
    live = (rank < heads).astype(jnp.int32).reshape(1, 1)
    head_at = jnp.minimum(rank, heads - 1)

    half = lane % 2
    own = lax.dynamic_slice_in_dim(tokens, half * piece, piece, axis=0)
    near = [own] + [
        lax.ppermute(own, "ctx", [(i, (i + k) % ranks) for i in range(ranks)])
        for k in range(1, ranks)
    ]
    near = jnp.concatenate(near, axis=0)
    x_all = jnp.concatenate([near, swap(near, "tp", 1)], axis=0)
    owner = deal // 2
    found = jnp.where(deal % 2 == half, 0, ranks) + (rank - owner) % ranks

    blocks = jnp.stack([w_query, w_key, w_value, w_house]).reshape(4, share, heads, width)
    blocks = blocks.transpose(2, 1, 0, 3).reshape(heads, share, 4 * width)
    beta_rows = jnp.pad(w_beta.T.reshape(heads, 1, share), ((0, 0), (0, 15), (0, 4 * width - share)))
    blocks = jnp.pad(jnp.concatenate([blocks, beta_rows], axis=1), ((0, spare), (0, 0), (0, 0)))
    blocks = over_shard(deal_out(blocks, "ctx"))
    w_all = blocks[:, :, :share].reshape(depth, 4 * width)
    wb_all = jnp.pad(blocks[:, :, share, :share].reshape(depth, 1), ((0, 0), (0, width - 1)))
    taps = lax.dynamic_slice_in_dim(conv_taps, head_at * width, width, axis=1)

    def fetch(weight):
        parts = weight.reshape(share, shards, part).transpose(1, 0, 2)
        rows = deal_out(parts, "shard").reshape(shards * share, part)
        return lax.all_gather(rows, "ctx", axis=0, tiled=True)

    wo_t = lax.all_gather(w_out.T, ("shard", "ctx"), axis=0, tiled=True)
    wg_all = fetch(w_gate)
    wu_all = fetch(w_up)
    wd_all = fetch(w_down.T)

    def to_plane(value):
        value = value.reshape(-1, shards, ranks, share).transpose(0, 2, 1, 3)
        return value.reshape(-1, depth)

    def from_plane(value):
        value = value.reshape(-1, ranks, shards, share).transpose(0, 2, 1, 3)
        return value.reshape(-1, depth)

    def my_rows(value):
        return lax.dynamic_slice_in_dim(value, lane * small, small, axis=0)

    grad_own = my_rows(cotangent)
    grad_plane = spread_rows(to_plane(grad_own), plane_steps)

    fwd = attend_forward(deal, found, lengths, x_all, attn_gain[None], w_all, wb_all, taps)
    head_out, h1, saved = fwd[0], fwd[1], fwd[2:]
    slots = jnp.arange(lanes, dtype=jnp.int32)
    order = jnp.full_like(slots, lane)
    for index, (_, bit) in enumerate(tp_steps):
        order = order ^ jnp.where((slots >> index) % 2 == 1, bit, 0)
    o_rows = deal_out(head_out.reshape(ranks, span, width), "ctx")[:heads]
    o_rows = o_rows.reshape(heads, lanes, small, width).transpose(1, 2, 0, 3)
    o_rows = jnp.take(o_rows, order, axis=0).reshape(span, columns)
    attn = gather_rows(dg(o_rows, wo_t, 1, 1), tp_steps)
    x_own = my_rows(tokens).astype(F32)
    middle = x_own + attn
    gain_two = mlp_gain.astype(F32)
    inv_two = lax.rsqrt(jnp.mean(middle * middle, axis=1, keepdims=True) + EPS)
    normed = (middle * inv_two * gain_two).astype(BF)
    h2 = spread_rows(to_plane(normed), plane_steps)

    gate = dg(h2, wg_all, 1, 0)
    up = dg(h2, wu_all, 1, 0)
    sig = jax.nn.sigmoid(gate)
    swish = gate * sig
    act = (swish * up).astype(BF)
    d_act = dg(grad_plane, wd_all, 1, 0)
    d_gate = (d_act * up * sig * (1.0 + gate * (1.0 - sig))).astype(BF)
    d_up = (d_act * swish).astype(BF)
    d_two = gather_rows(dg(d_gate, wg_all, 1, 1) + dg(d_up, wu_all, 1, 1), plane_steps)
    d_two = from_plane(d_two)
    mlp = from_plane(gather_rows(dg(act, wd_all, 1, 1), plane_steps))
    result = middle + mlp

    def give_back(left, right):
        grad = dg(left, right, 0, 0).astype(BF)
        grad = lax.psum_scatter(grad, "ctx", scatter_dimension=0, tiled=True)
        grad = deal_out(grad.reshape(shards, share, part), "shard")
        return grad.transpose(1, 0, 2).reshape(share, shards * part).astype(F32)

    d_wgate = give_back(h2, d_gate)
    d_wup = give_back(h2, d_up)
    d_wdown = give_back(grad_plane, act).T

    d_gain_two = jnp.sum(d_two * middle * inv_two, axis=0)
    d_middle = grad_own.astype(F32) + norm_back(middle, inv_two, gain_two, d_two)
    d_attn = spread_rows(d_middle.astype(BF), tp_steps)
    d_heads = dg(d_attn, wo_t, 1, 0).astype(BF).reshape(lanes, small, heads, width)
    natural = jnp.zeros_like(slots)
    for index, (_, bit) in enumerate(tp_steps):
        natural = natural + jnp.where(((slots ^ lane) & bit) != 0, 1 << index, 0)
    d_heads = jnp.take(d_heads, natural, axis=0).transpose(2, 0, 1, 3).reshape(heads, span, width)
    d_heads = deal_out(jnp.pad(d_heads, ((0, spare), (0, 0), (0, 0))), "ctx")
    d_wout = dg(d_attn, o_rows, 0, 0).astype(BF)
    d_wout = lax.psum_scatter(d_wout, ("shard", "ctx"), scatter_dimension=0, tiled=True)
    d_wout = d_wout.astype(F32).T

    given = jnp.arange(group // small, dtype=jnp.int32)
    apart = (given % lanes) ^ lane
    turned = jnp.zeros_like(apart)
    for index, (_, bit) in enumerate(tp_steps):
        turned = turned + jnp.where((apart & bit) != 0, 1 << index, 0)
    place = (turned * ranks + given // lanes)[None]
    d_one, d_w, d_b, d_taps = attend_backward(
        deal, place, lengths, live, d_heads.reshape(group, width), h1, w_all, wb_all, taps, saved
    )
    d_one = gather_rows(d_one, tp_steps)
    d_one = deal_out(d_one.astype(BF).reshape(ranks, small, depth), "ctx")
    d_one = jnp.sum(d_one.astype(F32), axis=0)
    gain_one = attn_gain.astype(F32)
    inv_one = lax.rsqrt(jnp.mean(x_own * x_own, axis=1, keepdims=True) + EPS)
    d_gain_one = jnp.sum(d_one * x_own * inv_one, axis=0)
    d_input = d_middle + norm_back(x_own, inv_one, gain_one, d_one)
    d_tokens = lax.all_gather(d_input.astype(BF), "tp", axis=0, tiled=True)
    output = lax.all_gather(result.astype(BF), "tp", axis=0, tiled=True)

    d_w = deal_out(d_w.reshape(shards, ranks * share, 4 * width), "shard")
    d_w = jnp.sum(d_w.astype(F32), axis=0).astype(BF)
    d_w = deal_out(d_w.reshape(ranks, share, 4 * width), "ctx")[:heads].astype(F32)
    d_w = d_w.reshape(heads, share, 4, width).transpose(2, 1, 0, 3).reshape(4, share, columns)

    mask = my_rows(valid_mask).astype(F32)
    totals = jnp.stack(
        [jnp.sum(mask * jnp.sum(b * b, axis=1)) for b in (x_own, attn, mlp, result)]
        + [jnp.sum(mask)]
    )
    mine = (jnp.arange(heads) == rank).astype(F32)
    beta_part = mine[:, None] * d_b[:, 0][None]
    taps_part = mine[:, None, None] * d_taps[None]
    beta_sum, taps_sum, one_sum, two_sum, totals = lax.psum(
        (beta_part, taps_part, d_gain_one, d_gain_two, totals), ("shard", "ctx")
    )
    one_sum, two_sum, totals = lax.psum((one_sum, two_sum, totals), "tp")
    d_beta = lax.dynamic_slice_in_dim(beta_sum, (shard * ranks + rank) * share, share, axis=1).T
    d_conv = taps_sum.transpose(1, 0, 2).reshape(conv_taps.shape)
    rms_stats = jnp.sqrt(totals[:4] / (jnp.maximum(totals[4], 1.0) * depth))
    return (
        output, d_tokens, one_sum, d_w[0], d_w[1], d_w[2], d_w[3], d_beta, d_conv,
        d_wout, two_sum, d_wgate, d_wup, d_wdown, rms_stats,
    )


def solution(mesh):
    rows = P(("shard", "ctx"), None)
    tiled = P(("shard", "ctx"), "tp")
    turned = P("tp", ("shard", "ctx"))
    placed = (
        rows, rows, P(("shard", "ctx")), P("shard", None), P("shard", None), P(),
        tiled, tiled, tiled, tiled, tiled, P(None, "tp"), turned, P(), tiled, tiled, turned,
    )
    return jax.shard_map(
        local,
        mesh=mesh,
        in_specs=placed,
        out_specs=(
            rows, rows, P(), tiled, tiled, tiled, tiled, tiled, P(None, "tp"),
            turned, P(), tiled, tiled, turned, P(),
        ),
        check_vma=False,
    )
```

```python
import functools

import jax
import jax.numpy as jnp
from jax import lax
from jax.experimental import pallas as pl
from jax.experimental.pallas import tpu as pltpu
from jax.sharding import PartitionSpec as P

EPS = 1e-06
NEG = -1e30
BF = jnp.bfloat16
F32 = jnp.float32
CHUNK = 128


def dg(left, right, cl, cr):
    return lax.dot_general(left, right, (((cl,), (cr,)), ((), ())), preferred_element_type=F32)


def halves(value):
    high = value.astype(BF)
    return high, (value - high.astype(F32)).astype(BF)


def joined(pairs, cl=1, cr=0):
    lefts, rights = [], []
    for left, right in pairs:
        if left.dtype == BF and right.dtype == BF:
            lefts += [left]
            rights += [right]
        elif left.dtype == BF:
            lefts += [left, left]
            rights += halves(right)
        elif right.dtype == BF:
            lefts += halves(left)
            rights += [right, right]
        else:
            lh, ll = halves(left)
            rh, rl = halves(right)
            lefts += [lh, lh, ll]
            rights += [rh, rl, rh]
    return dg(jnp.concatenate(lefts, axis=cl), jnp.concatenate(rights, axis=cr), cl, cr)


def mm(left, right, cl=1, cr=0):
    return joined([(left, right)], cl, cr)


def ml(left, right, cl=1, cr=0):
    return dg(left.astype(BF), right.astype(BF), cl, cr)


def seg_at(position, ends):
    seg = (position >= ends[0]).astype(jnp.int32)
    for end in ends[1:]:
        seg = seg + (position >= end).astype(jnp.int32)
    return seg


def seq_ends(len_ref):
    ends = [len_ref[0, 0]]
    for index in range(1, len_ref.shape[1] - 1):
        ends.append(ends[-1] + len_ref[0, index])
    return ends


def shifted_mask(rows, width, shift, ends):
    here = lax.broadcasted_iota(jnp.int32, (rows, width), 0)
    back = here - shift
    return (back >= 0) & (seg_at(here, ends) == seg_at(back, ends))


def tile_iota():
    row = lax.broadcasted_iota(jnp.int32, (CHUNK, CHUNK), 0)
    col = lax.broadcasted_iota(jnp.int32, (CHUNK, CHUNK), 1)
    return row, col


def forward_kernel(x_count, w_count, *refs):
    deal_ref, spot_ref, slot_ref, len_ref = refs[:4]
    x_refs, refs = refs[4:4 + x_count], refs[4 + x_count:]
    gain_ref, refs = refs[0], refs[1:]
    w_refs, refs = refs[:w_count], refs[w_count:]
    taps_ref, o_ref, refs = refs[0], refs[1], refs[2:]
    kept, refs = refs[:SAVED], refs[SAVED:]
    held, (proj_ref, score_ref, sems) = refs[:SAVED], refs[SAVED:]
    (
        w_ref, wb_ref, h1_ref, q_ref, k_ref, v_ref, house_ref, raw_ref, logit_ref, prob_ref,
        u_ref, kt_ref, tr_ref, tinv_ref, xq_ref, yk_ref, z_ref,
    ) = held
    piece, depth = x_refs[0].shape
    pieces = deal_ref.shape[1]
    rows = pieces * piece
    chunks = rows // CHUNK
    width = o_ref.shape[1]
    share = depth // w_count
    scale = width ** (-0.5)
    ends = seq_ends(len_ref)
    gain = gain_ref[...].astype(F32)

    def keep(first, last):
        for index in range(first, last):
            pltpu.make_async_copy(held[index], kept[index], sems.at[index]).start()

    pick = jnp.where(
        (lax.broadcasted_iota(jnp.int32, (16, width), 0) == 0)
        & (lax.broadcasted_iota(jnp.int32, (16, width), 1) == 0),
        1.0,
        0.0,
    ).astype(BF)
    for index, ref in enumerate(w_refs):
        base = pl.multiple_of(slot_ref[0, index] * share, share)
        w_ref[pl.ds(base, share), :] = ref[:share, :]
        wb_ref[pl.ds(base, share), :] = dg(ref[share:, :share], pick, 0, 0).astype(BF)
    for index, ref in enumerate(x_refs):
        x = ref[...].astype(F32)
        inv = lax.rsqrt(jnp.mean(x * x, axis=1, keepdims=True) + EPS)
        base = pl.multiple_of(spot_ref[0, index] * piece, piece)
        h1_ref[pl.ds(base, piece), :] = (x * inv * gain).astype(BF)
    keep(0, 3)

    def project(step, carry):
        base = pl.multiple_of(step * piece, piece)
        h1 = h1_ref[pl.ds(base, piece), :]
        proj_ref[pl.ds(base, piece), :] = dg(h1, w_ref[...], 1, 0)
        logit_ref[pl.ds(base, piece), :] = dg(h1, wb_ref[...], 1, 0)
        return carry

    lax.fori_loop(0, pieces, project, 0)
    q_ref[...] = proj_ref[:, :width].astype(BF)
    k_ref[...] = proj_ref[:, width:2 * width].astype(BF)
    v_ref[...] = proj_ref[:, 2 * width:3 * width].astype(BF)
    raw = proj_ref[:, 3 * width:4 * width]
    raw_ref[...] = raw
    taps = taps_ref[...].astype(F32)
    mixed = taps[0:1, :] * raw
    for shift in range(1, taps.shape[0]):
        moved = pltpu.roll(raw, shift, 0)
        mixed = mixed + taps[shift:shift + 1, :] * jnp.where(
            shifted_mask(rows, width, shift, ends), moved, 0.0
        )
    unit = mixed * lax.rsqrt(jnp.sum(mixed * mixed, axis=1, keepdims=True) + EPS)
    house_ref[...] = unit.astype(BF)
    keep(3, 9)

    row, col = tile_iota()
    strict = row > col
    eye = jnp.where(row == col, 1.0, 0.0)
    spans = [slice(n * CHUNK, (n + 1) * CHUNK) for n in range(chunks)]
    strength = [2.0 * jax.nn.sigmoid(logit_ref[s, 0:1]) for s in spans]
    system = []
    for n, s in enumerate(spans):
        house = house_ref[s, :]
        system.append(jnp.where(strict, strength[n] * dg(house, house, 1, 1), 0.0))
    inverse = [eye - jnp.where((row ^ col) == 1, a, 0.0) for a in system]
    level = 1
    while (1 << level) < CHUNK:
        block = ((row ^ col) >> level) == 1
        inner = [mm(jnp.where(block, a, 0.0), t) for a, t in zip(system, inverse)]
        inverse = [t - mm(t, i) for t, i in zip(inverse, inner)]
        level += 1
    for n, s in enumerate(spans):
        query, key, house = q_ref[s, :], k_ref[s, :], house_ref[s, :]
        tinv = inverse[n]
        tinv_ref[s, :] = tinv
        across = jnp.transpose(jnp.broadcast_to(strength[n], (CHUNK, CHUNK)))
        merged = tinv * across
        a_qw = jnp.where(row >= col, dg(query, house, 1, 1), 0.0)
        a_wk = jnp.where(strict, dg(house, key, 1, 1), 0.0)
        xq = mm(a_qw, merged)
        yk = mm(merged, a_wk)
        zz = mm(merged, house)
        xq_ref[s, :] = xq
        yk_ref[s, :] = yk
        z_ref[s, :] = zz
        score_ref[s, s] = (dg(query, key, 1, 1) - mm(xq, a_wk)) * scale
        proj_ref[s, :width] = query.astype(F32) - mm(xq, house)
        kt_ref[s, :] = key.astype(F32) - mm(yk, house, 0, 0)
        tr_ref[s, :] = eye - mm(house, zz, 0, 0)
    keep(11, SAVED)
    offset = 0
    for n in range(chunks - 2, -1, -1):
        later = slice((n + 1) * CHUNK, rows)
        count = rows - (n + 1) * CHUNK
        carried = proj_ref[later, :width]
        u_ref[offset:offset + count, :] = carried
        offset += count
        score_ref[later, spans[n]] = mm(carried, kt_ref[spans[n], :], 1, 1) * scale
        if n > 0:
            proj_ref[later, :width] = mm(carried, tr_ref[spans[n], :])
    keep(10, 11)
    for m, s in enumerate(spans):
        reach = (m + 1) * CHUNK
        at_row = lax.broadcasted_iota(jnp.int32, (CHUNK, reach), 0) + m * CHUNK
        at_col = lax.broadcasted_iota(jnp.int32, (CHUNK, reach), 1)
        seen = (at_row >= at_col) & (seg_at(at_row, ends) == seg_at(at_col, ends))
        logits = jnp.where(seen, score_ref[s, :reach], NEG)
        top = jnp.max(logits, axis=1, keepdims=True)
        grown = jnp.exp(logits - top)
        prob = grown / jnp.sum(grown, axis=1, keepdims=True)
        prob_ref[s, :reach] = prob
        proj_ref[s, :width] = dg(prob.astype(BF), v_ref[:reach, :], 1, 0)

    def give(step, carry):
        base = pl.multiple_of(step * piece, piece)
        given = pl.multiple_of(deal_ref[0, step] * piece, piece)
        o_ref[pl.ds(given, piece), :] = proj_ref[pl.ds(base, piece), :width].astype(BF)
        return carry

    keep(9, 10)
    lax.fori_loop(0, pieces, give, 0)
    for index in range(SAVED):
        pltpu.make_async_copy(held[index], kept[index], sems.at[index]).wait()


def backward_kernel(*refs):
    deal_ref, place_ref, len_ref, live_ref, do_ref, taps_ref = refs[:6]
    kept, refs = refs[6:6 + SAVED], refs[6 + SAVED:]
    (dh1_ref, dproj_ref, small_ref, dtaps_ref), refs = refs[:4], refs[4:]
    held, refs = refs[:SAVED], refs[SAVED:]
    ds_ref, dout_ref, du_ref, dkt_ref, dtr_ref, dhouse_ref, sems = refs
    (
        w_ref, wb_ref, h1_ref, q_ref, k_ref, v_ref, house_ref, raw_ref, logit_ref, prob_ref,
        u_ref, kt_ref, tr_ref, tinv_ref, xq_ref, yk_ref, z_ref,
    ) = held

    def fetch(index):
        return pltpu.make_async_copy(kept[index], held[index], sems.at[index])

    needed = (5, 9), (10, 11, 12), (3, 4, 6, 8, 13, 14, 15, 16), (7,), (0, 1, 2)
    for index in sum(needed, ()):
        fetch(index).start()

    def ready(stage):
        for index in needed[stage]:
            fetch(index).wait()

    rows = do_ref.shape[0]
    pieces = deal_ref.shape[1]
    piece = rows // pieces
    small = rows // place_ref.shape[1]
    chunks = rows // CHUNK
    width = do_ref.shape[1]
    scale = width ** (-0.5)
    ends = seq_ends(len_ref)
    spans = [slice(n * CHUNK, (n + 1) * CHUNK) for n in range(chunks)]
    row, col = tile_iota()
    strict = row > col

    def take(step, carry):
        base = pl.multiple_of(step * piece, piece)
        given = pl.multiple_of(deal_ref[0, step] * piece, piece)
        dout_ref[pl.ds(base, piece), :] = do_ref[pl.ds(given, piece), :]
        return carry

    lax.fori_loop(0, pieces, take, 0)
    ready(0)
    for m, s in enumerate(spans):
        reach = (m + 1) * CHUNK
        prob = prob_ref[s, :reach]
        dprob = dg(dout_ref[s, :], v_ref[:reach, :], 1, 1)
        dot = jnp.sum(prob * dprob, axis=1, keepdims=True)
        ds_ref[s, :reach] = prob * (dprob - dot) * scale
    for n, s in enumerate(spans):
        dproj_ref[s, 2 * width:3 * width] = dg(
            prob_ref[n * CHUNK:, s].astype(BF), dout_ref[n * CHUNK:, :], 0, 0
        ).astype(BF)
    starts = {}
    offset = 0
    for n in range(chunks - 2, -1, -1):
        starts[n] = offset
        offset += rows - (n + 1) * CHUNK
    ready(1)
    for n in range(chunks - 1):
        later = slice((n + 1) * CHUNK, rows)
        count = rows - (n + 1) * CHUNK
        grad = ds_ref[later, spans[n]]
        carried = u_ref[starts[n]:starts[n] + count, :]
        dkt_ref[spans[n], :] = mm(grad, carried, 0, 0)
        fresh = mm(grad, kt_ref[spans[n], :])
        if n > 0:
            before = du_ref[later, :]
            dtr_ref[spans[n], :] = mm(carried, before, 0, 0)
            fresh = fresh + mm(before, tr_ref[spans[n], :], 1, 1)
        du_ref[later, :] = fresh
    ready(2)
    for n, s in enumerate(spans):
        query, key, house = q_ref[s, :], k_ref[s, :], house_ref[s, :]
        strength = 2.0 * jax.nn.sigmoid(logit_ref[s, 0:1])
        tinv = tinv_ref[s, :]
        merged = tinv * jnp.transpose(jnp.broadcast_to(strength, (CHUNK, CHUNK)))
        a_qw = jnp.where(row >= col, dg(query, house, 1, 1), 0.0)
        a_wk = jnp.where(strict, dg(house, key, 1, 1), 0.0)
        gram = jnp.where(strict, dg(house, house, 1, 1), 0.0)
        xq, yk, zz = xq_ref[s, :], yk_ref[s, :], z_ref[s, :]
        di = ds_ref[s, s]
        first, final = n == 0, n == chunks - 1
        if first:
            dxq = mm(di, a_wk, 1, 1)
            da_qw = mm(di, yk, 1, 1)
        else:
            dqt = du_ref[s, :]
            dxq = joined([(di, a_wk), (dqt, house)], 1, 1)
            da_qw = joined([(di, yk), (dqt, zz)], 1, 1)
        da_qw = jnp.where(row >= col, da_qw, 0.0)
        dm = mm(a_qw, dxq, 0, 0)
        cross = [(xq, di)]
        if not final:
            dkt = dkt_ref[s, :]
            dyk = mm(house, dkt, 1, 1)
            cross.append((merged, dyk))
            outer = [(dyk, a_wk)]
            if not first:
                dtr = dtr_ref[s, :]
                wd = mm(house, dtr)
                outer.append((wd, house))
            dm = dm + joined(outer, 1, 1)
        da_wk = jnp.where(strict, joined(cross, 0, 0), 0.0)
        ee = mm(tinv, dm, 0, 0)
        rest = jnp.where(row == col, 1.0, 0.0) - mm(gram, merged)
        dstrength = -jnp.sum(ee * rest, axis=1, keepdims=True)
        dgram = jnp.where(strict, mm(strength * ee, merged, 1, 1), 0.0)
        dq = joined([(di, key), (-da_qw, house)])
        dk = joined([(di, query), (-da_wk, house)], 0, 0)
        tall = [(da_qw, query), (-dgram, house)]
        wide = [(da_wk, key), (-dgram, house)]
        if not first:
            dq = dq + dqt
            tall.append((xq, dqt))
        if not final:
            dk = dk + dkt
            wide.append((yk, dkt))
            if not first:
                tall.append((merged, wd))
        dw = joined(tall, 0, 0) + joined(wide)
        if not first and not final:
            dw = dw + mm(zz, dtr, 1, 1)
        dw = -dw
        dproj_ref[s, :width] = dq.astype(BF)
        dproj_ref[s, width:2 * width] = dk.astype(BF)
        dhouse_ref[s, :] = dw
        gate = 0.5 * strength
        dlogit = dstrength * 2.0 * gate * (1.0 - gate)
        lane = lax.broadcasted_iota(jnp.int32, (CHUNK, width), 1)
        dproj_ref[s, 4 * width:] = jnp.where(lane == 0, dlogit, 0.0).astype(BF)
    ready(3)
    raw = raw_ref[...]
    taps = taps_ref[...].astype(F32)
    count = taps.shape[0]
    mixed = taps[0:1, :] * raw
    earlier = [raw]
    masks = [None]
    for shift in range(1, count):
        masks.append(shifted_mask(rows, width, shift, ends))
        earlier.append(jnp.where(masks[shift], pltpu.roll(raw, shift, 0), 0.0))
        mixed = mixed + taps[shift:shift + 1, :] * earlier[shift]
    inv = lax.rsqrt(jnp.sum(mixed * mixed, axis=1, keepdims=True) + EPS)
    dunit = dhouse_ref[...]
    dmixed = inv * dunit - mixed * (
        inv * inv * inv * jnp.sum(dunit * mixed, axis=1, keepdims=True)
    )
    live = live_ref[0, 0].astype(F32)
    draw = taps[0:1, :] * dmixed
    dtaps_ref[0:1, :] = jnp.sum(dmixed * raw, axis=0, keepdims=True) * live
    for shift in range(1, count):
        dtaps_ref[shift:shift + 1, :] = (
            jnp.sum(dmixed * earlier[shift], axis=0, keepdims=True) * live
        )
        later = jnp.where(masks[shift], dmixed, 0.0)
        draw = draw + taps[shift:shift + 1, :] * pltpu.roll(later, rows - shift, 0)
    dproj_ref[:, 3 * width:4 * width] = draw.astype(BF)

    ready(4)

    def send(step, total):
        base = pl.multiple_of(step * piece, piece)
        grads = dproj_ref[pl.ds(base, piece), :]
        dh1 = dg(grads[:, :4 * width], w_ref[...], 1, 1) + dg(grads[:, 4 * width:], wb_ref[...], 1, 1)
        dh1 = dh1 * live
        h1 = h1_ref[pl.ds(base, piece), :].astype(F32)
        total = total + jnp.sum(dh1 * h1, axis=0, keepdims=True)
        dh1 = dh1.astype(dh1_ref.dtype)
        for part in range(piece // small):
            there = place_ref[0, deal_ref[0, step] * (piece // small) + part]
            dh1_ref[pl.ds(pl.multiple_of(there * small, small), small), :] = dh1[
                part * small:(part + 1) * small
            ]
        return total

    small_ref[...] = jnp.zeros_like(small_ref)
    small_ref[0:1, :] = lax.fori_loop(0, pieces, send, jnp.zeros((1, h1_ref.shape[1]), F32))
    beta = dg(dproj_ref[:, 4 * width:], h1_ref[...], 0, 0)
    small_ref[1:2, :] = beta[0:1, :] * live


SAVED = 17


def saved_shapes(rows, depth, width):
    chunks = rows // CHUNK
    carried = CHUNK * chunks * (chunks - 1) // 2
    slim = ((rows, width), BF)
    tall = ((rows, width), F32)
    return (
        ((depth, 4 * width), BF), ((depth, width), BF), ((rows, depth), BF), slim, slim, slim, slim,
        tall, tall, ((rows, rows), F32), ((carried, width), F32), tall, tall, tall, tall, tall, tall,
    )


VMEM = pl.BlockSpec(memory_space=pltpu.VMEM)
SMEM = pl.BlockSpec(memory_space=pltpu.SMEM)
AWAY = pl.BlockSpec(memory_space=pl.ANY)
LIMIT = pltpu.CompilerParams(vmem_limit_bytes=56 * 1024 * 1024)


def attend_forward(deal, spot, slot, lengths, x_parts, gain, w_parts, taps):
    piece, depth = x_parts[0].shape
    rows = piece * deal.shape[1]
    width = taps.shape[1]
    saved = saved_shapes(rows, depth, width)
    return pl.pallas_call(
        functools.partial(forward_kernel, len(x_parts), len(w_parts)),
        out_shape=(jax.ShapeDtypeStruct((rows, width), BF),)
        + tuple(jax.ShapeDtypeStruct(*entry) for entry in saved),
        in_specs=[SMEM] * 4 + [VMEM] * (len(x_parts) + len(w_parts) + 2),
        out_specs=(VMEM,) + (AWAY,) * SAVED,
        scratch_shapes=[pltpu.VMEM(*entry) for entry in saved]
        + [
            pltpu.VMEM((rows, 4 * width), F32),
            pltpu.VMEM((rows, rows), F32),
            pltpu.SemaphoreType.DMA((SAVED,)),
        ],
        compiler_params=LIMIT,
        name="attend_forward",
    )(deal, spot, slot, lengths, *x_parts, gain, *w_parts, taps)


def attend_backward(deal, place, lengths, live, d_out, taps, depth, kept):
    rows, width = d_out.shape
    saved = saved_shapes(rows, depth, width)
    return pl.pallas_call(
        backward_kernel,
        out_shape=(
            jax.ShapeDtypeStruct((rows, depth), BF),
            jax.ShapeDtypeStruct((rows, 5 * width), BF),
            jax.ShapeDtypeStruct((8, depth), F32),
            jax.ShapeDtypeStruct((taps.shape[0], width), F32),
        ),
        in_specs=[SMEM] * 4 + [VMEM] * 2 + [AWAY] * SAVED,
        out_specs=(VMEM,) * 4,
        scratch_shapes=[pltpu.VMEM(*entry) for entry in saved]
        + [
            pltpu.VMEM((rows, rows), F32),
            pltpu.VMEM((rows, width), BF),
            pltpu.VMEM((rows, width), F32),
            pltpu.VMEM((rows, width), F32),
            pltpu.VMEM((rows, width), F32),
            pltpu.VMEM((rows, width), F32),
            pltpu.SemaphoreType.DMA((SAVED,)),
        ],
        compiler_params=LIMIT,
        name="attend_backward",
    )(deal, place, lengths, live, d_out, taps, *kept)


def steps_of(axis, descending):
    size = lax.axis_size(axis)
    bits = []
    bit = 1
    while bit < size:
        bits.append((axis, bit))
        bit *= 2
    return bits[::-1] if descending else bits


def swap(value, axis, bit):
    size = lax.axis_size(axis)
    return lax.ppermute(value, axis, [(i, i ^ bit) for i in range(size)])


def spread_rows(value, steps):
    for axis, bit in steps:
        value = jnp.concatenate([value, swap(value, axis, bit)], axis=0)
    return value


def gather_rows(value, steps):
    for axis, bit in steps[::-1]:
        half = value.shape[0] // 2
        value = value[:half] + swap(value[half:].astype(BF), axis, bit).astype(F32)
    return value


def in_order(mine, other):
    first = lax.axis_index("shard") == 0
    return jnp.stack([jnp.where(first, mine, other), jnp.where(first, other, mine)])


def over_shard(value):
    if lax.axis_size("shard") == 2:
        return in_order(value, swap(value, "shard", 1))
    return lax.all_gather(value, "shard", axis=0, tiled=False)


def across_shard(parts):
    if lax.axis_size("shard") == 2:
        shard = lax.axis_index("shard")
        mine = lax.dynamic_index_in_dim(parts, shard, axis=0, keepdims=False)
        sent = lax.dynamic_index_in_dim(parts, 1 - shard, axis=0, keepdims=False)
        return in_order(mine, swap(sent, "shard", 1))
    return deal_out(parts, "shard")


def sum_shard(parts):
    if lax.axis_size("shard") == 2:
        shard = lax.axis_index("shard")
        mine = lax.dynamic_index_in_dim(parts, shard, axis=0, keepdims=False)
        sent = lax.dynamic_index_in_dim(parts, 1 - shard, axis=0, keepdims=False)
        return mine.astype(F32) + swap(sent, "shard", 1).astype(F32)
    return jnp.sum(deal_out(parts, "shard").astype(F32), axis=0)


def over_ctx(value):
    ranks = lax.axis_size("ctx")
    got = [value] + [
        lax.ppermute(value, "ctx", [(i, (i + k) % ranks) for i in range(ranks)])
        for k in range(1, ranks)
    ]
    return got


def sum_over(value, steps):
    for axis, bit in steps:
        value = value + swap(value, axis, bit)
    return value


def deal_out(value, axis):
    return lax.all_to_all(value, axis, split_axis=0, concat_axis=0, tiled=True)


def norm_back(value, inverse, gain, grad):
    scaled = grad * gain
    return inverse * scaled - value * inverse**3 * jnp.mean(scaled * value, axis=1, keepdims=True)


def local(
    tokens, cotangent, valid_mask, lengths, deal, attn_gain,
    w_query, w_key, w_value, w_house, w_beta, conv_taps, w_out,
    mlp_gain, w_gate, w_up, w_down,
):
    shards, ranks, lanes = (lax.axis_size(a) for a in ("shard", "ctx", "tp"))
    shard, rank, lane = (lax.axis_index(a) for a in ("shard", "ctx", "tp"))
    span, depth = tokens.shape
    share, columns = w_query.shape
    heads = w_beta.shape[1]
    width = columns // heads
    piece = span // 2
    group = ranks * span
    small = span // lanes
    part = w_gate.shape[1] // shards
    spare = ranks - heads
    tp_steps = steps_of("tp", True)
    plane_steps = steps_of("shard", False) + tp_steps
    live = (rank < heads).astype(jnp.int32).reshape(1, 1)
    head_at = jnp.minimum(rank, heads - 1)

    blocks = jnp.stack([w_query, w_key, w_value, w_house]).reshape(4, share, heads, width)
    blocks = blocks.transpose(2, 1, 0, 3).reshape(heads, share, 4 * width)
    beta_rows = jnp.pad(w_beta.T.reshape(heads, 1, share), ((0, 0), (0, 15), (0, 4 * width - share)))
    blocks = jnp.pad(jnp.concatenate([blocks, beta_rows], axis=1), ((0, spare), (0, 0), (0, 0)))
    crossed, slots_of = [], []
    for k in range(ranks):
        block = lax.dynamic_index_in_dim(blocks, (rank + k) % ranks, axis=0, keepdims=False)
        if k:
            block = lax.ppermute(
                block, "ctx",
                [(i, (i + k) % ranks) for i in range(ranks) if (i + k) % ranks < heads],
            )
        crossed.append(block)
    taps = lax.dynamic_slice_in_dim(conv_taps, head_at * width, width, axis=1)

    half = lane % 2
    own = lax.dynamic_slice_in_dim(tokens, half * piece, piece, axis=0)
    near = over_ctx(own)
    owners = (rank - jnp.arange(ranks, dtype=jnp.int32)) % ranks
    held = jnp.concatenate([2 * owners + half, 2 * owners + 1 - half])
    labels = jnp.arange(2 * ranks, dtype=jnp.int32)
    spot = jnp.sum(jnp.where(deal[0][None, :] == held[:, None], labels[None, :], 0), axis=1)[None]

    def parted(weight):
        return weight.reshape(share, shards, part).transpose(1, 0, 2)

    wo_rows = over_shard(w_out.T)
    hidden = jnp.concatenate([parted(w_gate), parted(w_up), parted(w_down.T)], axis=2)
    hidden = across_shard(hidden).reshape(shards * share, 3 * part)
    hidden, near, crossed = lax.optimization_barrier((hidden, near, crossed))
    hidden = lax.all_gather(hidden, "ctx", axis=0, tiled=True)
    wg_all, wu_all, wd_all = (hidden[:, i * part:(i + 1) * part] for i in range(3))
    x_parts = list(near) + [swap(part_, "tp", 1) for part_ in near]
    w_parts = []
    for k, block in enumerate(crossed):
        source = (rank - k) % ranks
        if shards == 2:
            w_parts += [block, swap(block, "shard", 1)]
            slots_of += [shard * ranks + source, (1 - shard) * ranks + source]
        else:
            every = lax.all_gather(block, "shard", axis=0, tiled=False)
            w_parts += [every[i] for i in range(shards)]
            slots_of += [i * ranks + source for i in range(shards)]
    slot = jnp.stack(slots_of)[None]
    wo_near = jnp.stack(over_ctx(wo_rows))
    wo_t = jnp.take(wo_near, (rank - jnp.arange(ranks)) % ranks, axis=0)
    wo_t = wo_t.transpose(1, 0, 2, 3).reshape(depth, columns)

    def to_plane(value):
        value = value.reshape(-1, shards, ranks, share).transpose(0, 2, 1, 3)
        return value.reshape(-1, depth)

    def from_plane(value):
        value = value.reshape(-1, ranks, shards, share).transpose(0, 2, 1, 3)
        return value.reshape(-1, depth)

    def my_rows(value):
        return lax.dynamic_slice_in_dim(value, lane * small, small, axis=0)

    grad_own = my_rows(cotangent)
    grad_plane = spread_rows(to_plane(grad_own), plane_steps)

    fwd = attend_forward(deal, spot, slot, lengths, x_parts, attn_gain[None], w_parts, taps)
    head_out, saved = fwd[0], fwd[1:]
    h1 = saved[2]
    slots = jnp.arange(lanes, dtype=jnp.int32)
    order = jnp.full_like(slots, lane)
    for index, (_, bit) in enumerate(tp_steps):
        order = order ^ jnp.where((slots >> index) % 2 == 1, bit, 0)
    o_rows = deal_out(head_out.reshape(ranks, span, width), "ctx")[:heads]
    o_rows = o_rows.reshape(heads, lanes, small, width).transpose(1, 2, 0, 3)
    o_rows = jnp.take(o_rows, order, axis=0).reshape(span, columns)
    attn = gather_rows(dg(o_rows, wo_t, 1, 1), tp_steps)
    x_own = my_rows(tokens).astype(F32)
    middle = x_own + attn
    gain_two = mlp_gain.astype(F32)
    inv_two = lax.rsqrt(jnp.mean(middle * middle, axis=1, keepdims=True) + EPS)
    normed = (middle * inv_two * gain_two).astype(BF)
    h2 = spread_rows(to_plane(normed), plane_steps)

    gate = dg(h2, wg_all, 1, 0)
    up = dg(h2, wu_all, 1, 0)
    sig = jax.nn.sigmoid(gate)
    swish = gate * sig
    act = (swish * up).astype(BF)
    d_act = dg(grad_plane, wd_all, 1, 0)
    d_gate = (d_act * up * sig * (1.0 + gate * (1.0 - sig))).astype(BF)
    d_up = (d_act * swish).astype(BF)
    d_two = dg(d_gate, wg_all, 1, 1) + dg(d_up, wu_all, 1, 1)
    d_two = gather_rows(d_two, plane_steps[-1:])
    down_grad = dg(grad_plane, act, 0, 0).astype(BF)
    pair_grad = dg(h2, jnp.concatenate([d_gate, d_up], axis=1), 0, 0).astype(BF)
    d_two, down_grad, pair_grad = lax.optimization_barrier((d_two, down_grad, pair_grad))
    down_sum = lax.psum_scatter(down_grad, "ctx", scatter_dimension=0, tiled=True)
    pair_sum = lax.psum_scatter(pair_grad, "ctx", scatter_dimension=0, tiled=True)
    d_two = gather_rows(d_two, plane_steps[:-1])
    d_two = from_plane(d_two)

    def give_back(grad):
        count = grad.shape[1] // part
        grad = across_shard(grad.reshape(shards, share, count * part))
        grad = grad.reshape(shards, share, count, part).transpose(2, 1, 0, 3)
        return grad.reshape(count, share, shards * part).astype(F32)

    d_gain_two = jnp.sum(d_two * middle * inv_two, axis=0)
    d_middle = grad_own.astype(F32) + norm_back(middle, inv_two, gain_two, d_two)
    d_attn = spread_rows(d_middle.astype(BF), tp_steps)
    d_heads = dg(d_attn, wo_t, 1, 0).astype(BF).reshape(lanes, small, heads, width)
    natural = jnp.zeros_like(slots)
    for index, (_, bit) in enumerate(tp_steps):
        natural = natural + jnp.where(((slots ^ lane) & bit) != 0, 1 << index, 0)
    d_heads = jnp.take(d_heads, natural, axis=0).transpose(2, 0, 1, 3).reshape(heads, span, width)
    d_heads = deal_out(jnp.pad(d_heads, ((0, spare), (0, 0), (0, 0))), "ctx")
    given = jnp.arange(group // small, dtype=jnp.int32)
    apart = (given % lanes) ^ lane
    turned = jnp.zeros_like(apart)
    for index, (_, bit) in enumerate(tp_steps):
        turned = turned + jnp.where((apart & bit) != 0, 1 << index, 0)
    place = (turned * ranks + given // lanes)[None]
    d_one, d_proj, d_small, d_taps = attend_backward(
        deal, place, lengths, live, d_heads.reshape(group, width), taps, depth, saved
    )
    gain_one = attn_gain.astype(F32)
    mine = (jnp.arange(heads) == rank).astype(F32)
    taps_part = (mine[None, :, None] * d_taps[:, None]).reshape(conv_taps.shape)
    taps_part = jnp.pad(taps_part, ((0, 0), (0, depth - columns)))
    sums = jnp.concatenate(
        [d_small[:1], d_gain_two[None], mine[:, None] * d_small[1][None], taps_part], axis=0
    )
    sum_steps = steps_of("ctx", False) + steps_of("shard", False)

    d_one = gather_rows(d_one, tp_steps[-1:])
    mlp = dg(act, wd_all, 1, 1)
    mlp = gather_rows(mlp, plane_steps[-1:])
    sums = sum_over(sums, sum_steps[:1])
    d_one, mlp, sums, d_proj, d_attn = lax.optimization_barrier((d_one, mlp, sums, d_proj, d_attn))

    d_one = gather_rows(d_one, tp_steps[:-1]).astype(BF).reshape(ranks, small, depth)
    d_w = dg(h1, d_proj[:, :4 * width], 0, 0).astype(BF)
    d_w = sum_shard(d_w.reshape(shards, ranks * share, 4 * width)).astype(BF)
    d_wout = dg(d_attn, o_rows, 0, 0).astype(BF)
    d_wout = sum_shard(d_wout.reshape(shards, ranks * share, columns)).astype(BF)
    sums = sum_over(sums, sum_steps[1:2])
    d_one, d_w, d_wout, mlp, sums = lax.optimization_barrier((d_one, d_w, d_wout, mlp, sums))

    total = lax.dynamic_index_in_dim(d_one, rank, axis=0, keepdims=False).astype(F32)
    for k in range(1, ranks):
        sent = lax.dynamic_index_in_dim(d_one, (rank + k) % ranks, axis=0, keepdims=False)
        got = lax.ppermute(sent, "ctx", [(i, (i + k) % ranks) for i in range(ranks)])
        total = total + got.astype(F32)
    d_one = total
    mlp = from_plane(gather_rows(mlp, plane_steps[:-1]))
    result = middle + mlp
    mask = my_rows(valid_mask).astype(F32)
    totals = jnp.stack(
        [jnp.sum(mask * jnp.sum(b * b, axis=1)) for b in (x_own, attn, mlp, result)]
        + [jnp.sum(mask)]
    )
    sums = sum_over(sums, sum_steps[2:])
    d_one, result, sums, d_w, d_wout, totals, down_sum, pair_sum = lax.optimization_barrier(
        (d_one, result, sums, d_w, d_wout, totals, down_sum, pair_sum)
    )

    inv_one = lax.rsqrt(jnp.mean(x_own * x_own, axis=1, keepdims=True) + EPS)
    d_input = d_middle + norm_back(x_own, inv_one, gain_one, d_one)
    ends = jnp.stack([d_input.astype(BF), result.astype(BF)], axis=1)
    ends = spread_rows(ends, tp_steps).reshape(lanes, small, 2, depth)
    ends = jnp.take(ends, natural, axis=0).reshape(span, 2, depth)
    d_tokens, output = ends[:, 0], ends[:, 1]
    d_w = deal_out(d_w.reshape(ranks, share, 4 * width), "ctx")[:heads].astype(F32)
    d_w = d_w.reshape(heads, share, 4, width).transpose(2, 1, 0, 3).reshape(4, share, columns)
    d_wout = deal_out(d_wout.reshape(ranks, share, columns), "ctx")
    d_wout = jnp.sum(d_wout.astype(F32), axis=0).T
    d_wdown = give_back(down_sum)[0].T
    d_wgate, d_wup = give_back(pair_sum)
    one_two = sum_over(sums[:2], tp_steps)
    totals = sum_over(totals[None], sum_steps + tp_steps)[0]
    one_sum, two_sum = one_two[0] / gain_one, one_two[1]
    beta_sum, taps_sum = sums[2:2 + heads], sums[2 + heads:]
    d_beta = lax.dynamic_slice_in_dim(beta_sum, (shard * ranks + rank) * share, share, axis=1).T
    d_conv = taps_sum[:, :columns]
    rms_stats = jnp.sqrt(totals[:4] / (jnp.maximum(totals[4], 1.0) * depth))
    return (
        output, d_tokens, one_sum, d_w[0], d_w[1], d_w[2], d_w[3], d_beta, d_conv,
        d_wout, two_sum, d_wgate, d_wup, d_wdown, rms_stats,
    )


def solution(mesh):
    rows = P(("shard", "ctx"), None)
    tiled = P(("shard", "ctx"), "tp")
    turned = P("tp", ("shard", "ctx"))
    placed = (
        rows, rows, P(("shard", "ctx")), P("shard", None), P("shard", None), P(),
        tiled, tiled, tiled, tiled, tiled, P(None, "tp"), turned, P(), tiled, tiled, turned,
    )
    return jax.shard_map(
        local,
        mesh=mesh,
        in_specs=placed,
        out_specs=(
            rows, rows, P(), tiled, tiled, tiled, tiled, tiled, P(None, "tp"),
            turned, P(), tiled, tiled, turned, P(),
        ),
        check_vma=False,
    )
```

```python
import functools

import jax
import jax.numpy as jnp
from jax import lax
from jax.experimental import pallas as pl
from jax.experimental.pallas import tpu as pltpu
from jax.sharding import PartitionSpec as P

EPS = 1e-06
NEG = -1e30
BF = jnp.bfloat16
F32 = jnp.float32
CHUNK = 128


def dg(left, right, cl, cr):
    return lax.dot_general(left, right, (((cl,), (cr,)), ((), ())), preferred_element_type=F32)


def halves(value):
    high = value.astype(BF)
    return high, (value - high.astype(F32)).astype(BF)


def joined(pairs, cl=1, cr=0):
    lefts, rights = [], []
    for left, right in pairs:
        if left.dtype == BF and right.dtype == BF:
            lefts += [left]
            rights += [right]
        elif left.dtype == BF:
            lefts += [left, left]
            rights += halves(right)
        elif right.dtype == BF:
            lefts += halves(left)
            rights += [right, right]
        else:
            lh, ll = halves(left)
            rh, rl = halves(right)
            lefts += [lh, lh, ll]
            rights += [rh, rl, rh]
    return dg(jnp.concatenate(lefts, axis=cl), jnp.concatenate(rights, axis=cr), cl, cr)


def mm(left, right, cl=1, cr=0):
    return joined([(left, right)], cl, cr)


def ml(left, right, cl=1, cr=0):
    return dg(left.astype(BF), right.astype(BF), cl, cr)


def seg_at(position, ends):
    seg = (position >= ends[0]).astype(jnp.int32)
    for end in ends[1:]:
        seg = seg + (position >= end).astype(jnp.int32)
    return seg


def seq_ends(len_ref):
    ends = [len_ref[0, 0]]
    for index in range(1, len_ref.shape[1] - 1):
        ends.append(ends[-1] + len_ref[0, index])
    return ends


def shifted_mask(rows, width, shift, ends):
    here = lax.broadcasted_iota(jnp.int32, (rows, width), 0)
    back = here - shift
    return (back >= 0) & (seg_at(here, ends) == seg_at(back, ends))


def tile_iota():
    row = lax.broadcasted_iota(jnp.int32, (CHUNK, CHUNK), 0)
    col = lax.broadcasted_iota(jnp.int32, (CHUNK, CHUNK), 1)
    return row, col


def forward_kernel(x_count, w_count, *refs):
    deal_ref, spot_ref, slot_ref, len_ref = refs[:4]
    here_ref, refs = refs[4], refs[5:]
    x_refs, refs = refs[:x_count], refs[x_count:]
    gain_ref, refs = refs[0], refs[1:]
    w_refs, refs = refs[:w_count], refs[w_count:]
    taps_ref, o_ref, refs = refs[0], refs[1], refs[2:]
    kept, refs = refs[:SAVED], refs[SAVED:]
    held, (proj_ref, score_ref, sems) = refs[:SAVED], refs[SAVED:]
    (
        w_ref, wb_ref, h1_ref, q_ref, k_ref, v_ref, house_ref, raw_ref, logit_ref, prob_ref,
        u_ref, kt_ref, tr_ref, tinv_ref, xq_ref, yk_ref, z_ref,
    ) = held
    small, depth = x_refs[0].shape
    pieces = deal_ref.shape[1]
    rows = here_ref.shape[0] + small * x_count
    piece = rows // pieces
    chunks = rows // CHUNK
    width = o_ref.shape[1]
    share = depth // w_count
    scale = width ** (-0.5)
    ends = seq_ends(len_ref)
    gain = gain_ref[...].astype(F32)

    def keep(first, last):
        for index in range(first, last):
            pltpu.make_async_copy(held[index], kept[index], sems.at[index]).start()

    pick = jnp.where(
        (lax.broadcasted_iota(jnp.int32, (16, width), 0) == 0)
        & (lax.broadcasted_iota(jnp.int32, (16, width), 1) == 0),
        1.0,
        0.0,
    ).astype(BF)
    for index, ref in enumerate(w_refs):
        base = pl.multiple_of(slot_ref[0, index] * share, share)
        w_ref[pl.ds(base, share), :] = ref[:share, :]
        wb_ref[pl.ds(base, share), :] = dg(ref[share:, :share], pick, 0, 0).astype(BF)

    def settle(x, index):
        x = x.astype(F32)
        inv = lax.rsqrt(jnp.mean(x * x, axis=1, keepdims=True) + EPS)
        base = pl.multiple_of(spot_ref[0, index] * small, small)
        h1_ref[pl.ds(base, small), :] = (x * inv * gain).astype(BF)

    local_count = here_ref.shape[0] // small
    for index in range(local_count):
        settle(here_ref[index * small:(index + 1) * small, :], index)
    for index, ref in enumerate(x_refs):
        settle(ref[...], local_count + index)
    keep(0, 3)

    def project(step, carry):
        base = pl.multiple_of(step * piece, piece)
        h1 = h1_ref[pl.ds(base, piece), :]
        proj_ref[pl.ds(base, piece), :] = dg(h1, w_ref[...], 1, 0)
        logit_ref[pl.ds(base, piece), :] = dg(h1, wb_ref[...], 1, 0)
        return carry

    lax.fori_loop(0, pieces, project, 0)
    q_ref[...] = proj_ref[:, :width].astype(BF)
    k_ref[...] = proj_ref[:, width:2 * width].astype(BF)
    v_ref[...] = proj_ref[:, 2 * width:3 * width].astype(BF)
    raw = proj_ref[:, 3 * width:4 * width]
    raw_ref[...] = raw
    taps = taps_ref[...].astype(F32)
    mixed = taps[0:1, :] * raw
    for shift in range(1, taps.shape[0]):
        moved = pltpu.roll(raw, shift, 0)
        mixed = mixed + taps[shift:shift + 1, :] * jnp.where(
            shifted_mask(rows, width, shift, ends), moved, 0.0
        )
    unit = mixed * lax.rsqrt(jnp.sum(mixed * mixed, axis=1, keepdims=True) + EPS)
    house_ref[...] = unit.astype(BF)
    keep(3, 9)

    row, col = tile_iota()
    strict = row > col
    eye = jnp.where(row == col, 1.0, 0.0)
    spans = [slice(n * CHUNK, (n + 1) * CHUNK) for n in range(chunks)]
    strength = [2.0 * jax.nn.sigmoid(logit_ref[s, 0:1]) for s in spans]
    system = []
    for n, s in enumerate(spans):
        house = house_ref[s, :]
        system.append(jnp.where(strict, strength[n] * dg(house, house, 1, 1), 0.0))
    inverse = [eye - jnp.where((row ^ col) == 1, a, 0.0) for a in system]
    level = 1
    while (1 << level) < CHUNK:
        block = ((row ^ col) >> level) == 1
        inner = [mm(jnp.where(block, a, 0.0), t) for a, t in zip(system, inverse)]
        inverse = [t - mm(t, i) for t, i in zip(inverse, inner)]
        level += 1
    for n, s in enumerate(spans):
        query, key, house = q_ref[s, :], k_ref[s, :], house_ref[s, :]
        tinv = inverse[n]
        tinv_ref[s, :] = tinv
        across = jnp.transpose(jnp.broadcast_to(strength[n], (CHUNK, CHUNK)))
        merged = tinv * across
        a_qw = jnp.where(row >= col, dg(query, house, 1, 1), 0.0)
        a_wk = jnp.where(strict, dg(house, key, 1, 1), 0.0)
        xq = mm(a_qw, merged)
        yk = mm(merged, a_wk)
        zz = mm(merged, house)
        xq_ref[s, :] = xq
        yk_ref[s, :] = yk
        z_ref[s, :] = zz
        score_ref[s, s] = (dg(query, key, 1, 1) - mm(xq, a_wk)) * scale
        proj_ref[s, :width] = query.astype(F32) - mm(xq, house)
        kt_ref[s, :] = key.astype(F32) - mm(yk, house, 0, 0)
        tr_ref[s, :] = eye - mm(house, zz, 0, 0)
    keep(11, SAVED)
    offset = 0
    for n in range(chunks - 2, -1, -1):
        later = slice((n + 1) * CHUNK, rows)
        count = rows - (n + 1) * CHUNK
        carried = proj_ref[later, :width]
        u_ref[offset:offset + count, :] = carried
        offset += count
        score_ref[later, spans[n]] = mm(carried, kt_ref[spans[n], :], 1, 1) * scale
        if n > 0:
            proj_ref[later, :width] = mm(carried, tr_ref[spans[n], :])
    keep(10, 11)
    for m, s in enumerate(spans):
        reach = (m + 1) * CHUNK
        at_row = lax.broadcasted_iota(jnp.int32, (CHUNK, reach), 0) + m * CHUNK
        at_col = lax.broadcasted_iota(jnp.int32, (CHUNK, reach), 1)
        seen = (at_row >= at_col) & (seg_at(at_row, ends) == seg_at(at_col, ends))
        logits = jnp.where(seen, score_ref[s, :reach], NEG)
        top = jnp.max(logits, axis=1, keepdims=True)
        grown = jnp.exp(logits - top)
        prob = grown / jnp.sum(grown, axis=1, keepdims=True)
        prob_ref[s, :reach] = prob
        proj_ref[s, :width] = dg(prob.astype(BF), v_ref[:reach, :], 1, 0)

    def give(step, carry):
        base = pl.multiple_of(step * piece, piece)
        given = pl.multiple_of(deal_ref[0, step] * piece, piece)
        o_ref[pl.ds(given, piece), :] = proj_ref[pl.ds(base, piece), :width].astype(BF)
        return carry

    keep(9, 10)
    lax.fori_loop(0, pieces, give, 0)
    for index in range(SAVED):
        pltpu.make_async_copy(held[index], kept[index], sems.at[index]).wait()


def backward_kernel(*refs):
    deal_ref, place_ref, source_ref, len_ref, live_ref, do_ref, taps_ref = refs[:7]
    kept, refs = refs[7:7 + SAVED], refs[7 + SAVED:]
    (dh1_ref, dproj_ref, small_ref, dtaps_ref), refs = refs[:4], refs[4:]
    held, refs = refs[:SAVED], refs[SAVED:]
    ds_ref, dout_ref, du_ref, dkt_ref, dtr_ref, dhouse_ref, sems = refs
    (
        w_ref, wb_ref, h1_ref, q_ref, k_ref, v_ref, house_ref, raw_ref, logit_ref, prob_ref,
        u_ref, kt_ref, tr_ref, tinv_ref, xq_ref, yk_ref, z_ref,
    ) = held

    def fetch(index):
        return pltpu.make_async_copy(kept[index], held[index], sems.at[index])

    needed = (5, 9), (10, 11, 12), (3, 4, 6, 8, 13, 14, 15, 16), (7,), (0, 1, 2)
    for index in sum(needed, ()):
        fetch(index).start()

    def ready(stage):
        for index in needed[stage]:
            fetch(index).wait()

    rows = do_ref.shape[0]
    pieces = deal_ref.shape[1]
    piece = rows // pieces
    small = rows // place_ref.shape[1]
    chunks = rows // CHUNK
    width = do_ref.shape[1]
    scale = width ** (-0.5)
    ends = seq_ends(len_ref)
    spans = [slice(n * CHUNK, (n + 1) * CHUNK) for n in range(chunks)]
    row, col = tile_iota()
    strict = row > col

    def take(step, carry):
        base = pl.multiple_of(step * piece, piece)
        for part in range(piece // small):
            there = source_ref[0, deal_ref[0, step] * (piece // small) + part]
            dout_ref[pl.ds(base + part * small, small), :] = do_ref[
                pl.ds(pl.multiple_of(there * small, small), small), :
            ]
        return carry

    lax.fori_loop(0, pieces, take, 0)
    ready(0)
    for m, s in enumerate(spans):
        reach = (m + 1) * CHUNK
        prob = prob_ref[s, :reach]
        dprob = dg(dout_ref[s, :], v_ref[:reach, :], 1, 1)
        dot = jnp.sum(prob * dprob, axis=1, keepdims=True)
        ds_ref[s, :reach] = prob * (dprob - dot) * scale
    for n, s in enumerate(spans):
        dproj_ref[s, 2 * width:3 * width] = dg(
            prob_ref[n * CHUNK:, s].astype(BF), dout_ref[n * CHUNK:, :], 0, 0
        ).astype(BF)
    starts = {}
    offset = 0
    for n in range(chunks - 2, -1, -1):
        starts[n] = offset
        offset += rows - (n + 1) * CHUNK
    ready(1)
    for n in range(chunks - 1):
        later = slice((n + 1) * CHUNK, rows)
        count = rows - (n + 1) * CHUNK
        grad = ds_ref[later, spans[n]]
        carried = u_ref[starts[n]:starts[n] + count, :]
        dkt_ref[spans[n], :] = mm(grad, carried, 0, 0)
        fresh = mm(grad, kt_ref[spans[n], :])
        if n > 0:
            before = du_ref[later, :]
            dtr_ref[spans[n], :] = mm(carried, before, 0, 0)
            fresh = fresh + mm(before, tr_ref[spans[n], :], 1, 1)
        du_ref[later, :] = fresh
    ready(2)
    for n, s in enumerate(spans):
        query, key, house = q_ref[s, :], k_ref[s, :], house_ref[s, :]
        strength = 2.0 * jax.nn.sigmoid(logit_ref[s, 0:1])
        tinv = tinv_ref[s, :]
        merged = tinv * jnp.transpose(jnp.broadcast_to(strength, (CHUNK, CHUNK)))
        a_qw = jnp.where(row >= col, dg(query, house, 1, 1), 0.0)
        a_wk = jnp.where(strict, dg(house, key, 1, 1), 0.0)
        gram = jnp.where(strict, dg(house, house, 1, 1), 0.0)
        xq, yk, zz = xq_ref[s, :], yk_ref[s, :], z_ref[s, :]
        di = ds_ref[s, s]
        first, final = n == 0, n == chunks - 1
        if first:
            dxq = mm(di, a_wk, 1, 1)
            da_qw = mm(di, yk, 1, 1)
        else:
            dqt = du_ref[s, :]
            dxq = joined([(di, a_wk), (dqt, house)], 1, 1)
            da_qw = joined([(di, yk), (dqt, zz)], 1, 1)
        da_qw = jnp.where(row >= col, da_qw, 0.0)
        dm = mm(a_qw, dxq, 0, 0)
        cross = [(xq, di)]
        if not final:
            dkt = dkt_ref[s, :]
            dyk = mm(house, dkt, 1, 1)
            cross.append((merged, dyk))
            outer = [(dyk, a_wk)]
            if not first:
                dtr = dtr_ref[s, :]
                wd = mm(house, dtr)
                outer.append((wd, house))
            dm = dm + joined(outer, 1, 1)
        da_wk = jnp.where(strict, joined(cross, 0, 0), 0.0)
        ee = mm(tinv, dm, 0, 0)
        rest = jnp.where(row == col, 1.0, 0.0) - mm(gram, merged)
        dstrength = -jnp.sum(ee * rest, axis=1, keepdims=True)
        dgram = jnp.where(strict, mm(strength * ee, merged, 1, 1), 0.0)
        dq = joined([(di, key), (-da_qw, house)])
        dk = joined([(di, query), (-da_wk, house)], 0, 0)
        tall = [(da_qw, query), (-dgram, house)]
        wide = [(da_wk, key), (-dgram, house)]
        if not first:
            dq = dq + dqt
            tall.append((xq, dqt))
        if not final:
            dk = dk + dkt
            wide.append((yk, dkt))
            if not first:
                tall.append((merged, wd))
        dw = joined(tall, 0, 0) + joined(wide)
        if not first and not final:
            dw = dw + mm(zz, dtr, 1, 1)
        dw = -dw
        dproj_ref[s, :width] = dq.astype(BF)
        dproj_ref[s, width:2 * width] = dk.astype(BF)
        dhouse_ref[s, :] = dw
        gate = 0.5 * strength
        dlogit = dstrength * 2.0 * gate * (1.0 - gate)
        lane = lax.broadcasted_iota(jnp.int32, (CHUNK, width), 1)
        dproj_ref[s, 4 * width:] = jnp.where(lane == 0, dlogit, 0.0).astype(BF)
    ready(3)
    raw = raw_ref[...]
    taps = taps_ref[...].astype(F32)
    count = taps.shape[0]
    mixed = taps[0:1, :] * raw
    earlier = [raw]
    masks = [None]
    for shift in range(1, count):
        masks.append(shifted_mask(rows, width, shift, ends))
        earlier.append(jnp.where(masks[shift], pltpu.roll(raw, shift, 0), 0.0))
        mixed = mixed + taps[shift:shift + 1, :] * earlier[shift]
    inv = lax.rsqrt(jnp.sum(mixed * mixed, axis=1, keepdims=True) + EPS)
    dunit = dhouse_ref[...]
    dmixed = inv * dunit - mixed * (
        inv * inv * inv * jnp.sum(dunit * mixed, axis=1, keepdims=True)
    )
    live = live_ref[0, 0].astype(F32)
    draw = taps[0:1, :] * dmixed
    dtaps_ref[0:1, :] = jnp.sum(dmixed * raw, axis=0, keepdims=True) * live
    for shift in range(1, count):
        dtaps_ref[shift:shift + 1, :] = (
            jnp.sum(dmixed * earlier[shift], axis=0, keepdims=True) * live
        )
        later = jnp.where(masks[shift], dmixed, 0.0)
        draw = draw + taps[shift:shift + 1, :] * pltpu.roll(later, rows - shift, 0)
    dproj_ref[:, 3 * width:4 * width] = draw.astype(BF)

    ready(4)

    def send(step, total):
        base = pl.multiple_of(step * piece, piece)
        grads = dproj_ref[pl.ds(base, piece), :]
        dh1 = dg(grads[:, :4 * width], w_ref[...], 1, 1) + dg(grads[:, 4 * width:], wb_ref[...], 1, 1)
        dh1 = dh1 * live
        h1 = h1_ref[pl.ds(base, piece), :].astype(F32)
        total = total + jnp.sum(dh1 * h1, axis=0, keepdims=True)
        dh1 = dh1.astype(dh1_ref.dtype)
        for part in range(piece // small):
            there = place_ref[0, deal_ref[0, step] * (piece // small) + part]
            dh1_ref[pl.ds(pl.multiple_of(there * small, small), small), :] = dh1[
                part * small:(part + 1) * small
            ]
        return total

    small_ref[...] = jnp.zeros_like(small_ref)
    small_ref[0:1, :] = lax.fori_loop(0, pieces, send, jnp.zeros((1, h1_ref.shape[1]), F32))
    beta = dg(dproj_ref[:, 4 * width:], h1_ref[...], 0, 0)
    small_ref[1:2, :] = beta[0:1, :] * live


SAVED = 17


def saved_shapes(rows, depth, width):
    chunks = rows // CHUNK
    carried = CHUNK * chunks * (chunks - 1) // 2
    slim = ((rows, width), BF)
    tall = ((rows, width), F32)
    return (
        ((depth, 4 * width), BF), ((depth, width), BF), ((rows, depth), BF), slim, slim, slim, slim,
        tall, tall, ((rows, rows), F32), ((carried, width), F32), tall, tall, tall, tall, tall, tall,
    )


VMEM = pl.BlockSpec(memory_space=pltpu.VMEM)
SMEM = pl.BlockSpec(memory_space=pltpu.SMEM)
AWAY = pl.BlockSpec(memory_space=pl.ANY)
LIMIT = pltpu.CompilerParams(vmem_limit_bytes=56 * 1024 * 1024)


def attend_forward(deal, spot, slot, lengths, here, x_parts, gain, w_parts, taps):
    small, depth = x_parts[0].shape
    rows = here.shape[0] + small * len(x_parts)
    width = taps.shape[1]
    saved = saved_shapes(rows, depth, width)
    return pl.pallas_call(
        functools.partial(forward_kernel, len(x_parts), len(w_parts)),
        out_shape=(jax.ShapeDtypeStruct((rows, width), BF),)
        + tuple(jax.ShapeDtypeStruct(*entry) for entry in saved),
        in_specs=[SMEM] * 4 + [VMEM] * (len(x_parts) + len(w_parts) + 3),
        out_specs=(VMEM,) + (AWAY,) * SAVED,
        scratch_shapes=[pltpu.VMEM(*entry) for entry in saved]
        + [
            pltpu.VMEM((rows, 4 * width), F32),
            pltpu.VMEM((rows, rows), F32),
            pltpu.SemaphoreType.DMA((SAVED,)),
        ],
        compiler_params=LIMIT,
        cost_estimate=pl.CostEstimate(flops=16 * 10**9, bytes_accessed=10**7, transcendentals=0),
        name="attend_forward",
    )(deal, spot, slot, lengths, here, *x_parts, gain, *w_parts, taps)


def attend_backward(deal, place, source, lengths, live, d_out, taps, depth, kept):
    rows, width = d_out.shape
    saved = saved_shapes(rows, depth, width)
    return pl.pallas_call(
        backward_kernel,
        out_shape=(
            jax.ShapeDtypeStruct((rows, depth), BF),
            jax.ShapeDtypeStruct((rows, 5 * width), BF),
            jax.ShapeDtypeStruct((8, depth), F32),
            jax.ShapeDtypeStruct((taps.shape[0], width), F32),
        ),
        in_specs=[SMEM] * 5 + [VMEM] * 2 + [AWAY] * SAVED,
        out_specs=(VMEM,) * 4,
        scratch_shapes=[pltpu.VMEM(*entry) for entry in saved]
        + [
            pltpu.VMEM((rows, rows), F32),
            pltpu.VMEM((rows, width), BF),
            pltpu.VMEM((rows, width), F32),
            pltpu.VMEM((rows, width), F32),
            pltpu.VMEM((rows, width), F32),
            pltpu.VMEM((rows, width), F32),
            pltpu.SemaphoreType.DMA((SAVED,)),
        ],
        compiler_params=LIMIT,
        cost_estimate=pl.CostEstimate(flops=20 * 10**9, bytes_accessed=10**7, transcendentals=0),
        name="attend_backward",
    )(deal, place, source, lengths, live, d_out, taps, *kept)


def head_kernel(left_ref, right_ref, out_ref):
    width = out_ref.shape[2]
    heads = right_ref.shape[1] // width
    for head in range(out_ref.shape[0]):
        if head < heads:
            out_ref[head] = dg(
                left_ref[...], right_ref[:, head * width:(head + 1) * width], 1, 0
            ).astype(BF)
        else:
            out_ref[head] = jnp.zeros(out_ref.shape[1:], BF)


def by_head(left, right, width, ranks):
    return pl.pallas_call(
        head_kernel,
        out_shape=jax.ShapeDtypeStruct((ranks, left.shape[0], width), BF),
        in_specs=[VMEM, VMEM],
        out_specs=VMEM,
        compiler_params=LIMIT,
        name="by_head",
    )(left, right)


def pack_kernel(heads, ranks, shards, *refs):
    head_ref, order_ref = refs[:2]
    projections = refs[2:6]
    beta_ref, gate_ref, up_ref, down_ref, out_ref = refs[6:11]
    blocks, parts, turned_ref = refs[11:11 + ranks], refs[11 + ranks:11 + ranks + shards], refs[-1]
    share, columns = projections[0].shape
    width = columns // heads
    part = gate_ref.shape[1] // shards
    eye = jnp.where(
        lax.broadcasted_iota(jnp.int32, (share, share), 0)
        == lax.broadcasted_iota(jnp.int32, (share, share), 1),
        1.0,
        0.0,
    ).astype(BF)
    beta = dg(beta_ref[...], eye, 0, 0)
    for k, block in enumerate(blocks):
        head = head_ref[0, k]
        at = pl.multiple_of(head * width, width)
        for index, ref in enumerate(projections):
            block[:share, index * width:(index + 1) * width] = ref[:, pl.ds(at, width)]
        row = beta[0:1, :]
        for other in range(1, heads):
            row = jnp.where(head == other, beta[other:other + 1, :], row)
        block[share:, :] = jnp.zeros((block.shape[0] - share, block.shape[1]), BF)
        block[share:, :share] = jnp.broadcast_to(row, (block.shape[0] - share, share)).astype(BF)
    for index, ref in enumerate(parts):
        at = pl.multiple_of(order_ref[0, index] * part, part)
        ref[:, :part] = gate_ref[:, pl.ds(at, part)]
        ref[:, part:2 * part] = up_ref[:, pl.ds(at, part)]
        ref[:, 2 * part:] = down_ref[pl.ds(at, part), :].astype(F32).T.astype(BF)
    turned_ref[...] = out_ref[...].astype(F32).T.astype(BF)


def pack(head, order, projections, w_beta, w_gate, w_up, w_down, w_out, ranks):
    share, columns = projections[0].shape
    heads = w_beta.shape[1]
    shards = order.shape[1]
    width = columns // heads
    part = w_gate.shape[1] // shards
    out = pl.pallas_call(
        functools.partial(pack_kernel, heads, ranks, shards),
        out_shape=(jax.ShapeDtypeStruct((share + 16, 4 * width), BF),) * ranks
        + (jax.ShapeDtypeStruct((share, 3 * part), BF),) * shards
        + (jax.ShapeDtypeStruct((share, columns), BF),),
        in_specs=[SMEM, SMEM] + [VMEM] * 9,
        out_specs=(VMEM,) * (ranks + shards + 1),
        compiler_params=LIMIT,
        name="pack",
    )(head, order, *projections, w_beta, w_gate, w_up, w_down, w_out)
    return list(out[:ranks]), list(out[ranks:ranks + shards]), out[-1]


def unpack_hidden_kernel(shards, *refs):
    order_ref, downs, pairs = refs[0], refs[1:1 + shards], refs[1 + shards:1 + 2 * shards]
    gate_ref, up_ref, down_ref = refs[1 + 2 * shards:]
    part = downs[0].shape[1]
    for index in range(shards):
        at = pl.multiple_of(order_ref[0, index] * part, part)
        gate_ref[:, pl.ds(at, part)] = pairs[index][:, :part].astype(F32)
        up_ref[:, pl.ds(at, part)] = pairs[index][:, part:].astype(F32)
        down_ref[pl.ds(at, part), :] = downs[index][...].astype(F32).T


def unpack_hidden(order, downs, pairs):
    shards = len(downs)
    share, part = downs[0].shape
    wide = jax.ShapeDtypeStruct((share, shards * part), F32)
    return pl.pallas_call(
        functools.partial(unpack_hidden_kernel, shards),
        out_shape=(wide, wide, jax.ShapeDtypeStruct((shards * part, share), F32)),
        in_specs=[SMEM] + [VMEM] * (2 * shards),
        out_specs=(VMEM,) * 3,
        compiler_params=LIMIT,
        name="unpack_hidden",
    )(order, *downs, *pairs)


def unpack_heads_kernel(ranks, heads, *refs):
    source_ref, blocks, out_ref = refs[0], refs[1:1 + ranks], refs[1 + ranks]
    grads, turned_ref = refs[2 + ranks:-1], refs[-1]
    width = blocks[0].shape[1] // len(grads)
    for k, block in enumerate(blocks):
        source = source_ref[0, k]

        @pl.when(source < heads)
        def _():
            at = pl.multiple_of(source * width, width)
            for index, ref in enumerate(grads):
                ref[:, pl.ds(at, width)] = block[:, index * width:(index + 1) * width].astype(F32)

    turned_ref[...] = out_ref[...].T


def unpack_heads(source, blocks, d_out, heads):
    ranks = len(blocks)
    share, columns = d_out.shape
    return pl.pallas_call(
        functools.partial(unpack_heads_kernel, ranks, heads),
        out_shape=(jax.ShapeDtypeStruct((share, columns), F32),) * 4
        + (jax.ShapeDtypeStruct((columns, share), F32),),
        in_specs=[SMEM] + [VMEM] * (ranks + 1),
        out_specs=(VMEM,) * 5,
        compiler_params=LIMIT,
        name="unpack_heads",
    )(source, *blocks, d_out)


def steps_of(axis, descending):
    size = lax.axis_size(axis)
    bits = []
    bit = 1
    while bit < size:
        bits.append((axis, bit))
        bit *= 2
    return bits[::-1] if descending else bits


def swap(value, axis, bit):
    size = lax.axis_size(axis)
    return lax.ppermute(value, axis, [(i, i ^ bit) for i in range(size)])


def spread_rows(value, steps):
    for axis, bit in steps:
        value = jnp.concatenate([value, swap(value, axis, bit)], axis=0)
    return value


def gather_rows(value, steps):
    for axis, bit in steps[::-1]:
        half = value.shape[0] // 2
        value = value[:half] + swap(value[half:].astype(BF), axis, bit).astype(F32)
    return value


def in_order(mine, other):
    first = lax.axis_index("shard") == 0
    return jnp.stack([jnp.where(first, mine, other), jnp.where(first, other, mine)])


def over_shard(value):
    if lax.axis_size("shard") == 2:
        return in_order(value, swap(value, "shard", 1))
    return lax.all_gather(value, "shard", axis=0, tiled=False)


def across_shard(parts):
    if lax.axis_size("shard") == 2:
        shard = lax.axis_index("shard")
        mine = lax.dynamic_index_in_dim(parts, shard, axis=0, keepdims=False)
        sent = lax.dynamic_index_in_dim(parts, 1 - shard, axis=0, keepdims=False)
        return in_order(mine, swap(sent, "shard", 1))
    return deal_out(parts, "shard")


def sum_shard(parts):
    if lax.axis_size("shard") == 2:
        shard = lax.axis_index("shard")
        mine = lax.dynamic_index_in_dim(parts, shard, axis=0, keepdims=False)
        sent = lax.dynamic_index_in_dim(parts, 1 - shard, axis=0, keepdims=False)
        return mine.astype(F32) + swap(sent, "shard", 1).astype(F32)
    return jnp.sum(deal_out(parts, "shard").astype(F32), axis=0)


def over_ctx(value):
    ranks = lax.axis_size("ctx")
    got = [value] + [
        lax.ppermute(value, "ctx", [(i, (i + k) % ranks) for i in range(ranks)])
        for k in range(1, ranks)
    ]
    return got


def sum_over(value, steps):
    for axis, bit in steps:
        value = value + swap(value, axis, bit)
    return value


def deal_out(value, axis):
    return lax.all_to_all(value, axis, split_axis=0, concat_axis=0, tiled=True)


def norm_back(value, inverse, gain, grad):
    scaled = grad * gain
    return inverse * scaled - value * inverse**3 * jnp.mean(scaled * value, axis=1, keepdims=True)


def local(
    tokens, cotangent, valid_mask, lengths, deal, attn_gain,
    w_query, w_key, w_value, w_house, w_beta, conv_taps, w_out,
    mlp_gain, w_gate, w_up, w_down,
):
    shards, ranks, lanes = (lax.axis_size(a) for a in ("shard", "ctx", "tp"))
    shard, rank, lane = (lax.axis_index(a) for a in ("shard", "ctx", "tp"))
    span, depth = tokens.shape
    share, columns = w_query.shape
    heads = w_beta.shape[1]
    width = columns // heads
    piece = span // 2
    group = ranks * span
    small = span // lanes
    part = w_gate.shape[1] // shards
    spare = ranks - heads
    tp_steps = steps_of("tp", True)
    plane_steps = steps_of("shard", False) + tp_steps
    live = (rank < heads).astype(jnp.int32).reshape(1, 1)
    head_at = jnp.minimum(rank, heads - 1)

    shifted = over_ctx(lax.dynamic_slice_in_dim(tokens, lane * small, small, axis=0))[1:]

    turn = jnp.arange(ranks, dtype=jnp.int32)
    order_s = jnp.arange(shards, dtype=jnp.int32)
    if shards == 2:
        order_s = order_s ^ shard
    blocks, hidden, wo_rows = pack(
        jnp.minimum((rank + turn) % ranks, heads - 1)[None], order_s[None],
        (w_query, w_key, w_value, w_house), w_beta, w_gate, w_up, w_down, w_out, ranks,
    )
    crossed = [blocks[0]]
    for k in range(1, ranks):
        pairs = [(i, (i + k) % ranks) for i in range(ranks) if (i + k) % ranks < heads]
        crossed.append(lax.ppermute(blocks[k], "ctx", pairs))
    slots_of = []
    taps = lax.dynamic_slice_in_dim(conv_taps, head_at * width, width, axis=1)

    x_parts, apart_of = list(shifted), [0]
    for axis, bit in tp_steps:
        x_parts = x_parts + [swap(part_, axis, bit) for part_ in x_parts]
        apart_of = apart_of + [other ^ bit for other in apart_of]
    owners = (rank - jnp.arange(1, ranks, dtype=jnp.int32)) % ranks
    blocks_of = [rank * lanes + jnp.arange(lanes, dtype=jnp.int32)]
    blocks_of += [owners * lanes + (lane ^ apart) for apart in apart_of]
    blocks_of = jnp.concatenate(blocks_of)
    labels = jnp.arange(2 * ranks, dtype=jnp.int32)
    per_piece = lanes // 2
    at_piece = jnp.sum(
        jnp.where(deal[0][None, :] == (blocks_of // per_piece)[:, None], labels[None, :], 0), axis=1
    )
    spot = (at_piece * per_piece + blocks_of % per_piece)[None]
    w_parts = []
    for k, block in enumerate(crossed):
        source = (rank - k) % ranks
        if shards == 2:
            w_parts += [block, swap(block, "shard", 1)]
            slots_of += [shard * ranks + source, (1 - shard) * ranks + source]
        else:
            every = lax.all_gather(block, "shard", axis=0, tiled=False)
            w_parts += [every[i] for i in range(shards)]
            slots_of += [i * ranks + source for i in range(shards)]
    slot = jnp.stack(slots_of)[None]

    wo_t = over_shard(wo_rows).reshape(shards * share, columns)
    wo_t = lax.all_gather(wo_t, "ctx", axis=0, tiled=False)
    wo_t = wo_t.reshape(ranks, shards, share, columns).transpose(1, 0, 2, 3).reshape(depth, columns)
    if shards == 2:
        hidden = [hidden[0], swap(hidden[1], "shard", 1)]
    else:
        hidden = list(deal_out(jnp.stack(hidden), "shard"))
    hidden, _, _ = lax.optimization_barrier((hidden, shifted, crossed))
    hidden = in_order(*hidden) if shards == 2 else jnp.stack(hidden)
    hidden = hidden.reshape(shards * share, 3 * part)
    hidden = lax.all_gather(hidden, "ctx", axis=0, tiled=True)
    wg_all, wu_all, wd_all = (hidden[:, i * part:(i + 1) * part] for i in range(3))

    def to_plane(value):
        value = value.reshape(-1, shards, ranks, share).transpose(0, 2, 1, 3)
        return value.reshape(-1, depth)

    def from_plane(value):
        value = value.reshape(-1, ranks, shards, share).transpose(0, 2, 1, 3)
        return value.reshape(-1, depth)

    def my_rows(value):
        return lax.dynamic_slice_in_dim(value, lane * small, small, axis=0)

    grad_own = my_rows(cotangent)
    grad_plane = spread_rows(to_plane(grad_own), plane_steps)

    fwd = attend_forward(deal, spot, slot, lengths, tokens, x_parts, attn_gain[None], w_parts, taps)
    head_out, saved = fwd[0], fwd[1:]
    h1 = saved[2]
    slots = jnp.arange(lanes, dtype=jnp.int32)
    order = jnp.full_like(slots, lane)
    for index, (_, bit) in enumerate(tp_steps):
        order = order ^ jnp.where((slots >> index) % 2 == 1, bit, 0)
    natural = jnp.zeros_like(slots)
    for index, (_, bit) in enumerate(tp_steps):
        natural = natural + jnp.where(((slots ^ lane) & bit) != 0, 1 << index, 0)
    o_rows = deal_out(head_out.reshape(ranks, span, width), "ctx")[:heads]
    o_rows = o_rows.reshape(heads, lanes, small, width).transpose(1, 2, 0, 3)
    o_rows = jnp.take(o_rows, order, axis=0).reshape(span, columns)
    attn = gather_rows(dg(o_rows, wo_t, 1, 1), tp_steps)
    x_own = my_rows(tokens).astype(F32)
    middle = x_own + attn
    gain_two = mlp_gain.astype(F32)
    inv_two = lax.rsqrt(jnp.mean(middle * middle, axis=1, keepdims=True) + EPS)
    normed = (middle * inv_two * gain_two).astype(BF)
    h2 = spread_rows(to_plane(normed), plane_steps)

    gate = dg(h2, wg_all, 1, 0)
    up = dg(h2, wu_all, 1, 0)
    sig = jax.nn.sigmoid(gate)
    swish = gate * sig
    act = (swish * up).astype(BF)
    d_act = dg(grad_plane, wd_all, 1, 0)
    d_gate = (d_act * up * sig * (1.0 + gate * (1.0 - sig))).astype(BF)
    d_up = (d_act * swish).astype(BF)
    d_two = dg(d_gate, wg_all, 1, 1) + dg(d_up, wu_all, 1, 1)
    d_two = gather_rows(d_two, plane_steps[-1:])
    down_grad = dg(grad_plane, act, 0, 0).astype(BF)
    d_two, down_grad = lax.optimization_barrier((d_two, down_grad))
    down_sum = lax.psum_scatter(down_grad, "ctx", scatter_dimension=0, tiled=True)
    middle_steps = plane_steps[len(plane_steps) - len(tp_steps):-1]
    d_two = gather_rows(d_two, middle_steps)
    pair_grad = dg(h2, jnp.concatenate([d_gate, d_up], axis=1), 0, 0).astype(BF)
    d_two, pair_grad = lax.optimization_barrier((d_two, pair_grad))
    pair_sum = lax.psum_scatter(pair_grad, "ctx", scatter_dimension=0, tiled=True)
    d_two = gather_rows(d_two, plane_steps[:-len(tp_steps)])
    d_two = from_plane(d_two)

    def by_shard(grad):
        grad = grad.reshape(shards, share, grad.shape[1])
        if shards == 2:
            mine = lax.dynamic_index_in_dim(grad, shard, axis=0, keepdims=False)
            sent = lax.dynamic_index_in_dim(grad, 1 - shard, axis=0, keepdims=False)
            return [mine, swap(sent, "shard", 1)]
        return list(deal_out(grad, "shard"))

    d_gain_two = jnp.sum(d_two * middle * inv_two, axis=0)
    d_middle = grad_own.astype(F32) + norm_back(middle, inv_two, gain_two, d_two)
    d_attn = spread_rows(d_middle.astype(BF), tp_steps)
    d_wout = dg(d_attn, o_rows, 0, 0).astype(BF)
    d_wout = sum_shard(d_wout.reshape(shards, ranks * share, columns)).astype(BF)
    d_heads = deal_out(by_head(d_attn, wo_t, width, ranks), "ctx")
    d_heads, d_wout, down_sum = lax.optimization_barrier((d_heads, d_wout, down_sum))
    mlp = dg(act, wd_all, 1, 1)
    mlp = gather_rows(mlp, plane_steps[-1:])

    given = jnp.arange(group // small, dtype=jnp.int32)
    apart = (given % lanes) ^ lane
    turned = jnp.zeros_like(apart)
    for index, (_, bit) in enumerate(tp_steps):
        turned = turned + jnp.where((apart & bit) != 0, 1 << index, 0)
    place = (turned * ranks + given // lanes)[None]
    source = (given // lanes * lanes + turned)[None]
    d_one, d_proj, d_small, d_taps = attend_backward(
        deal, place, source, lengths, live, d_heads.reshape(group, width), taps, depth, saved
    )
    gain_one = attn_gain.astype(F32)
    mine = (jnp.arange(heads) == rank).astype(F32)
    taps_part = (mine[None, :, None] * d_taps[:, None]).reshape(conv_taps.shape)
    taps_part = jnp.pad(taps_part, ((0, 0), (0, depth - columns)))
    sums = jnp.concatenate(
        [d_small[:1], d_gain_two[None], mine[:, None] * d_small[1][None], taps_part], axis=0
    )
    sum_steps = steps_of("ctx", False) + steps_of("shard", False)

    d_one = gather_rows(d_one, tp_steps[-1:])
    d_w = dg(h1, d_proj[:, :4 * width], 0, 0).astype(BF)
    d_one, mlp, d_w, sums = lax.optimization_barrier((d_one, mlp, d_w, sums))

    d_one = gather_rows(d_one, tp_steps[:-1]).astype(BF).reshape(ranks, small, depth)
    d_w = sum_shard(d_w.reshape(shards, ranks * share, 4 * width)).astype(BF)
    mlp = gather_rows(mlp, tp_steps[:-1])
    mlp = from_plane(gather_rows(mlp, plane_steps[:-len(tp_steps)]))
    result = middle + mlp
    mask = my_rows(valid_mask).astype(F32)
    mask = mask[:, None]
    branches = [x_own, attn, mlp, result]
    totals = [jnp.sum(mask * b * b, axis=0, keepdims=True) for b in branches]
    totals += [jnp.broadcast_to(jnp.sum(mask, axis=0, keepdims=True), (1, depth))]
    sums = jnp.concatenate(totals + [sums], axis=0)
    d_one, d_w, result, sums = lax.optimization_barrier((d_one, d_w, result, sums))

    def sum_ctx(parts):
        total = lax.dynamic_index_in_dim(parts, rank, axis=0, keepdims=False).astype(F32)
        for k in range(1, ranks):
            sent = lax.dynamic_index_in_dim(parts, (rank + k) % ranks, axis=0, keepdims=False)
            got = lax.ppermute(sent, "ctx", [(i, (i + k) % ranks) for i in range(ranks)])
            total = total + got.astype(F32)
        return total

    total = sum_ctx(d_one)
    sums = sum_over(sums, sum_steps[:2])
    downs, pairs = by_shard(down_sum), by_shard(pair_sum)
    d_one, result, sums, d_w, d_wout, downs, pairs = lax.optimization_barrier(
        (total, result, sums, d_w, d_wout, downs, pairs)
    )

    d_w = d_w.reshape(ranks, share, 4 * width)
    w_blocks = [lax.dynamic_index_in_dim(d_w, rank, axis=0, keepdims=False)]
    for k in range(1, ranks):
        sent = lax.dynamic_index_in_dim(d_w, (rank + k) % ranks, axis=0, keepdims=False)
        pairs_k = [(i, (i + k) % ranks) for i in range(heads)]
        w_blocks.append(lax.ppermute(sent, "ctx", pairs_k))
    d_wout = sum_ctx(d_wout.reshape(ranks, share, columns))
    d_wgate, d_wup, d_wdown = unpack_hidden(order_s[None], downs, pairs)
    inv_one = lax.rsqrt(jnp.mean(x_own * x_own, axis=1, keepdims=True) + EPS)
    d_input = d_middle + norm_back(x_own, inv_one, gain_one, d_one)
    both = jnp.concatenate([d_input.astype(BF), result.astype(BF)], axis=1)
    both = spread_rows(both, tp_steps).reshape(lanes, small, 2 * depth)
    both = jnp.take(both, natural, axis=0).reshape(span, 2 * depth)
    d_tokens, output = both[:, :depth], both[:, depth:]
    sums = sum_over(sums, sum_steps[2:])
    every = sum_over(sums[:7], tp_steps)
    totals, one_sum, two_sum = jnp.sum(every[:4], axis=1), every[5] / gain_one, every[6]
    beta_sum, taps_sum = sums[7:7 + heads], sums[7 + heads:]
    d_beta = lax.dynamic_slice_in_dim(beta_sum, (shard * ranks + rank) * share, share, axis=1).T
    d_conv = taps_sum[:, :columns]
    *d_w, d_wout = unpack_heads(((rank - turn) % ranks)[None], w_blocks, d_wout, heads)
    rms_stats = jnp.sqrt(totals / (jnp.maximum(every[4, 0], 1.0) * depth))
    return (
        output, d_tokens, one_sum, d_w[0], d_w[1], d_w[2], d_w[3], d_beta, d_conv,
        d_wout, two_sum, d_wgate, d_wup, d_wdown, rms_stats,
    )


def solution(mesh):
    rows = P(("shard", "ctx"), None)
    tiled = P(("shard", "ctx"), "tp")
    turned = P("tp", ("shard", "ctx"))
    placed = (
        rows, rows, P(("shard", "ctx")), P("shard", None), P("shard", None), P(),
        tiled, tiled, tiled, tiled, tiled, P(None, "tp"), turned, P(), tiled, tiled, turned,
    )
    return jax.shard_map(
        local,
        mesh=mesh,
        in_specs=placed,
        out_specs=(
            rows, rows, P(), tiled, tiled, tiled, tiled, tiled, P(None, "tp"),
            turned, P(), tiled, tiled, turned, P(),
        ),
        check_vma=False,
    )
```

```python
import functools

import jax
import jax.numpy as jnp
from jax import lax
from jax.experimental import pallas as pl
from jax.experimental.pallas import tpu as pltpu
from jax.sharding import PartitionSpec as P

EPS = 1e-06
NEG = -1e30
BF = jnp.bfloat16
F32 = jnp.float32
CHUNK = 128


def dg(left, right, cl, cr):
    return lax.dot_general(left, right, (((cl,), (cr,)), ((), ())), preferred_element_type=F32)


def halves(value):
    high = value.astype(BF)
    return high, (value - high.astype(F32)).astype(BF)


def joined(pairs, cl=1, cr=0):
    lefts, rights = [], []
    for left, right in pairs:
        if left.dtype == BF and right.dtype == BF:
            lefts += [left]
            rights += [right]
        elif left.dtype == BF:
            lefts += [left, left]
            rights += halves(right)
        elif right.dtype == BF:
            lefts += halves(left)
            rights += [right, right]
        else:
            lh, ll = halves(left)
            rh, rl = halves(right)
            lefts += [lh, lh, ll]
            rights += [rh, rl, rh]
    return dg(jnp.concatenate(lefts, axis=cl), jnp.concatenate(rights, axis=cr), cl, cr)


def mm(left, right, cl=1, cr=0):
    return joined([(left, right)], cl, cr)


def ml(left, right, cl=1, cr=0):
    return dg(left.astype(BF), right.astype(BF), cl, cr)


def seg_at(position, ends):
    seg = (position >= ends[0]).astype(jnp.int32)
    for end in ends[1:]:
        seg = seg + (position >= end).astype(jnp.int32)
    return seg


def seq_ends(len_ref):
    ends = [len_ref[0, 0]]
    for index in range(1, len_ref.shape[1] - 1):
        ends.append(ends[-1] + len_ref[0, index])
    return ends


def shifted_mask(rows, width, shift, ends):
    here = lax.broadcasted_iota(jnp.int32, (rows, width), 0)
    back = here - shift
    return (back >= 0) & (seg_at(here, ends) == seg_at(back, ends))


def tile_iota():
    row = lax.broadcasted_iota(jnp.int32, (CHUNK, CHUNK), 0)
    col = lax.broadcasted_iota(jnp.int32, (CHUNK, CHUNK), 1)
    return row, col


def forward_kernel(x_count, w_count, *refs):
    deal_ref, spot_ref, slot_ref, len_ref = refs[:4]
    here_ref, refs = refs[4], refs[5:]
    x_refs, refs = refs[:x_count], refs[x_count:]
    gain_ref, refs = refs[0], refs[1:]
    w_refs, refs = refs[:w_count], refs[w_count:]
    taps_ref, o_ref, refs = refs[0], refs[1], refs[2:]
    kept, refs = refs[:SAVED], refs[SAVED:]
    held, (proj_ref, score_ref, sems) = refs[:SAVED], refs[SAVED:]
    (
        w_ref, wb_ref, h1_ref, q_ref, k_ref, v_ref, house_ref, raw_ref, logit_ref, prob_ref,
        u_ref, kt_ref, tr_ref, tinv_ref, xq_ref, yk_ref, z_ref,
    ) = held
    depth = here_ref.shape[1]
    pieces = deal_ref.shape[1]
    small = h1_ref.shape[0] // spot_ref.shape[1]
    rows = h1_ref.shape[0]
    piece = rows // pieces
    chunks = rows // CHUNK
    width = o_ref.shape[1]
    share = depth // w_count
    scale = width ** (-0.5)
    ends = seq_ends(len_ref)
    gain = gain_ref[...].astype(F32)

    def keep(first, last):
        for index in range(first, last):
            pltpu.make_async_copy(held[index], kept[index], sems.at[index]).start()

    pick = jnp.where(
        (lax.broadcasted_iota(jnp.int32, (16, width), 0) == 0)
        & (lax.broadcasted_iota(jnp.int32, (16, width), 1) == 0),
        1.0,
        0.0,
    ).astype(BF)
    for index, ref in enumerate(w_refs):
        base = pl.multiple_of(slot_ref[0, index] * share, share)
        w_ref[pl.ds(base, share), :] = ref[:share, :]
        wb_ref[pl.ds(base, share), :] = dg(ref[share:, :share], pick, 0, 0).astype(BF)

    def settle(x, index):
        x = x.astype(F32)
        inv = lax.rsqrt(jnp.mean(x * x, axis=1, keepdims=True) + EPS)
        base = pl.multiple_of(spot_ref[0, index] * small, small)
        h1_ref[pl.ds(base, small), :] = (x * inv * gain).astype(BF)

    local_count = here_ref.shape[0] // small
    for index in range(local_count):
        settle(here_ref[index * small:(index + 1) * small, :], index)
    for ref in x_refs:
        for index in range(ref.shape[0] // small):
            settle(ref[index * small:(index + 1) * small, :], local_count + index)
        local_count += ref.shape[0] // small
    keep(0, 3)

    def project(step, carry):
        base = pl.multiple_of(step * piece, piece)
        h1 = h1_ref[pl.ds(base, piece), :]
        proj_ref[pl.ds(base, piece), :] = dg(h1, w_ref[...], 1, 0)
        logit_ref[pl.ds(base, piece), :] = dg(h1, wb_ref[...], 1, 0)
        return carry

    lax.fori_loop(0, pieces, project, 0)
    q_ref[...] = proj_ref[:, :width].astype(BF)
    k_ref[...] = proj_ref[:, width:2 * width].astype(BF)
    v_ref[...] = proj_ref[:, 2 * width:3 * width].astype(BF)
    raw = proj_ref[:, 3 * width:4 * width]
    raw_ref[...] = raw
    taps = taps_ref[...].astype(F32)
    mixed = taps[0:1, :] * raw
    for shift in range(1, taps.shape[0]):
        moved = pltpu.roll(raw, shift, 0)
        mixed = mixed + taps[shift:shift + 1, :] * jnp.where(
            shifted_mask(rows, width, shift, ends), moved, 0.0
        )
    unit = mixed * lax.rsqrt(jnp.sum(mixed * mixed, axis=1, keepdims=True) + EPS)
    house_ref[...] = unit.astype(BF)
    keep(3, 9)

    row, col = tile_iota()
    strict = row > col
    eye = jnp.where(row == col, 1.0, 0.0)
    spans = [slice(n * CHUNK, (n + 1) * CHUNK) for n in range(chunks)]
    strength = [2.0 * jax.nn.sigmoid(logit_ref[s, 0:1]) for s in spans]
    system = []
    for n, s in enumerate(spans):
        house = house_ref[s, :]
        system.append(jnp.where(strict, strength[n] * dg(house, house, 1, 1), 0.0))
    inverse = [eye - jnp.where((row ^ col) == 1, a, 0.0) for a in system]
    level = 1
    while (1 << level) < CHUNK:
        block = ((row ^ col) >> level) == 1
        inner = [mm(jnp.where(block, a, 0.0), t) for a, t in zip(system, inverse)]
        inverse = [t - mm(t, i) for t, i in zip(inverse, inner)]
        level += 1
    for n, s in enumerate(spans):
        query, key, house = q_ref[s, :], k_ref[s, :], house_ref[s, :]
        tinv = inverse[n]
        tinv_ref[s, :] = tinv
        across = jnp.transpose(jnp.broadcast_to(strength[n], (CHUNK, CHUNK)))
        merged = tinv * across
        a_qw = jnp.where(row >= col, dg(query, house, 1, 1), 0.0)
        a_wk = jnp.where(strict, dg(house, key, 1, 1), 0.0)
        xq = mm(a_qw, merged)
        yk = mm(merged, a_wk)
        zz = mm(merged, house)
        xq_ref[s, :] = xq
        yk_ref[s, :] = yk
        z_ref[s, :] = zz
        score_ref[s, s] = (dg(query, key, 1, 1) - mm(xq, a_wk)) * scale
        proj_ref[s, :width] = query.astype(F32) - mm(xq, house)
        kt_ref[s, :] = key.astype(F32) - mm(yk, house, 0, 0)
        tr_ref[s, :] = eye - mm(house, zz, 0, 0)
    keep(11, SAVED)
    offset = 0
    for n in range(chunks - 2, -1, -1):
        later = slice((n + 1) * CHUNK, rows)
        count = rows - (n + 1) * CHUNK
        carried = proj_ref[later, :width]
        u_ref[offset:offset + count, :] = carried
        offset += count
        score_ref[later, spans[n]] = mm(carried, kt_ref[spans[n], :], 1, 1) * scale
        if n > 0:
            proj_ref[later, :width] = mm(carried, tr_ref[spans[n], :])
    keep(10, 11)
    for m, s in enumerate(spans):
        reach = (m + 1) * CHUNK
        at_row = lax.broadcasted_iota(jnp.int32, (CHUNK, reach), 0) + m * CHUNK
        at_col = lax.broadcasted_iota(jnp.int32, (CHUNK, reach), 1)
        seen = (at_row >= at_col) & (seg_at(at_row, ends) == seg_at(at_col, ends))
        logits = jnp.where(seen, score_ref[s, :reach], NEG)
        top = jnp.max(logits, axis=1, keepdims=True)
        grown = jnp.exp(logits - top)
        prob = grown / jnp.sum(grown, axis=1, keepdims=True)
        prob_ref[s, :reach] = prob
        proj_ref[s, :width] = dg(prob.astype(BF), v_ref[:reach, :], 1, 0)

    def give(step, carry):
        base = pl.multiple_of(step * piece, piece)
        given = pl.multiple_of(deal_ref[0, step] * piece, piece)
        o_ref[pl.ds(given, piece), :] = proj_ref[pl.ds(base, piece), :width].astype(BF)
        return carry

    keep(9, 10)
    lax.fori_loop(0, pieces, give, 0)
    for index in range(SAVED):
        pltpu.make_async_copy(held[index], kept[index], sems.at[index]).wait()


def backward_kernel(*refs):
    deal_ref, place_ref, source_ref, len_ref, live_ref, do_ref, taps_ref = refs[:7]
    kept, refs = refs[7:7 + SAVED], refs[7 + SAVED:]
    (near_ref, far_ref, dproj_ref, small_ref, dtaps_ref), refs = refs[:5], refs[5:]
    held, refs = refs[:SAVED], refs[SAVED:]
    ds_ref, dout_ref, du_ref, dkt_ref, dtr_ref, dhouse_ref, sems = refs
    (
        w_ref, wb_ref, h1_ref, q_ref, k_ref, v_ref, house_ref, raw_ref, logit_ref, prob_ref,
        u_ref, kt_ref, tr_ref, tinv_ref, xq_ref, yk_ref, z_ref,
    ) = held

    def fetch(index):
        return pltpu.make_async_copy(kept[index], held[index], sems.at[index])

    needed = (5, 9), (10, 11, 12), (3, 4, 6, 8, 13, 14, 15, 16), (7,), (0, 1, 2)
    for index in sum(needed, ()):
        fetch(index).start()

    def ready(stage):
        for index in needed[stage]:
            fetch(index).wait()

    rows = do_ref.shape[0]
    pieces = deal_ref.shape[1]
    piece = rows // pieces
    small = rows // place_ref.shape[1]
    chunks = rows // CHUNK
    width = do_ref.shape[1]
    scale = width ** (-0.5)
    ends = seq_ends(len_ref)
    spans = [slice(n * CHUNK, (n + 1) * CHUNK) for n in range(chunks)]
    row, col = tile_iota()
    strict = row > col

    def take(step, carry):
        base = pl.multiple_of(step * piece, piece)
        for part in range(piece // small):
            there = source_ref[0, deal_ref[0, step] * (piece // small) + part]
            dout_ref[pl.ds(base + part * small, small), :] = do_ref[
                pl.ds(pl.multiple_of(there * small, small), small), :
            ]
        return carry

    lax.fori_loop(0, pieces, take, 0)
    ready(0)
    for m, s in enumerate(spans):
        reach = (m + 1) * CHUNK
        prob = prob_ref[s, :reach]
        dprob = dg(dout_ref[s, :], v_ref[:reach, :], 1, 1)
        dot = jnp.sum(prob * dprob, axis=1, keepdims=True)
        ds_ref[s, :reach] = prob * (dprob - dot) * scale
    for n, s in enumerate(spans):
        dproj_ref[s, 2 * width:3 * width] = dg(
            prob_ref[n * CHUNK:, s].astype(BF), dout_ref[n * CHUNK:, :], 0, 0
        ).astype(BF)
    starts = {}
    offset = 0
    for n in range(chunks - 2, -1, -1):
        starts[n] = offset
        offset += rows - (n + 1) * CHUNK
    ready(1)
    for n in range(chunks - 1):
        later = slice((n + 1) * CHUNK, rows)
        count = rows - (n + 1) * CHUNK
        grad = ds_ref[later, spans[n]]
        carried = u_ref[starts[n]:starts[n] + count, :]
        dkt_ref[spans[n], :] = mm(grad, carried, 0, 0)
        fresh = mm(grad, kt_ref[spans[n], :])
        if n > 0:
            before = du_ref[later, :]
            dtr_ref[spans[n], :] = mm(carried, before, 0, 0)
            fresh = fresh + mm(before, tr_ref[spans[n], :], 1, 1)
        du_ref[later, :] = fresh
    ready(2)
    for n, s in enumerate(spans):
        query, key, house = q_ref[s, :], k_ref[s, :], house_ref[s, :]
        strength = 2.0 * jax.nn.sigmoid(logit_ref[s, 0:1])
        tinv = tinv_ref[s, :]
        merged = tinv * jnp.transpose(jnp.broadcast_to(strength, (CHUNK, CHUNK)))
        a_qw = jnp.where(row >= col, dg(query, house, 1, 1), 0.0)
        a_wk = jnp.where(strict, dg(house, key, 1, 1), 0.0)
        gram = jnp.where(strict, dg(house, house, 1, 1), 0.0)
        xq, yk, zz = xq_ref[s, :], yk_ref[s, :], z_ref[s, :]
        di = ds_ref[s, s]
        first, final = n == 0, n == chunks - 1
        if first:
            dxq = mm(di, a_wk, 1, 1)
            da_qw = mm(di, yk, 1, 1)
        else:
            dqt = du_ref[s, :]
            dxq = joined([(di, a_wk), (dqt, house)], 1, 1)
            da_qw = joined([(di, yk), (dqt, zz)], 1, 1)
        da_qw = jnp.where(row >= col, da_qw, 0.0)
        dm = mm(a_qw, dxq, 0, 0)
        cross = [(xq, di)]
        if not final:
            dkt = dkt_ref[s, :]
            dyk = mm(house, dkt, 1, 1)
            cross.append((merged, dyk))
            outer = [(dyk, a_wk)]
            if not first:
                dtr = dtr_ref[s, :]
                wd = mm(house, dtr)
                outer.append((wd, house))
            dm = dm + joined(outer, 1, 1)
        da_wk = jnp.where(strict, joined(cross, 0, 0), 0.0)
        ee = mm(tinv, dm, 0, 0)
        rest = jnp.where(row == col, 1.0, 0.0) - mm(gram, merged)
        dstrength = -jnp.sum(ee * rest, axis=1, keepdims=True)
        dgram = jnp.where(strict, mm(strength * ee, merged, 1, 1), 0.0)
        dq = joined([(di, key), (-da_qw, house)])
        dk = joined([(di, query), (-da_wk, house)], 0, 0)
        tall = [(da_qw, query), (-dgram, house)]
        wide = [(da_wk, key), (-dgram, house)]
        if not first:
            dq = dq + dqt
            tall.append((xq, dqt))
        if not final:
            dk = dk + dkt
            wide.append((yk, dkt))
            if not first:
                tall.append((merged, wd))
        dw = joined(tall, 0, 0) + joined(wide)
        if not first and not final:
            dw = dw + mm(zz, dtr, 1, 1)
        dw = -dw
        dproj_ref[s, :width] = dq.astype(BF)
        dproj_ref[s, width:2 * width] = dk.astype(BF)
        dhouse_ref[s, :] = dw
        gate = 0.5 * strength
        dlogit = dstrength * 2.0 * gate * (1.0 - gate)
        lane = lax.broadcasted_iota(jnp.int32, (CHUNK, width), 1)
        dproj_ref[s, 4 * width:] = jnp.where(lane == 0, dlogit, 0.0).astype(BF)
    ready(3)
    raw = raw_ref[...]
    taps = taps_ref[...].astype(F32)
    count = taps.shape[0]
    mixed = taps[0:1, :] * raw
    earlier = [raw]
    masks = [None]
    for shift in range(1, count):
        masks.append(shifted_mask(rows, width, shift, ends))
        earlier.append(jnp.where(masks[shift], pltpu.roll(raw, shift, 0), 0.0))
        mixed = mixed + taps[shift:shift + 1, :] * earlier[shift]
    inv = lax.rsqrt(jnp.sum(mixed * mixed, axis=1, keepdims=True) + EPS)
    dunit = dhouse_ref[...]
    dmixed = inv * dunit - mixed * (
        inv * inv * inv * jnp.sum(dunit * mixed, axis=1, keepdims=True)
    )
    live = live_ref[0, 0].astype(F32)
    draw = taps[0:1, :] * dmixed
    dtaps_ref[0:1, :] = jnp.sum(dmixed * raw, axis=0, keepdims=True) * live
    for shift in range(1, count):
        dtaps_ref[shift:shift + 1, :] = (
            jnp.sum(dmixed * earlier[shift], axis=0, keepdims=True) * live
        )
        later = jnp.where(masks[shift], dmixed, 0.0)
        draw = draw + taps[shift:shift + 1, :] * pltpu.roll(later, rows - shift, 0)
    dproj_ref[:, 3 * width:4 * width] = draw.astype(BF)

    ready(4)

    def send(step, total):
        base = pl.multiple_of(step * piece, piece)
        grads = dproj_ref[pl.ds(base, piece), :]
        dh1 = dg(grads[:, :4 * width], w_ref[...], 1, 1) + dg(grads[:, 4 * width:], wb_ref[...], 1, 1)
        dh1 = dh1 * live
        h1 = h1_ref[pl.ds(base, piece), :].astype(F32)
        total = total + jnp.sum(dh1 * h1, axis=0, keepdims=True)
        count = near_ref.shape[0] // small
        for part in range(piece // small):
            there = place_ref[0, deal_ref[0, step] * (piece // small) + part]
            block = dh1[part * small:(part + 1) * small]

            @pl.when(there < count)
            def _():
                near_ref[pl.ds(pl.multiple_of(there * small, small), small), :] = block

            @pl.when(there >= count)
            def _():
                at = pl.multiple_of((there - count) * small, small)
                far_ref[pl.ds(at, small), :] = block.astype(BF)

        return total

    small_ref[...] = jnp.zeros_like(small_ref)
    small_ref[0:1, :] = lax.fori_loop(0, pieces, send, jnp.zeros((1, h1_ref.shape[1]), F32))
    beta = dg(dproj_ref[:, 4 * width:], h1_ref[...], 0, 0)
    small_ref[1:2, :] = beta[0:1, :] * live


SAVED = 17


def saved_shapes(rows, depth, width):
    chunks = rows // CHUNK
    carried = CHUNK * chunks * (chunks - 1) // 2
    slim = ((rows, width), BF)
    tall = ((rows, width), F32)
    return (
        ((depth, 4 * width), BF), ((depth, width), BF), ((rows, depth), BF), slim, slim, slim, slim,
        tall, tall, ((rows, rows), F32), ((carried, width), F32), tall, tall, tall, tall, tall, tall,
    )


VMEM = pl.BlockSpec(memory_space=pltpu.VMEM)
SMEM = pl.BlockSpec(memory_space=pltpu.SMEM)
AWAY = pl.BlockSpec(memory_space=pl.ANY)
LIMIT = pltpu.CompilerParams(vmem_limit_bytes=56 * 1024 * 1024)


def attend_forward(deal, spot, slot, lengths, here, x_parts, gain, w_parts, taps):
    depth = here.shape[1]
    rows = here.shape[0] + sum(part_.shape[0] for part_ in x_parts)
    width = taps.shape[1]
    saved = saved_shapes(rows, depth, width)
    return pl.pallas_call(
        functools.partial(forward_kernel, len(x_parts), len(w_parts)),
        out_shape=(jax.ShapeDtypeStruct((rows, width), BF),)
        + tuple(jax.ShapeDtypeStruct(*entry) for entry in saved),
        in_specs=[SMEM] * 4 + [VMEM] * (len(x_parts) + len(w_parts) + 3),
        out_specs=(VMEM,) + (AWAY,) * SAVED,
        scratch_shapes=[pltpu.VMEM(*entry) for entry in saved]
        + [
            pltpu.VMEM((rows, 4 * width), F32),
            pltpu.VMEM((rows, rows), F32),
            pltpu.SemaphoreType.DMA((SAVED,)),
        ],
        compiler_params=LIMIT,
        cost_estimate=pl.CostEstimate(flops=16 * 10**9, bytes_accessed=10**7, transcendentals=0),
        name="attend_forward",
    )(deal, spot, slot, lengths, here, *x_parts, gain, *w_parts, taps)


def attend_backward(deal, place, source, lengths, live, d_out, taps, depth, kept):
    rows, width = d_out.shape
    saved = saved_shapes(rows, depth, width)
    return pl.pallas_call(
        backward_kernel,
        out_shape=(
            jax.ShapeDtypeStruct((rows // 2, depth), F32),
            jax.ShapeDtypeStruct((rows // 2, depth), BF),
            jax.ShapeDtypeStruct((rows, 5 * width), BF),
            jax.ShapeDtypeStruct((8, depth), F32),
            jax.ShapeDtypeStruct((taps.shape[0], width), F32),
        ),
        in_specs=[SMEM] * 5 + [VMEM] * 2 + [AWAY] * SAVED,
        out_specs=(VMEM,) * 5,
        scratch_shapes=[pltpu.VMEM(*entry) for entry in saved]
        + [
            pltpu.VMEM((rows, rows), F32),
            pltpu.VMEM((rows, width), BF),
            pltpu.VMEM((rows, width), F32),
            pltpu.VMEM((rows, width), F32),
            pltpu.VMEM((rows, width), F32),
            pltpu.VMEM((rows, width), F32),
            pltpu.SemaphoreType.DMA((SAVED,)),
        ],
        compiler_params=LIMIT,
        cost_estimate=pl.CostEstimate(flops=20 * 10**9, bytes_accessed=10**7, transcendentals=0),
        name="attend_backward",
    )(deal, place, source, lengths, live, d_out, taps, *kept)


def head_kernel(left_ref, right_ref, out_ref):
    width = out_ref.shape[2]
    heads = right_ref.shape[1] // width
    for head in range(out_ref.shape[0]):
        if head < heads:
            out_ref[head] = dg(
                left_ref[...], right_ref[:, head * width:(head + 1) * width], 1, 0
            ).astype(BF)
        else:
            out_ref[head] = jnp.zeros(out_ref.shape[1:], BF)


def by_head(left, right, width, ranks):
    return pl.pallas_call(
        head_kernel,
        out_shape=jax.ShapeDtypeStruct((ranks, left.shape[0], width), BF),
        in_specs=[VMEM, VMEM],
        out_specs=VMEM,
        compiler_params=LIMIT,
        cost_estimate=pl.CostEstimate(flops=3 * 10**9, bytes_accessed=10**6, transcendentals=0),
        name="by_head",
    )(left, right)


def pack_kernel(heads, ranks, shards, *refs):
    head_ref, order_ref = refs[:2]
    projections = refs[2:6]
    beta_ref, gate_ref, up_ref, down_ref = refs[6:10]
    blocks, parts = refs[10:10 + ranks], refs[10 + ranks:]
    share, columns = projections[0].shape
    width = columns // heads
    part = gate_ref.shape[1] // shards
    beta = beta_ref[...].astype(F32)
    for k, block in enumerate(blocks):
        head = head_ref[0, k]
        at = pl.multiple_of(head * width, width)
        for index, ref in enumerate(projections):
            block[:share, index * width:(index + 1) * width] = ref[:, pl.ds(at, width)]
        row = beta[0:1, :]
        for other in range(1, heads):
            row = jnp.where(head == other, beta[other:other + 1, :], row)
        block[share:, :] = jnp.zeros((block.shape[0] - share, block.shape[1]), BF)
        block[share:, :share] = jnp.broadcast_to(row, (block.shape[0] - share, share)).astype(BF)
    for index, ref in enumerate(parts):
        at = pl.multiple_of(order_ref[0, index] * part, part)
        ref[:, :part] = gate_ref[:, pl.ds(at, part)]
        ref[:, part:2 * part] = up_ref[:, pl.ds(at, part)]
        ref[:, 2 * part:] = down_ref[:, pl.ds(at, part)]


def pack(head, order, projections, w_beta, w_gate, w_up, w_down, ranks):
    share, columns = projections[0].shape
    heads = w_beta.shape[0]
    shards = order.shape[1]
    width = columns // heads
    part = w_gate.shape[1] // shards
    out = pl.pallas_call(
        functools.partial(pack_kernel, heads, ranks, shards),
        out_shape=(jax.ShapeDtypeStruct((share + 16, 4 * width), BF),) * ranks
        + (jax.ShapeDtypeStruct((share, 3 * part), BF),) * shards,
        in_specs=[SMEM, SMEM] + [VMEM] * 8,
        out_specs=(VMEM,) * (ranks + shards),
        compiler_params=LIMIT,
        cost_estimate=pl.CostEstimate(flops=3 * 10**9, bytes_accessed=10**6, transcendentals=0),
        name="pack",
    )(head, order, *projections, w_beta, w_gate, w_up, w_down)
    return list(out[:ranks]), list(out[ranks:])


def unpack_hidden_kernel(shards, *refs):
    order_ref, blocks = refs[0], refs[1:1 + shards]
    gate_ref, up_ref, down_ref = refs[1 + shards:]
    part = blocks[0].shape[1] // 3
    for index, block in enumerate(blocks):
        at = pl.multiple_of(order_ref[0, index] * part, part)
        gate_ref[:, pl.ds(at, part)] = block[:, :part].astype(F32)
        up_ref[:, pl.ds(at, part)] = block[:, part:2 * part].astype(F32)
        down_ref[:, pl.ds(at, part)] = block[:, 2 * part:].astype(F32)


def unpack_hidden(order, blocks):
    shards = len(blocks)
    share, part = blocks[0].shape[0], blocks[0].shape[1] // 3
    wide = jax.ShapeDtypeStruct((share, shards * part), F32)
    return pl.pallas_call(
        functools.partial(unpack_hidden_kernel, shards),
        out_shape=(wide,) * 3,
        in_specs=[SMEM] + [VMEM] * shards,
        out_specs=(VMEM,) * 3,
        compiler_params=LIMIT,
        cost_estimate=pl.CostEstimate(flops=2 * 10**9, bytes_accessed=10**6, transcendentals=0),
        name="unpack_hidden",
    )(order, *blocks)


def merge_kernel(order_ref, o_ref, w_ref, rows_ref, near_ref, far_ref):
    span, columns = rows_ref.shape
    width = o_ref.shape[2]
    small = span // order_ref.shape[1]
    for slot in range(order_ref.shape[1]):
        at = pl.multiple_of(order_ref[0, slot] * small, small)
        for head in range(columns // width):
            rows_ref[slot * small:(slot + 1) * small, head * width:(head + 1) * width] = o_ref[
                head, pl.ds(at, small), :
            ]
    total = dg(rows_ref[...], w_ref[...], 1, 1)
    near_ref[...] = total[:span // 2]
    far_ref[...] = total[span // 2:].astype(BF)


def merge_heads(order, head_rows, w_out, heads):
    span, width = head_rows.shape[1:]
    depth = w_out.shape[0]
    return pl.pallas_call(
        merge_kernel,
        out_shape=(
            jax.ShapeDtypeStruct((span, heads * width), BF),
            jax.ShapeDtypeStruct((span // 2, depth), F32),
            jax.ShapeDtypeStruct((span // 2, depth), BF),
        ),
        in_specs=[SMEM, VMEM, VMEM],
        out_specs=(VMEM,) * 3,
        compiler_params=LIMIT,
        cost_estimate=pl.CostEstimate(flops=3 * 10**9, bytes_accessed=10**6, transcendentals=0),
        name="merge_heads",
    )(order, head_rows, w_out)


def hidden_kernel(
    near_ref, far_ref, grad_ref, w_ref, h2_ref, act_ref, pair_ref,
    d_near_ref, d_far_ref, m_near_ref, m_far_ref,
):
    half = near_ref.shape[0]
    part = act_ref.shape[1]
    tile = min(part, 256)
    h2_ref[:half, :] = near_ref[...]
    h2_ref[half:, :] = far_ref[...]
    for start in range(0, part, tile):
        gate = dg(h2_ref[...], w_ref[:, start:start + tile], 1, 0)
        up = dg(h2_ref[...], w_ref[:, part + start:part + start + tile], 1, 0)
        d_act = dg(grad_ref[...], w_ref[:, 2 * part + start:2 * part + start + tile], 1, 0)
        sig = jax.nn.sigmoid(gate)
        swish = gate * sig
        act_ref[:, start:start + tile] = (swish * up).astype(BF)
        pair_ref[:, start:start + tile] = (
            d_act * up * sig * (1.0 + gate * (1.0 - sig))
        ).astype(BF)
        pair_ref[:, part + start:part + start + tile] = (d_act * swish).astype(BF)
    d_far_ref[...] = dg(pair_ref[half:, :], w_ref[:, :2 * part], 1, 1).astype(BF)
    d_near_ref[...] = dg(pair_ref[:half, :], w_ref[:, :2 * part], 1, 1)
    m_far_ref[...] = dg(act_ref[half:, :], w_ref[:, 2 * part:], 1, 1).astype(BF)
    m_near_ref[...] = dg(act_ref[:half, :], w_ref[:, 2 * part:], 1, 1)


def hidden_pass(near, far, grad, weights):
    half, depth = near.shape
    part = weights.shape[1] // 3
    keep = jax.ShapeDtypeStruct((half, depth), F32)
    sent = jax.ShapeDtypeStruct((half, depth), BF)
    return pl.pallas_call(
        hidden_kernel,
        out_shape=(
            jax.ShapeDtypeStruct((2 * half, depth), BF),
            jax.ShapeDtypeStruct((2 * half, part), BF),
            jax.ShapeDtypeStruct((2 * half, 2 * part), BF),
            keep, sent, keep, sent,
        ),
        in_specs=[VMEM] * 4,
        out_specs=(VMEM,) * 7,
        compiler_params=LIMIT,
        cost_estimate=pl.CostEstimate(flops=9 * 10**9, bytes_accessed=10**6, transcendentals=0),
        name="hidden_pass",
    )(near, far, grad, weights)


def hidden_grad_kernel(h2_ref, grad_ref, act_ref, pair_ref, out_ref):
    part = act_ref.shape[1]
    tile = 256

    def one(step, carry):
        at = pl.multiple_of(step * tile, tile)
        out_ref[pl.ds(at, tile), :2 * part] = dg(
            h2_ref[:, pl.ds(at, tile)], pair_ref[...], 0, 0
        ).astype(BF)
        out_ref[pl.ds(at, tile), 2 * part:] = dg(
            grad_ref[:, pl.ds(at, tile)], act_ref[...], 0, 0
        ).astype(BF)
        return carry

    lax.fori_loop(0, h2_ref.shape[1] // tile, one, 0)


def hidden_grad(h2, grad, act, pair):
    depth, part = h2.shape[1], act.shape[1]
    return pl.pallas_call(
        hidden_grad_kernel,
        out_shape=jax.ShapeDtypeStruct((depth, 3 * part), BF),
        in_specs=[VMEM] * 4,
        out_specs=VMEM,
        compiler_params=LIMIT,
        cost_estimate=pl.CostEstimate(flops=8 * 10**9, bytes_accessed=10**6, transcendentals=0),
        name="hidden_grad",
    )(h2, grad, act, pair)


def unpack_heads_kernel(ranks, heads, *refs):
    source_ref, blocks, grads = refs[0], refs[1:1 + ranks], refs[1 + ranks:]
    width = blocks[0].shape[1] // len(grads)
    for k, block in enumerate(blocks):
        source = source_ref[0, k]

        @pl.when(source < heads)
        def _():
            at = pl.multiple_of(source * width, width)
            for index, ref in enumerate(grads):
                ref[:, pl.ds(at, width)] = block[:, index * width:(index + 1) * width].astype(F32)


def unpack_heads(source, blocks, heads):
    ranks = len(blocks)
    share, columns = blocks[0].shape[0], blocks[0].shape[1] // 4 * heads
    return pl.pallas_call(
        functools.partial(unpack_heads_kernel, ranks, heads),
        out_shape=(jax.ShapeDtypeStruct((share, columns), F32),) * 4,
        in_specs=[SMEM] + [VMEM] * ranks,
        out_specs=(VMEM,) * 4,
        compiler_params=LIMIT,
        cost_estimate=pl.CostEstimate(flops=2 * 10**9, bytes_accessed=10**6, transcendentals=0),
        name="unpack_heads",
    )(source, *blocks)


def steps_of(axis, descending):
    size = lax.axis_size(axis)
    bits = []
    bit = 1
    while bit < size:
        bits.append((axis, bit))
        bit *= 2
    return bits[::-1] if descending else bits


def swap(value, axis, bit):
    size = lax.axis_size(axis)
    return lax.ppermute(value, axis, [(i, i ^ bit) for i in range(size)])


def spread_rows(value, steps):
    for axis, bit in steps:
        value = jnp.concatenate([value, swap(value, axis, bit)], axis=0)
    return value


def gather_rows(value, steps):
    for axis, bit in steps[::-1]:
        half = value.shape[0] // 2
        value = value[:half] + swap(value[half:].astype(BF), axis, bit).astype(F32)
    return value


def in_order(mine, other):
    first = lax.axis_index("shard") == 0
    return jnp.stack([jnp.where(first, mine, other), jnp.where(first, other, mine)])


def over_shard(value):
    if lax.axis_size("shard") == 2:
        return in_order(value, swap(value, "shard", 1))
    return lax.all_gather(value, "shard", axis=0, tiled=False)


def across_shard(parts):
    if lax.axis_size("shard") == 2:
        shard = lax.axis_index("shard")
        mine = lax.dynamic_index_in_dim(parts, shard, axis=0, keepdims=False)
        sent = lax.dynamic_index_in_dim(parts, 1 - shard, axis=0, keepdims=False)
        return in_order(mine, swap(sent, "shard", 1))
    return deal_out(parts, "shard")


def sum_shard(parts):
    if lax.axis_size("shard") == 2:
        shard = lax.axis_index("shard")
        mine = lax.dynamic_index_in_dim(parts, shard, axis=0, keepdims=False)
        sent = lax.dynamic_index_in_dim(parts, 1 - shard, axis=0, keepdims=False)
        return mine.astype(F32) + swap(sent, "shard", 1).astype(F32)
    return jnp.sum(deal_out(parts, "shard").astype(F32), axis=0)


def over_ctx(value):
    ranks = lax.axis_size("ctx")
    got = [value] + [
        lax.ppermute(value, "ctx", [(i, (i + k) % ranks) for i in range(ranks)])
        for k in range(1, ranks)
    ]
    return got


def sum_over(value, steps):
    for axis, bit in steps:
        value = value + swap(value, axis, bit)
    return value


def deal_out(value, axis):
    return lax.all_to_all(value, axis, split_axis=0, concat_axis=0, tiled=True)


def norm_back(value, inverse, gain, grad):
    scaled = grad * gain
    return inverse * scaled - value * inverse**3 * jnp.mean(scaled * value, axis=1, keepdims=True)


def local(
    tokens, cotangent, valid_mask, lengths, deal, attn_gain,
    w_query, w_key, w_value, w_house, w_beta, conv_taps, w_out,
    mlp_gain, w_gate, w_up, w_down,
):
    shards, ranks, lanes = (lax.axis_size(a) for a in ("shard", "ctx", "tp"))
    shard, rank, lane = (lax.axis_index(a) for a in ("shard", "ctx", "tp"))
    span, depth = tokens.shape
    share, columns = w_query.shape
    heads = w_beta.shape[1]
    width = columns // heads
    piece = span // 2
    group = ranks * span
    small = span // lanes
    part = w_gate.shape[1] // shards
    spare = ranks - heads
    tp_steps = steps_of("tp", True)
    plane_steps = steps_of("shard", False) + tp_steps
    live = (rank < heads).astype(jnp.int32).reshape(1, 1)
    head_at = jnp.minimum(rank, heads - 1)

    shifted = over_ctx(lax.dynamic_slice_in_dim(tokens, lane * small, small, axis=0))[1:]

    turn = jnp.arange(ranks, dtype=jnp.int32)
    order_s = jnp.arange(shards, dtype=jnp.int32)
    if shards == 2:
        order_s = order_s ^ shard
    blocks, hidden = pack(
        jnp.minimum((rank + turn) % ranks, heads - 1)[None], order_s[None],
        (w_query, w_key, w_value, w_house), w_beta.T, w_gate, w_up, w_down.T, ranks,
    )
    crossed = [blocks[0]]
    for k in range(1, ranks):
        pairs = [(i, (i + k) % ranks) for i in range(ranks) if (i + k) % ranks < heads]
        crossed.append(lax.ppermute(blocks[k], "ctx", pairs))
    slots_of = []
    taps = lax.dynamic_slice_in_dim(conv_taps, head_at * width, width, axis=1)

    x_parts, apart_of = list(shifted), [0]
    x_parts = [jnp.concatenate(shifted, axis=0)]
    for axis, bit in tp_steps:
        joined_parts = jnp.concatenate(x_parts, axis=0) if len(x_parts) > 1 else x_parts[0]
        x_parts = x_parts + [swap(joined_parts, axis, bit)]
        apart_of = apart_of + [other ^ bit for other in apart_of]
    owners = (rank - jnp.arange(1, ranks, dtype=jnp.int32)) % ranks
    blocks_of = [rank * lanes + jnp.arange(lanes, dtype=jnp.int32)]
    blocks_of += [owners * lanes + (lane ^ apart) for apart in apart_of]
    blocks_of = jnp.concatenate(blocks_of)
    labels = jnp.arange(2 * ranks, dtype=jnp.int32)
    per_piece = lanes // 2
    at_piece = jnp.sum(
        jnp.where(deal[0][None, :] == (blocks_of // per_piece)[:, None], labels[None, :], 0), axis=1
    )
    spot = (at_piece * per_piece + blocks_of % per_piece)[None]
    w_parts = []
    for k, block in enumerate(crossed):
        source = (rank - k) % ranks
        if shards == 2:
            w_parts += [block, swap(block, "shard", 1)]
            slots_of += [shard * ranks + source, (1 - shard) * ranks + source]
        else:
            every = lax.all_gather(block, "shard", axis=0, tiled=False)
            w_parts += [every[i] for i in range(shards)]
            slots_of += [i * ranks + source for i in range(shards)]
    slot = jnp.stack(slots_of)[None]

    wo_t = over_shard(w_out.T).reshape(shards * share, columns)
    wo_t = lax.all_gather(wo_t, "ctx", axis=0, tiled=False)
    wo_t = wo_t.reshape(ranks, shards, share, columns).transpose(1, 0, 2, 3).reshape(depth, columns)
    if shards == 2:
        hidden = [hidden[0], swap(hidden[1], "shard", 1)]
    else:
        hidden = list(deal_out(jnp.stack(hidden), "shard"))
    def to_plane(value):
        value = value.reshape(-1, shards, ranks, share).transpose(0, 2, 1, 3)
        return value.reshape(-1, depth)

    def from_plane(value):
        value = value.reshape(-1, ranks, shards, share).transpose(0, 2, 1, 3)
        return value.reshape(-1, depth)

    def my_rows(value):
        return lax.dynamic_slice_in_dim(value, lane * small, small, axis=0)

    grad_own = my_rows(cotangent)
    grad_plane = spread_rows(to_plane(grad_own), plane_steps)
    hidden, _, _ = lax.optimization_barrier((hidden, shifted, crossed))
    hidden = in_order(*hidden) if shards == 2 else jnp.stack(hidden)
    hidden = hidden.reshape(shards * share, 3 * part)
    hidden = lax.all_gather(hidden, "ctx", axis=0, tiled=True)
    fwd = attend_forward(deal, spot, slot, lengths, tokens, x_parts, attn_gain[None], w_parts, taps)
    head_out, saved = fwd[0], fwd[1:]
    h1 = saved[2]
    slots = jnp.arange(lanes, dtype=jnp.int32)
    order = jnp.full_like(slots, lane)
    for index, (_, bit) in enumerate(tp_steps):
        order = order ^ jnp.where((slots >> index) % 2 == 1, bit, 0)
    natural = jnp.zeros_like(slots)
    for index, (_, bit) in enumerate(tp_steps):
        natural = natural + jnp.where(((slots ^ lane) & bit) != 0, 1 << index, 0)
    head_out, grad_plane = lax.optimization_barrier((head_out, grad_plane))
    o_all = deal_out(head_out.reshape(ranks, span, width), "ctx")
    o_rows, near, far = merge_heads(order[None], o_all, wo_t, heads)
    attn = gather_rows(near + swap(far, *tp_steps[-1]).astype(F32), tp_steps[:-1])
    x_own = my_rows(tokens).astype(F32)
    middle = x_own + attn
    gain_two = mlp_gain.astype(F32)
    inv_two = lax.rsqrt(jnp.mean(middle * middle, axis=1, keepdims=True) + EPS)
    normed = (middle * inv_two * gain_two).astype(BF)
    near = spread_rows(to_plane(normed), plane_steps[:-1])
    far = swap(near, *tp_steps[-1])

    h2, act, pair, near, far, mlp, m_far = hidden_pass(near, far, grad_plane, hidden)
    d_two = near + swap(far, *tp_steps[-1]).astype(F32)
    d_two, act, pair = lax.optimization_barrier((d_two, act, pair))
    mlp = mlp + swap(m_far, *tp_steps[-1]).astype(F32)
    middle_steps = plane_steps[len(plane_steps) - len(tp_steps):-1]
    shard_steps = plane_steps[:-len(tp_steps)]
    d_two = gather_rows(d_two, middle_steps)
    hidden_sum = hidden_grad(h2, grad_plane, act, pair)
    d_two, hidden_sum, mlp = lax.optimization_barrier((d_two, hidden_sum, mlp))
    hidden_sum = lax.psum_scatter(hidden_sum, "ctx", scatter_dimension=0, tiled=True)
    d_two = from_plane(gather_rows(d_two, shard_steps))

    def by_shard(grad):
        grad = grad.reshape(shards, share, grad.shape[1])
        if shards == 2:
            mine = lax.dynamic_index_in_dim(grad, shard, axis=0, keepdims=False)
            sent = lax.dynamic_index_in_dim(grad, 1 - shard, axis=0, keepdims=False)
            return [mine, swap(sent, "shard", 1)]
        return list(deal_out(grad, "shard"))

    d_gain_two = jnp.sum(d_two * middle * inv_two, axis=0)
    d_middle = grad_own.astype(F32) + norm_back(middle, inv_two, gain_two, d_two)
    d_attn = spread_rows(d_middle.astype(BF), tp_steps[:-1])
    d_attn = spread_rows(d_attn, tp_steps[-1:])
    d_heads = by_head(d_attn, wo_t, width, ranks)
    d_heads, d_attn, mlp = lax.optimization_barrier((d_heads, d_attn, mlp))
    d_heads = deal_out(d_heads, "ctx")
    d_wout = dg(d_attn, o_rows, 0, 0).astype(BF)
    d_wout = sum_shard(d_wout.reshape(shards, ranks * share, columns)).astype(BF)
    mlp = gather_rows(mlp, middle_steps)
    d_heads, d_wout, mlp = lax.optimization_barrier((d_heads, d_wout, mlp))

    given = jnp.arange(group // small, dtype=jnp.int32)
    apart = (given % lanes) ^ lane
    turned = jnp.zeros_like(apart)
    for index, (_, bit) in enumerate(tp_steps):
        turned = turned + jnp.where((apart & bit) != 0, 1 << index, 0)
    place = (turned * ranks + given // lanes)[None]
    source = (given // lanes * lanes + turned)[None]
    near, far, d_proj, d_small, d_taps = attend_backward(
        deal, place, source, lengths, live, d_heads.reshape(group, width), taps, depth, saved
    )
    gain_one = attn_gain.astype(F32)
    mine = (jnp.arange(heads) == rank).astype(F32)
    taps_part = (mine[None, :, None] * d_taps[:, None]).reshape(conv_taps.shape)
    taps_part = jnp.pad(taps_part, ((0, 0), (0, depth - columns)))
    sum_steps = steps_of("ctx", False) + steps_of("shard", False)

    d_one = near + swap(far, *tp_steps[-1]).astype(F32)
    d_one, d_proj, mlp, d_wout = lax.optimization_barrier((d_one, d_proj, mlp, d_wout))

    d_one = gather_rows(d_one, tp_steps[:-1]).astype(BF).reshape(ranks, small, depth)
    d_w = dg(h1, d_proj[:, :4 * width], 0, 0).astype(BF)
    d_w = sum_shard(d_w.reshape(shards, ranks * share, 4 * width)).astype(BF)
    mlp = from_plane(gather_rows(mlp, shard_steps))
    result = middle + mlp
    mask = my_rows(valid_mask).astype(F32)[:, None]
    branches = [x_own, attn, mlp, result]
    sums = [jnp.sum(mask * b * b, axis=0, keepdims=True) for b in branches]
    sums += [jnp.broadcast_to(jnp.sum(mask, axis=0, keepdims=True), (1, depth))]
    sums += [d_small[:1], d_gain_two[None], mine[:, None] * d_small[1][None], taps_part]
    sums = jnp.concatenate(sums, axis=0)
    def sum_ctx(parts):
        total = lax.dynamic_index_in_dim(parts, rank, axis=0, keepdims=False).astype(F32)
        for k in range(1, ranks):
            sent = lax.dynamic_index_in_dim(parts, (rank + k) % ranks, axis=0, keepdims=False)
            got = lax.ppermute(sent, "ctx", [(i, (i + k) % ranks) for i in range(ranks)])
            total = total + got.astype(F32)
        return total

    d_wout = sum_ctx(d_wout.reshape(ranks, share, columns)).T
    d_one, sums, result, d_wout = lax.optimization_barrier((d_one, sums, result, d_wout))
    total = sum_ctx(d_one)
    sums = sum_over(sums, sum_steps[:1])
    hidden_parts = by_shard(hidden_sum)
    d_one, result, sums, d_w, hidden_parts = lax.optimization_barrier(
        (total, result, sums, d_w, hidden_parts)
    )
    sums = sum_over(sums, sum_steps[1:])
    every = sum_over(sums[:7], tp_steps)

    d_w = d_w.reshape(ranks, share, 4 * width)
    w_blocks = [lax.dynamic_index_in_dim(d_w, rank, axis=0, keepdims=False)]
    for k in range(1, ranks):
        sent = lax.dynamic_index_in_dim(d_w, (rank + k) % ranks, axis=0, keepdims=False)
        pairs_k = [(i, (i + k) % ranks) for i in range(heads)]
        w_blocks.append(lax.ppermute(sent, "ctx", pairs_k))
    d_wgate, d_wup, d_wdown = unpack_hidden(order_s[None], hidden_parts)
    d_wdown = d_wdown.T
    inv_one = lax.rsqrt(jnp.mean(x_own * x_own, axis=1, keepdims=True) + EPS)
    d_input = d_middle + norm_back(x_own, inv_one, gain_one, d_one)
    both = jnp.concatenate([d_input.astype(BF), result.astype(BF)], axis=1)
    both = spread_rows(both, tp_steps).reshape(lanes, small, 2 * depth)
    both = jnp.take(both, natural, axis=0).reshape(span, 2 * depth)
    d_tokens, output = both[:, :depth], both[:, depth:]
    totals, one_sum, two_sum = jnp.sum(every[:4], axis=1), every[5] / gain_one, every[6]
    beta_sum, taps_sum = sums[7:7 + heads], sums[7 + heads:]
    d_beta = lax.dynamic_slice_in_dim(beta_sum, (shard * ranks + rank) * share, share, axis=1).T
    d_conv = taps_sum[:, :columns]
    d_w = unpack_heads(((rank - turn) % ranks)[None], w_blocks, heads)
    rms_stats = jnp.sqrt(totals / (jnp.maximum(every[4, 0], 1.0) * depth))
    return (
        output, d_tokens, one_sum, d_w[0], d_w[1], d_w[2], d_w[3], d_beta, d_conv,
        d_wout, two_sum, d_wgate, d_wup, d_wdown, rms_stats,
    )


def solution(mesh):
    rows = P(("shard", "ctx"), None)
    tiled = P(("shard", "ctx"), "tp")
    turned = P("tp", ("shard", "ctx"))
    placed = (
        rows, rows, P(("shard", "ctx")), P("shard", None), P("shard", None), P(),
        tiled, tiled, tiled, tiled, tiled, P(None, "tp"), turned, P(), tiled, tiled, turned,
    )
    return jax.shard_map(
        local,
        mesh=mesh,
        in_specs=placed,
        out_specs=(
            rows, rows, P(), tiled, tiled, tiled, tiled, tiled, P(None, "tp"),
            turned, P(), tiled, tiled, turned, P(),
        ),
        check_vma=False,
    )
```

```python
import functools

import jax
import jax.numpy as jnp
from jax import lax
from jax.experimental import pallas as pl
from jax.experimental.pallas import tpu as pltpu
from jax.sharding import PartitionSpec as P

EPS = 1e-06
NEG = -1e30
BF = jnp.bfloat16
F32 = jnp.float32
CHUNK = 128


def dg(left, right, cl, cr):
    return lax.dot_general(left, right, (((cl,), (cr,)), ((), ())), preferred_element_type=F32)


def halves(value):
    high = value.astype(BF)
    return high, (value - high.astype(F32)).astype(BF)


def joined(pairs, cl=1, cr=0):
    lefts, rights = [], []
    for left, right in pairs:
        if left.dtype == BF and right.dtype == BF:
            lefts += [left]
            rights += [right]
        elif left.dtype == BF:
            lefts += [left, left]
            rights += halves(right)
        elif right.dtype == BF:
            lefts += halves(left)
            rights += [right, right]
        else:
            lh, ll = halves(left)
            rh, rl = halves(right)
            lefts += [lh, lh, ll]
            rights += [rh, rl, rh]
    return dg(jnp.concatenate(lefts, axis=cl), jnp.concatenate(rights, axis=cr), cl, cr)


def mm(left, right, cl=1, cr=0):
    return joined([(left, right)], cl, cr)


def ml(left, right, cl=1, cr=0):
    return dg(left.astype(BF), right.astype(BF), cl, cr)


def seg_at(position, ends):
    seg = (position >= ends[0]).astype(jnp.int32)
    for end in ends[1:]:
        seg = seg + (position >= end).astype(jnp.int32)
    return seg


def seq_ends(len_ref):
    ends = [len_ref[0, 0]]
    for index in range(1, len_ref.shape[1] - 1):
        ends.append(ends[-1] + len_ref[0, index])
    return ends


def shifted_mask(rows, width, shift, ends):
    here = lax.broadcasted_iota(jnp.int32, (rows, width), 0)
    back = here - shift
    return (back >= 0) & (seg_at(here, ends) == seg_at(back, ends))


def tile_iota():
    row = lax.broadcasted_iota(jnp.int32, (CHUNK, CHUNK), 0)
    col = lax.broadcasted_iota(jnp.int32, (CHUNK, CHUNK), 1)
    return row, col


def forward_kernel(x_count, w_count, *refs):
    deal_ref, spot_ref, slot_ref, len_ref = refs[:4]
    here_ref, refs = refs[4], refs[5:]
    x_refs, refs = refs[:x_count], refs[x_count:]
    gain_ref, refs = refs[0], refs[1:]
    w_refs, refs = refs[:w_count], refs[w_count:]
    taps_ref, o_ref, refs = refs[0], refs[1], refs[2:]
    kept, refs = refs[:SAVED], refs[SAVED:]
    held, (proj_ref, score_ref, sems) = refs[:SAVED], refs[SAVED:]
    (
        w_ref, wb_ref, h1_ref, q_ref, k_ref, v_ref, house_ref, raw_ref, logit_ref, prob_ref,
        u_ref, kt_ref, tr_ref, tinv_ref, xq_ref, yk_ref, z_ref,
    ) = held
    depth = here_ref.shape[1]
    pieces = deal_ref.shape[1]
    small = h1_ref.shape[0] // spot_ref.shape[1]
    rows = h1_ref.shape[0]
    piece = rows // pieces
    chunks = rows // CHUNK
    width = o_ref.shape[1]
    share = depth // w_count
    scale = width ** (-0.5)
    ends = seq_ends(len_ref)
    gain = gain_ref[...].astype(F32)

    def keep(first, last):
        for index in range(first, last):
            pltpu.make_async_copy(held[index], kept[index], sems.at[index]).start()

    pick = jnp.where(
        (lax.broadcasted_iota(jnp.int32, (16, width), 0) == 0)
        & (lax.broadcasted_iota(jnp.int32, (16, width), 1) == 0),
        1.0,
        0.0,
    ).astype(BF)
    for index, ref in enumerate(w_refs):
        base = pl.multiple_of(slot_ref[0, index] * share, share)
        w_ref[pl.ds(base, share), :] = ref[:share, :]
        wb_ref[pl.ds(base, share), :] = dg(ref[share:, :share], pick, 0, 0).astype(BF)

    def settle(x, index):
        x = x.astype(F32)
        inv = lax.rsqrt(jnp.mean(x * x, axis=1, keepdims=True) + EPS)
        base = pl.multiple_of(spot_ref[0, index] * small, small)
        h1_ref[pl.ds(base, small), :] = (x * inv * gain).astype(BF)

    local_count = here_ref.shape[0] // small
    for index in range(local_count):
        settle(here_ref[index * small:(index + 1) * small, :], index)
    for ref in x_refs:
        for index in range(ref.shape[0] // small):
            settle(ref[index * small:(index + 1) * small, :], local_count + index)
        local_count += ref.shape[0] // small
    keep(0, 3)

    for step in range(4):
        at = slice(step * width, (step + 1) * width)
        proj_ref[:, at] = dg(h1_ref[...], w_ref[:, at], 1, 0)
    logit_ref[...] = dg(h1_ref[...], wb_ref[...], 1, 0)
    q_ref[...] = proj_ref[:, :width].astype(BF)
    k_ref[...] = proj_ref[:, width:2 * width].astype(BF)
    v_ref[...] = proj_ref[:, 2 * width:3 * width].astype(BF)
    raw = proj_ref[:, 3 * width:4 * width]
    raw_ref[...] = raw
    taps = taps_ref[...].astype(F32)
    mixed = taps[0:1, :] * raw
    for shift in range(1, taps.shape[0]):
        moved = pltpu.roll(raw, shift, 0)
        mixed = mixed + taps[shift:shift + 1, :] * jnp.where(
            shifted_mask(rows, width, shift, ends), moved, 0.0
        )
    unit = mixed * lax.rsqrt(jnp.sum(mixed * mixed, axis=1, keepdims=True) + EPS)
    house_ref[...] = unit.astype(BF)
    keep(3, 9)

    row, col = tile_iota()
    strict = row > col
    eye = jnp.where(row == col, 1.0, 0.0)
    spans = [slice(n * CHUNK, (n + 1) * CHUNK) for n in range(chunks)]
    strength = [2.0 * jax.nn.sigmoid(logit_ref[s, 0:1]) for s in spans]
    system = []
    for n, s in enumerate(spans):
        house = house_ref[s, :]
        system.append(jnp.where(strict, strength[n] * dg(house, house, 1, 1), 0.0))
    inverse = [eye - jnp.where((row ^ col) == 1, a, 0.0) for a in system]
    level = 1
    while (1 << level) < CHUNK:
        block = ((row ^ col) >> level) == 1
        inner = [mm(jnp.where(block, a, 0.0), t) for a, t in zip(system, inverse)]
        inverse = [t - mm(t, i) for t, i in zip(inverse, inner)]
        level += 1
    for n, s in enumerate(spans):
        query, key, house = q_ref[s, :], k_ref[s, :], house_ref[s, :]
        tinv = inverse[n]
        tinv_ref[s, :] = tinv
        across = jnp.transpose(jnp.broadcast_to(strength[n], (CHUNK, CHUNK)))
        merged = tinv * across
        a_qw = jnp.where(row >= col, dg(query, house, 1, 1), 0.0)
        a_wk = jnp.where(strict, dg(house, key, 1, 1), 0.0)
        xq = mm(a_qw, merged)
        yk = mm(merged, a_wk)
        zz = mm(merged, house)
        xq_ref[s, :] = xq
        yk_ref[s, :] = yk
        z_ref[s, :] = zz
        score_ref[s, s] = (dg(query, key, 1, 1) - mm(xq, a_wk)) * scale
        proj_ref[s, :width] = query.astype(F32) - mm(xq, house)
        kt_ref[s, :] = key.astype(F32) - mm(yk, house, 0, 0)
        tr_ref[s, :] = eye - mm(house, zz, 0, 0)
    keep(11, SAVED)
    offset = 0
    for n in range(chunks - 2, -1, -1):
        later = slice((n + 1) * CHUNK, rows)
        count = rows - (n + 1) * CHUNK
        carried = proj_ref[later, :width]
        u_ref[offset:offset + count, :] = carried
        offset += count
        score_ref[later, spans[n]] = mm(carried, kt_ref[spans[n], :], 1, 1) * scale
        if n > 0:
            proj_ref[later, :width] = mm(carried, tr_ref[spans[n], :])
    keep(10, 11)
    for m, s in enumerate(spans):
        reach = (m + 1) * CHUNK
        at_row = lax.broadcasted_iota(jnp.int32, (CHUNK, reach), 0) + m * CHUNK
        at_col = lax.broadcasted_iota(jnp.int32, (CHUNK, reach), 1)
        seen = (at_row >= at_col) & (seg_at(at_row, ends) == seg_at(at_col, ends))
        logits = jnp.where(seen, score_ref[s, :reach], NEG)
        top = jnp.max(logits, axis=1, keepdims=True)
        grown = jnp.exp(logits - top)
        prob = grown / jnp.sum(grown, axis=1, keepdims=True)
        prob_ref[s, :reach] = prob
        proj_ref[s, :width] = dg(prob.astype(BF), v_ref[:reach, :], 1, 0)

    def give(step, carry):
        base = pl.multiple_of(step * piece, piece)
        given = pl.multiple_of(deal_ref[0, step] * piece, piece)
        o_ref[pl.ds(given, piece), :] = proj_ref[pl.ds(base, piece), :width].astype(BF)
        return carry

    keep(9, 10)
    lax.fori_loop(0, pieces, give, 0)
    for index in range(SAVED):
        pltpu.make_async_copy(held[index], kept[index], sems.at[index]).wait()


def backward_kernel(*refs):
    deal_ref, place_ref, source_ref, from_ref, len_ref, live_ref = refs[:6]
    ranks = from_ref.shape[1]
    parts, taps_ref, refs = refs[6:6 + ranks], refs[6 + ranks], refs[7 + ranks:]
    kept, refs = refs[:SAVED], refs[SAVED:]
    (near_ref, far_ref, dproj_ref, small_ref, dtaps_ref), refs = refs[:5], refs[5:]
    held, refs = refs[:SAVED], refs[SAVED:]
    ds_ref, dout_ref, du_ref, dkt_ref, dtr_ref, dhouse_ref, do_ref, sems = refs
    (
        w_ref, wb_ref, h1_ref, q_ref, k_ref, v_ref, house_ref, raw_ref, logit_ref, prob_ref,
        u_ref, kt_ref, tr_ref, tinv_ref, xq_ref, yk_ref, z_ref,
    ) = held

    def fetch(index):
        return pltpu.make_async_copy(kept[index], held[index], sems.at[index])

    needed = (5, 9), (10, 11, 12), (3, 4, 6, 8, 13, 14, 15, 16), (7,), (0, 1, 2)
    for index in sum(needed, ()):
        fetch(index).start()
    for k, ref in enumerate(parts):
        span = ref.shape[0]
        do_ref[pl.ds(pl.multiple_of(from_ref[0, k] * span, span), span), :] = ref[...]

    def ready(stage):
        for index in needed[stage]:
            fetch(index).wait()

    rows = do_ref.shape[0]
    pieces = deal_ref.shape[1]
    piece = rows // pieces
    small = rows // place_ref.shape[1]
    chunks = rows // CHUNK
    width = do_ref.shape[1]
    scale = width ** (-0.5)
    ends = seq_ends(len_ref)
    spans = [slice(n * CHUNK, (n + 1) * CHUNK) for n in range(chunks)]
    row, col = tile_iota()
    strict = row > col

    def take(step, carry):
        base = pl.multiple_of(step * piece, piece)
        for part in range(piece // small):
            there = source_ref[0, deal_ref[0, step] * (piece // small) + part]
            dout_ref[pl.ds(base + part * small, small), :] = do_ref[
                pl.ds(pl.multiple_of(there * small, small), small), :
            ]
        return carry

    lax.fori_loop(0, pieces, take, 0)
    ready(0)
    for m, s in enumerate(spans):
        reach = (m + 1) * CHUNK
        prob = prob_ref[s, :reach]
        dprob = dg(dout_ref[s, :], v_ref[:reach, :], 1, 1)
        dot = jnp.sum(prob * dprob, axis=1, keepdims=True)
        ds_ref[s, :reach] = prob * (dprob - dot) * scale
    for n, s in enumerate(spans):
        dproj_ref[s, 2 * width:3 * width] = dg(
            prob_ref[n * CHUNK:, s].astype(BF), dout_ref[n * CHUNK:, :], 0, 0
        ).astype(BF)
    starts = {}
    offset = 0
    for n in range(chunks - 2, -1, -1):
        starts[n] = offset
        offset += rows - (n + 1) * CHUNK
    ready(1)
    for n in range(chunks - 1):
        later = slice((n + 1) * CHUNK, rows)
        count = rows - (n + 1) * CHUNK
        grad = ds_ref[later, spans[n]]
        carried = u_ref[starts[n]:starts[n] + count, :]
        dkt_ref[spans[n], :] = mm(grad, carried, 0, 0)
        fresh = mm(grad, kt_ref[spans[n], :])
        if n > 0:
            before = du_ref[later, :]
            dtr_ref[spans[n], :] = mm(carried, before, 0, 0)
            fresh = fresh + mm(before, tr_ref[spans[n], :], 1, 1)
        du_ref[later, :] = fresh
    ready(2)
    for n, s in enumerate(spans):
        query, key, house = q_ref[s, :], k_ref[s, :], house_ref[s, :]
        strength = 2.0 * jax.nn.sigmoid(logit_ref[s, 0:1])
        tinv = tinv_ref[s, :]
        merged = tinv * jnp.transpose(jnp.broadcast_to(strength, (CHUNK, CHUNK)))
        a_qw = jnp.where(row >= col, dg(query, house, 1, 1), 0.0)
        a_wk = jnp.where(strict, dg(house, key, 1, 1), 0.0)
        gram = jnp.where(strict, dg(house, house, 1, 1), 0.0)
        xq, yk, zz = xq_ref[s, :], yk_ref[s, :], z_ref[s, :]
        di = ds_ref[s, s]
        first, final = n == 0, n == chunks - 1
        if first:
            dxq = mm(di, a_wk, 1, 1)
            da_qw = mm(di, yk, 1, 1)
        else:
            dqt = du_ref[s, :]
            dxq = joined([(di, a_wk), (dqt, house)], 1, 1)
            da_qw = joined([(di, yk), (dqt, zz)], 1, 1)
        da_qw = jnp.where(row >= col, da_qw, 0.0)
        dm = mm(a_qw, dxq, 0, 0)
        cross = [(xq, di)]
        if not final:
            dkt = dkt_ref[s, :]
            dyk = mm(house, dkt, 1, 1)
            cross.append((merged, dyk))
            outer = [(dyk, a_wk)]
            if not first:
                dtr = dtr_ref[s, :]
                wd = mm(house, dtr)
                outer.append((wd, house))
            dm = dm + joined(outer, 1, 1)
        da_wk = jnp.where(strict, joined(cross, 0, 0), 0.0)
        ee = mm(tinv, dm, 0, 0)
        rest = jnp.where(row == col, 1.0, 0.0) - mm(gram, merged)
        dstrength = -jnp.sum(ee * rest, axis=1, keepdims=True)
        dgram = jnp.where(strict, mm(strength * ee, merged, 1, 1), 0.0)
        dq = joined([(di, key), (-da_qw, house)])
        dk = joined([(di, query), (-da_wk, house)], 0, 0)
        tall = [(da_qw, query), (-dgram, house)]
        wide = [(da_wk, key), (-dgram, house)]
        if not first:
            dq = dq + dqt
            tall.append((xq, dqt))
        if not final:
            dk = dk + dkt
            wide.append((yk, dkt))
            if not first:
                tall.append((merged, wd))
        dw = joined(tall, 0, 0) + joined(wide)
        if not first and not final:
            dw = dw + mm(zz, dtr, 1, 1)
        dw = -dw
        dproj_ref[s, :width] = dq.astype(BF)
        dproj_ref[s, width:2 * width] = dk.astype(BF)
        dhouse_ref[s, :] = dw
        gate = 0.5 * strength
        dlogit = dstrength * 2.0 * gate * (1.0 - gate)
        lane = lax.broadcasted_iota(jnp.int32, (CHUNK, width), 1)
        dproj_ref[s, 4 * width:] = jnp.where(lane == 0, dlogit, 0.0).astype(BF)
    ready(3)
    raw = raw_ref[...]
    taps = taps_ref[...].astype(F32)
    count = taps.shape[0]
    mixed = taps[0:1, :] * raw
    earlier = [raw]
    masks = [None]
    for shift in range(1, count):
        masks.append(shifted_mask(rows, width, shift, ends))
        earlier.append(jnp.where(masks[shift], pltpu.roll(raw, shift, 0), 0.0))
        mixed = mixed + taps[shift:shift + 1, :] * earlier[shift]
    inv = lax.rsqrt(jnp.sum(mixed * mixed, axis=1, keepdims=True) + EPS)
    dunit = dhouse_ref[...]
    dmixed = inv * dunit - mixed * (
        inv * inv * inv * jnp.sum(dunit * mixed, axis=1, keepdims=True)
    )
    live = live_ref[0, 0].astype(F32)
    draw = taps[0:1, :] * dmixed
    dtaps_ref[0:1, :] = jnp.sum(dmixed * raw, axis=0, keepdims=True) * live
    for shift in range(1, count):
        dtaps_ref[shift:shift + 1, :] = (
            jnp.sum(dmixed * earlier[shift], axis=0, keepdims=True) * live
        )
        later = jnp.where(masks[shift], dmixed, 0.0)
        draw = draw + taps[shift:shift + 1, :] * pltpu.roll(later, rows - shift, 0)
    dproj_ref[:, 3 * width:4 * width] = draw.astype(BF)

    ready(4)

    small_ref[...] = jnp.zeros_like(small_ref)
    count = near_ref.shape[0] // small
    tile = 256

    def send(step, carry):
        at = pl.ds(pl.multiple_of(step * tile, tile), tile)
        dh1 = dg(dproj_ref[:, :4 * width], w_ref[at, :], 1, 1)
        dh1 = (dh1 + dg(dproj_ref[:, 4 * width:], wb_ref[at, :], 1, 1)) * live
        small_ref[0:1, at] = jnp.sum(dh1 * h1_ref[:, at].astype(F32), axis=0, keepdims=True)
        for block in range(rows // small):
            given = deal_ref[0, block * small // piece] * (piece // small)
            there = place_ref[0, given + block % (piece // small)]
            values = dh1[block * small:(block + 1) * small]

            @pl.when(there < count)
            def _():
                near_ref[pl.ds(pl.multiple_of(there * small, small), small), at] = values

            @pl.when(there >= count)
            def _():
                to = pl.ds(pl.multiple_of((there - count) * small, small), small)
                far_ref[to, at] = values.astype(BF)

        return carry

    lax.fori_loop(0, h1_ref.shape[1] // tile, send, 0)
    beta = dg(dproj_ref[:, 4 * width:], h1_ref[...], 0, 0)
    small_ref[1:2, :] = beta[0:1, :] * live


SAVED = 17


def saved_shapes(rows, depth, width):
    chunks = rows // CHUNK
    carried = CHUNK * chunks * (chunks - 1) // 2
    slim = ((rows, width), BF)
    tall = ((rows, width), F32)
    return (
        ((depth, 4 * width), BF), ((depth, width), BF), ((rows, depth), BF), slim, slim, slim, slim,
        tall, tall, ((rows, rows), F32), ((carried, width), F32), tall, tall, tall, tall, tall, tall,
    )


VMEM = pl.BlockSpec(memory_space=pltpu.VMEM)
SMEM = pl.BlockSpec(memory_space=pltpu.SMEM)
AWAY = pl.BlockSpec(memory_space=pl.ANY)
LIMIT = pltpu.CompilerParams(vmem_limit_bytes=56 * 1024 * 1024)


def attend_forward(deal, spot, slot, lengths, here, x_parts, gain, w_parts, taps):
    depth = here.shape[1]
    rows = here.shape[0] + sum(part_.shape[0] for part_ in x_parts)
    width = taps.shape[1]
    saved = saved_shapes(rows, depth, width)
    return pl.pallas_call(
        functools.partial(forward_kernel, len(x_parts), len(w_parts)),
        out_shape=(jax.ShapeDtypeStruct((rows, width), BF),)
        + tuple(jax.ShapeDtypeStruct(*entry) for entry in saved),
        in_specs=[SMEM] * 4 + [VMEM] * (len(x_parts) + len(w_parts) + 3),
        out_specs=(VMEM,) + (AWAY,) * SAVED,
        scratch_shapes=[pltpu.VMEM(*entry) for entry in saved]
        + [
            pltpu.VMEM((rows, 4 * width), F32),
            pltpu.VMEM((rows, rows), F32),
            pltpu.SemaphoreType.DMA((SAVED,)),
        ],
        compiler_params=LIMIT,
        cost_estimate=pl.CostEstimate(flops=16 * 10**9, bytes_accessed=10**7, transcendentals=0),
        name="attend_forward",
    )(deal, spot, slot, lengths, here, *x_parts, gain, *w_parts, taps)


def attend_backward(deal, place, source, origin, lengths, live, d_out, taps, depth, kept):
    rows, width = d_out[0].shape[0] * len(d_out), d_out[0].shape[1]
    saved = saved_shapes(rows, depth, width)
    return pl.pallas_call(
        backward_kernel,
        out_shape=(
            jax.ShapeDtypeStruct((rows // 2, depth), F32),
            jax.ShapeDtypeStruct((rows // 2, depth), BF),
            jax.ShapeDtypeStruct((rows, 5 * width), BF),
            jax.ShapeDtypeStruct((8, depth), F32),
            jax.ShapeDtypeStruct((taps.shape[0], width), F32),
        ),
        in_specs=[SMEM] * 6 + [VMEM] * (len(d_out) + 1) + [AWAY] * SAVED,
        out_specs=(VMEM,) * 5,
        scratch_shapes=[pltpu.VMEM(*entry) for entry in saved]
        + [
            pltpu.VMEM((rows, rows), F32),
            pltpu.VMEM((rows, width), BF),
            pltpu.VMEM((rows, width), F32),
            pltpu.VMEM((rows, width), F32),
            pltpu.VMEM((rows, width), F32),
            pltpu.VMEM((rows, width), F32),
            pltpu.VMEM((rows, width), BF),
            pltpu.SemaphoreType.DMA((SAVED,)),
        ],
        compiler_params=LIMIT,
        cost_estimate=pl.CostEstimate(flops=20 * 10**9, bytes_accessed=10**7, transcendentals=0),
        name="attend_backward",
    )(deal, place, source, origin, lengths, live, *d_out, taps, *kept)


def head_kernel(head_ref, left_ref, right_ref, *outs):
    width = outs[0].shape[1]
    every = dg(left_ref[...], right_ref[...], 1, 0).astype(BF)
    for k, out in enumerate(outs):
        for head in range(right_ref.shape[1] // width):

            @pl.when(head_ref[0, k] == head)
            def _():
                out[...] = every[:, head * width:(head + 1) * width]


def by_head(head, left, right, width):
    ranks = head.shape[1]
    return pl.pallas_call(
        head_kernel,
        out_shape=(jax.ShapeDtypeStruct((left.shape[0], width), BF),) * ranks,
        in_specs=[SMEM, VMEM, VMEM],
        out_specs=(VMEM,) * ranks,
        compiler_params=LIMIT,
        cost_estimate=pl.CostEstimate(flops=3 * 10**9, bytes_accessed=10**6, transcendentals=0),
        name="by_head",
    )(head, left, right)


def pack_kernel(heads, ranks, shards, *refs):
    head_ref, order_ref = refs[:2]
    projections = refs[2:6]
    beta_ref, gate_ref, up_ref, down_ref = refs[6:10]
    blocks, parts = refs[10:10 + ranks], refs[10 + ranks:]
    share, columns = projections[0].shape
    width = columns // heads
    part = gate_ref.shape[1] // shards
    beta = beta_ref[...].astype(F32)
    for k, block in enumerate(blocks):
        head = head_ref[0, k]
        at = pl.multiple_of(head * width, width)
        for index, ref in enumerate(projections):
            block[:share, index * width:(index + 1) * width] = ref[:, pl.ds(at, width)]
        row = beta[0:1, :]
        for other in range(1, heads):
            row = jnp.where(head == other, beta[other:other + 1, :], row)
        block[share:, :] = jnp.zeros((block.shape[0] - share, block.shape[1]), BF)
        block[share:, :share] = jnp.broadcast_to(row, (block.shape[0] - share, share)).astype(BF)
    for index, ref in enumerate(parts):
        at = pl.multiple_of(order_ref[0, index] * part, part)
        ref[:, :part] = gate_ref[:, pl.ds(at, part)]
        ref[:, part:2 * part] = up_ref[:, pl.ds(at, part)]
        ref[:, 2 * part:] = down_ref[:, pl.ds(at, part)]


def pack(head, order, projections, w_beta, w_gate, w_up, w_down, ranks):
    share, columns = projections[0].shape
    heads = w_beta.shape[0]
    shards = order.shape[1]
    width = columns // heads
    part = w_gate.shape[1] // shards
    out = pl.pallas_call(
        functools.partial(pack_kernel, heads, ranks, shards),
        out_shape=(jax.ShapeDtypeStruct((share + 16, 4 * width), BF),) * ranks
        + (jax.ShapeDtypeStruct((share, 3 * part), BF),) * shards,
        in_specs=[SMEM, SMEM] + [VMEM] * 8,
        out_specs=(VMEM,) * (ranks + shards),
        compiler_params=LIMIT,
        cost_estimate=pl.CostEstimate(flops=3 * 10**9, bytes_accessed=10**6, transcendentals=0),
        name="pack",
    )(head, order, *projections, w_beta, w_gate, w_up, w_down)
    return list(out[:ranks]), list(out[ranks:])


def unpack_hidden_kernel(shards, *refs):
    order_ref, blocks = refs[0], refs[1:1 + shards]
    gate_ref, up_ref, down_ref = refs[1 + shards:]
    part = blocks[0].shape[1] // 3
    for index, block in enumerate(blocks):
        at = pl.multiple_of(order_ref[0, index] * part, part)
        gate_ref[:, pl.ds(at, part)] = block[:, :part].astype(F32)
        up_ref[:, pl.ds(at, part)] = block[:, part:2 * part].astype(F32)
        down_ref[:, pl.ds(at, part)] = block[:, 2 * part:].astype(F32)


def unpack_hidden(order, blocks):
    shards = len(blocks)
    share, part = blocks[0].shape[0], blocks[0].shape[1] // 3
    wide = jax.ShapeDtypeStruct((share, shards * part), F32)
    return pl.pallas_call(
        functools.partial(unpack_hidden_kernel, shards),
        out_shape=(wide,) * 3,
        in_specs=[SMEM] + [VMEM] * shards,
        out_specs=(VMEM,) * 3,
        compiler_params=LIMIT,
        cost_estimate=pl.CostEstimate(flops=2 * 10**9, bytes_accessed=10**6, transcendentals=0),
        name="unpack_hidden",
    )(order, *blocks)


def merge_kernel(order_ref, o_ref, w_ref, rows_ref, near_ref, far_ref):
    span, columns = rows_ref.shape
    width = o_ref.shape[2]
    small = span // order_ref.shape[1]
    for slot in range(order_ref.shape[1]):
        at = pl.multiple_of(order_ref[0, slot] * small, small)
        for head in range(columns // width):
            rows_ref[slot * small:(slot + 1) * small, head * width:(head + 1) * width] = o_ref[
                head, pl.ds(at, small), :
            ]
    total = dg(rows_ref[...], w_ref[...], 1, 1)
    near_ref[...] = total[:span // 2]
    far_ref[...] = total[span // 2:].astype(BF)


def merge_heads(order, head_rows, w_out, heads):
    span, width = head_rows.shape[1:]
    depth = w_out.shape[0]
    return pl.pallas_call(
        merge_kernel,
        out_shape=(
            jax.ShapeDtypeStruct((span, heads * width), BF),
            jax.ShapeDtypeStruct((span // 2, depth), F32),
            jax.ShapeDtypeStruct((span // 2, depth), BF),
        ),
        in_specs=[SMEM, VMEM, VMEM],
        out_specs=(VMEM,) * 3,
        compiler_params=LIMIT,
        cost_estimate=pl.CostEstimate(flops=3 * 10**9, bytes_accessed=10**6, transcendentals=0),
        name="merge_heads",
    )(order, head_rows, w_out)


def hidden_kernel(
    near_ref, far_ref, grad_ref, w_ref, h2_ref, act_ref, pair_ref,
    d_near_ref, d_far_ref, m_near_ref, m_far_ref,
):
    half = near_ref.shape[0]
    part = act_ref.shape[1]
    tile = min(part, 256)
    h2_ref[:half, :] = near_ref[...]
    h2_ref[half:, :] = far_ref[...]
    for start in range(0, part, tile):
        gate = dg(h2_ref[...], w_ref[:, start:start + tile], 1, 0)
        up = dg(h2_ref[...], w_ref[:, part + start:part + start + tile], 1, 0)
        d_act = dg(grad_ref[...], w_ref[:, 2 * part + start:2 * part + start + tile], 1, 0)
        sig = jax.nn.sigmoid(gate)
        swish = gate * sig
        act_ref[:, start:start + tile] = (swish * up).astype(BF)
        pair_ref[:, start:start + tile] = (
            d_act * up * sig * (1.0 + gate * (1.0 - sig))
        ).astype(BF)
        pair_ref[:, part + start:part + start + tile] = (d_act * swish).astype(BF)
    d_far_ref[...] = dg(pair_ref[half:, :], w_ref[:, :2 * part], 1, 1).astype(BF)
    d_near_ref[...] = dg(pair_ref[:half, :], w_ref[:, :2 * part], 1, 1)
    m_far_ref[...] = dg(act_ref[half:, :], w_ref[:, 2 * part:], 1, 1).astype(BF)
    m_near_ref[...] = dg(act_ref[:half, :], w_ref[:, 2 * part:], 1, 1)


def hidden_pass(near, far, grad, weights):
    half, depth = near.shape
    part = weights.shape[1] // 3
    keep = jax.ShapeDtypeStruct((half, depth), F32)
    sent = jax.ShapeDtypeStruct((half, depth), BF)
    return pl.pallas_call(
        hidden_kernel,
        out_shape=(
            jax.ShapeDtypeStruct((2 * half, depth), BF),
            jax.ShapeDtypeStruct((2 * half, part), BF),
            jax.ShapeDtypeStruct((2 * half, 2 * part), BF),
            keep, sent, keep, sent,
        ),
        in_specs=[VMEM] * 4,
        out_specs=(VMEM,) * 7,
        compiler_params=LIMIT,
        cost_estimate=pl.CostEstimate(flops=9 * 10**9, bytes_accessed=10**6, transcendentals=0),
        name="hidden_pass",
    )(near, far, grad, weights)


def hidden_grad_kernel(h2_ref, grad_ref, act_ref, pair_ref, out_ref, turned_ref):
    depth, part = out_ref.shape[0], act_ref.shape[1]
    tile = min(part, 256)
    for source, value, start in ((h2_ref, pair_ref, 0), (grad_ref, act_ref, 2 * part)):
        for at in range(0, depth, 256):
            turned_ref[at:at + 256, :] = source[:, at:at + 256].astype(F32).T.astype(BF)
        for at in range(0, value.shape[1], tile):
            out_ref[:, start + at:start + at + tile] = dg(
                turned_ref[...], value[:, at:at + tile], 1, 0
            ).astype(BF)


def hidden_grad(h2, grad, act, pair):
    depth, part = h2.shape[1], act.shape[1]
    return pl.pallas_call(
        hidden_grad_kernel,
        out_shape=jax.ShapeDtypeStruct((depth, 3 * part), BF),
        in_specs=[VMEM] * 4,
        out_specs=VMEM,
        scratch_shapes=[pltpu.VMEM((depth, h2.shape[0]), BF)],
        compiler_params=LIMIT,
        cost_estimate=pl.CostEstimate(flops=8 * 10**9, bytes_accessed=10**6, transcendentals=0),
        name="hidden_grad",
    )(h2, grad, act, pair)


def unpack_heads_kernel(ranks, heads, *refs):
    source_ref, blocks, grads = refs[0], refs[1:1 + ranks], refs[1 + ranks:]
    width = blocks[0].shape[1] // len(grads)
    for k, block in enumerate(blocks):
        source = source_ref[0, k]

        @pl.when(source < heads)
        def _():
            at = pl.multiple_of(source * width, width)
            for index, ref in enumerate(grads):
                ref[:, pl.ds(at, width)] = block[:, index * width:(index + 1) * width].astype(F32)


def unpack_heads(source, blocks, heads):
    ranks = len(blocks)
    share, columns = blocks[0].shape[0], blocks[0].shape[1] // 4 * heads
    return pl.pallas_call(
        functools.partial(unpack_heads_kernel, ranks, heads),
        out_shape=(jax.ShapeDtypeStruct((share, columns), F32),) * 4,
        in_specs=[SMEM] + [VMEM] * ranks,
        out_specs=(VMEM,) * 4,
        compiler_params=LIMIT,
        cost_estimate=pl.CostEstimate(flops=2 * 10**9, bytes_accessed=10**6, transcendentals=0),
        name="unpack_heads",
    )(source, *blocks)


def steps_of(axis, descending):
    size = lax.axis_size(axis)
    bits = []
    bit = 1
    while bit < size:
        bits.append((axis, bit))
        bit *= 2
    return bits[::-1] if descending else bits


def swap(value, axis, bit):
    size = lax.axis_size(axis)
    return lax.ppermute(value, axis, [(i, i ^ bit) for i in range(size)])


def spread_rows(value, steps):
    for axis, bit in steps:
        value = jnp.concatenate([value, swap(value, axis, bit)], axis=0)
    return value


def gather_rows(value, steps):
    for axis, bit in steps[::-1]:
        half = value.shape[0] // 2
        value = value[:half] + swap(value[half:].astype(BF), axis, bit).astype(F32)
    return value


def fold(kept, got, steps):
    for axis, bit in steps[::-1]:
        half = kept.shape[0] // 2
        sent = (kept[half:] + got[half:].astype(F32)).astype(BF)
        kept, got = kept[:half] + got[:half].astype(F32), swap(sent, axis, bit)
    return kept + got.astype(F32)


def in_order(mine, other):
    first = lax.axis_index("shard") == 0
    return jnp.stack([jnp.where(first, mine, other), jnp.where(first, other, mine)])


def over_shard(value):
    if lax.axis_size("shard") == 2:
        return in_order(value, swap(value, "shard", 1))
    return lax.all_gather(value, "shard", axis=0, tiled=False)


def across_shard(parts):
    if lax.axis_size("shard") == 2:
        shard = lax.axis_index("shard")
        mine = lax.dynamic_index_in_dim(parts, shard, axis=0, keepdims=False)
        sent = lax.dynamic_index_in_dim(parts, 1 - shard, axis=0, keepdims=False)
        return in_order(mine, swap(sent, "shard", 1))
    return deal_out(parts, "shard")


def sum_shard(parts):
    if lax.axis_size("shard") == 2:
        shard = lax.axis_index("shard")
        mine = lax.dynamic_index_in_dim(parts, shard, axis=0, keepdims=False)
        sent = lax.dynamic_index_in_dim(parts, 1 - shard, axis=0, keepdims=False)
        return mine.astype(F32) + swap(sent, "shard", 1).astype(F32)
    return jnp.sum(deal_out(parts, "shard").astype(F32), axis=0)


def over_ctx(value):
    ranks = lax.axis_size("ctx")
    got = [value] + [
        lax.ppermute(value, "ctx", [(i, (i + k) % ranks) for i in range(ranks)])
        for k in range(1, ranks)
    ]
    return got


def sum_over(value, steps):
    for axis, bit in steps:
        value = value + swap(value, axis, bit)
    return value


def deal_out(value, axis):
    return lax.all_to_all(value, axis, split_axis=0, concat_axis=0, tiled=True)


def norm_back(value, inverse, gain, grad):
    scaled = grad * gain
    return inverse * scaled - value * inverse**3 * jnp.mean(scaled * value, axis=1, keepdims=True)


def local(
    tokens, cotangent, valid_mask, lengths, deal, attn_gain,
    w_query, w_key, w_value, w_house, w_beta, conv_taps, w_out,
    mlp_gain, w_gate, w_up, w_down,
):
    shards, ranks, lanes = (lax.axis_size(a) for a in ("shard", "ctx", "tp"))
    shard, rank, lane = (lax.axis_index(a) for a in ("shard", "ctx", "tp"))
    span, depth = tokens.shape
    share, columns = w_query.shape
    heads = w_beta.shape[1]
    width = columns // heads
    piece = span // 2
    group = ranks * span
    small = span // lanes
    part = w_gate.shape[1] // shards
    spare = ranks - heads
    tp_steps = steps_of("tp", True)
    plane_steps = steps_of("shard", False) + tp_steps
    live = (rank < heads).astype(jnp.int32).reshape(1, 1)
    head_at = jnp.minimum(rank, heads - 1)

    shifted = over_ctx(lax.dynamic_slice_in_dim(tokens, lane * small, small, axis=0))[1:]

    turn = jnp.arange(ranks, dtype=jnp.int32)
    order_s = jnp.arange(shards, dtype=jnp.int32)
    if shards == 2:
        order_s = order_s ^ shard
    head_of = jnp.minimum((rank + turn) % ranks, heads - 1)[None]
    blocks, hidden = pack(
        head_of, order_s[None],
        (w_query, w_key, w_value, w_house), w_beta.T, w_gate, w_up, w_down.T, ranks,
    )
    crossed = [blocks[0]]
    for k in range(1, ranks):
        pairs = [(i, (i + k) % ranks) for i in range(ranks) if (i + k) % ranks < heads]
        crossed.append(lax.ppermute(blocks[k], "ctx", pairs))
    slots_of = []
    taps = lax.dynamic_slice_in_dim(conv_taps, head_at * width, width, axis=1)

    x_parts, apart_of = list(shifted), [0]
    x_parts = [jnp.concatenate(shifted, axis=0)]
    for axis, bit in tp_steps:
        joined_parts = jnp.concatenate(x_parts, axis=0) if len(x_parts) > 1 else x_parts[0]
        x_parts = x_parts + [swap(joined_parts, axis, bit)]
        apart_of = apart_of + [other ^ bit for other in apart_of]
    owners = (rank - jnp.arange(1, ranks, dtype=jnp.int32)) % ranks
    blocks_of = [rank * lanes + jnp.arange(lanes, dtype=jnp.int32)]
    blocks_of += [owners * lanes + (lane ^ apart) for apart in apart_of]
    blocks_of = jnp.concatenate(blocks_of)
    labels = jnp.arange(2 * ranks, dtype=jnp.int32)
    per_piece = lanes // 2
    at_piece = jnp.sum(
        jnp.where(deal[0][None, :] == (blocks_of // per_piece)[:, None], labels[None, :], 0), axis=1
    )
    spot = (at_piece * per_piece + blocks_of % per_piece)[None]
    w_parts = []
    for k, block in enumerate(crossed):
        source = (rank - k) % ranks
        if shards == 2:
            w_parts += [block, swap(block, "shard", 1)]
            slots_of += [shard * ranks + source, (1 - shard) * ranks + source]
        else:
            every = lax.all_gather(block, "shard", axis=0, tiled=False)
            w_parts += [every[i] for i in range(shards)]
            slots_of += [i * ranks + source for i in range(shards)]
    slot = jnp.stack(slots_of)[None]

    wo_t = over_shard(w_out.T).reshape(shards * share, columns)
    wo_t = lax.all_gather(wo_t, "ctx", axis=0, tiled=False)
    wo_t = wo_t.reshape(ranks, shards, share, columns).transpose(1, 0, 2, 3).reshape(depth, columns)
    grad_own = lax.dynamic_slice_in_dim(cotangent, lane * small, small, axis=0)
    hidden, grad_start, _ = lax.optimization_barrier((hidden, grad_own, shifted))
    if shards == 2:
        hidden = [hidden[0], swap(hidden[1], "shard", 1)]
    else:
        hidden = list(deal_out(jnp.stack(hidden), "shard"))
    def to_plane(value):
        value = value.reshape(-1, shards, ranks, share).transpose(0, 2, 1, 3)
        return value.reshape(-1, depth)

    def from_plane(value):
        value = value.reshape(-1, ranks, shards, share).transpose(0, 2, 1, 3)
        return value.reshape(-1, depth)

    def my_rows(value):
        return lax.dynamic_slice_in_dim(value, lane * small, small, axis=0)

    grad_plane = spread_rows(to_plane(grad_start), plane_steps)
    hidden, _, _ = lax.optimization_barrier((hidden, shifted, crossed))
    hidden = in_order(*hidden) if shards == 2 else jnp.stack(hidden)
    hidden = hidden.reshape(shards * share, 3 * part)
    hidden = lax.all_gather(hidden, "ctx", axis=0, tiled=True)
    fwd = attend_forward(deal, spot, slot, lengths, tokens, x_parts, attn_gain[None], w_parts, taps)
    head_out, saved = fwd[0], fwd[1:]
    h1 = saved[2]
    slots = jnp.arange(lanes, dtype=jnp.int32)
    order = jnp.full_like(slots, lane)
    for index, (_, bit) in enumerate(tp_steps):
        order = order ^ jnp.where((slots >> index) % 2 == 1, bit, 0)
    natural = jnp.zeros_like(slots)
    for index, (_, bit) in enumerate(tp_steps):
        natural = natural + jnp.where(((slots ^ lane) & bit) != 0, 1 << index, 0)
    head_out, grad_plane = lax.optimization_barrier((head_out, grad_plane))
    o_all = deal_out(head_out.reshape(ranks, span, width), "ctx")
    o_rows, near, far = merge_heads(order[None], o_all, wo_t, heads)
    attn = fold(near, swap(far, *tp_steps[-1]), tp_steps[:-1])
    x_own = my_rows(tokens).astype(F32)
    middle = x_own + attn
    gain_two = mlp_gain.astype(F32)
    inv_two = lax.rsqrt(jnp.mean(middle * middle, axis=1, keepdims=True) + EPS)
    normed = (middle * inv_two * gain_two).astype(BF)
    near = spread_rows(to_plane(normed), plane_steps[:-1])
    far = swap(near, *tp_steps[-1])

    h2, act, pair, near, far, mlp, m_far = hidden_pass(near, far, grad_plane, hidden)
    far, act, pair = lax.optimization_barrier((swap(far, *tp_steps[-1]), act, pair))
    mlp = mlp + swap(m_far, *tp_steps[-1]).astype(F32)
    middle_steps = plane_steps[len(plane_steps) - len(tp_steps):-1]
    shard_steps = plane_steps[:-len(tp_steps)]
    d_two = fold(near, far, middle_steps)
    hidden_sum = hidden_grad(h2, grad_plane, act, pair)
    d_two, hidden_sum, mlp = lax.optimization_barrier((d_two, hidden_sum, mlp))
    hidden_sum = lax.psum_scatter(hidden_sum, "ctx", scatter_dimension=0, tiled=True)
    d_two = from_plane(gather_rows(d_two, shard_steps))

    def by_shard(grad):
        grad = grad.reshape(shards, share, grad.shape[1])
        if shards == 2:
            mine = lax.dynamic_index_in_dim(grad, shard, axis=0, keepdims=False)
            sent = lax.dynamic_index_in_dim(grad, 1 - shard, axis=0, keepdims=False)
            return [mine, swap(sent, "shard", 1)]
        return list(deal_out(grad, "shard"))

    d_gain_two = jnp.sum(d_two * middle * inv_two, axis=0)
    d_middle = grad_own.astype(F32) + norm_back(middle, inv_two, gain_two, d_two)
    d_attn = spread_rows(d_middle.astype(BF), tp_steps[:-1])
    d_attn = spread_rows(d_attn, tp_steps[-1:])
    d_heads = by_head(head_of, d_attn, wo_t, width)
    d_heads, d_attn, mlp = lax.optimization_barrier((d_heads, d_attn, mlp))
    d_heads = [d_heads[0]] + [
        lax.ppermute(
            d_heads[k], "ctx",
            [(i, (i + k) % ranks) for i in range(ranks) if (i + k) % ranks < heads],
        )
        for k in range(1, ranks)
    ]
    d_wout = dg(d_attn, o_rows, 0, 0).astype(BF)
    d_wout = sum_shard(d_wout.reshape(shards, ranks * share, columns)).astype(BF)
    mlp = gather_rows(mlp, middle_steps)
    d_heads, d_wout, mlp = lax.optimization_barrier((d_heads, d_wout, mlp))

    given = jnp.arange(group // small, dtype=jnp.int32)
    apart = (given % lanes) ^ lane
    turned = jnp.zeros_like(apart)
    for index, (_, bit) in enumerate(tp_steps):
        turned = turned + jnp.where((apart & bit) != 0, 1 << index, 0)
    place = (turned * ranks + given // lanes)[None]
    source = (given // lanes * lanes + turned)[None]
    near, far, d_proj, d_small, d_taps = attend_backward(
        deal, place, source, ((rank - turn) % ranks)[None], lengths, live, d_heads, taps, depth, saved
    )
    gain_one = attn_gain.astype(F32)
    mine = (jnp.arange(heads) == rank).astype(F32)
    taps_part = (mine[None, :, None] * d_taps[:, None]).reshape(conv_taps.shape)
    taps_part = jnp.pad(taps_part, ((0, 0), (0, depth - columns)))
    sum_steps = steps_of("ctx", False) + steps_of("shard", False)

    got = swap(far, *tp_steps[-1])
    mlp = from_plane(gather_rows(mlp, shard_steps))
    for axis, bit in tp_steps[:-1][::-1]:
        count, wide = near.shape[0] // 2, depth // 2
        sent = (near[count:] + got[count:].astype(F32)).astype(BF)
        first, last = swap(sent[:, :wide], axis, bit), swap(sent[:, wide:], axis, bit)
        near = near[:count] + got[:count].astype(F32)
        first, d_proj, mlp, d_wout = lax.optimization_barrier((first, d_proj, mlp, d_wout))

    d_one = jnp.concatenate(
        [near[:, :wide] + first.astype(F32), near[:, wide:] + last.astype(F32)], axis=1
    ).astype(BF).reshape(ranks, small, depth)
    d_w = dg(h1, d_proj[:, :4 * width], 0, 0).astype(BF)
    d_w = sum_shard(d_w.reshape(shards, ranks * share, 4 * width)).astype(BF)
    result = middle + mlp
    mask = my_rows(valid_mask).astype(F32)[:, None]
    branches = [x_own, attn, mlp, result]
    sums = [jnp.sum(mask * b * b, axis=0, keepdims=True) for b in branches]
    sums += [jnp.broadcast_to(jnp.sum(mask, axis=0, keepdims=True), (1, depth))]
    sums += [d_small[:1], d_gain_two[None], mine[:, None] * d_small[1][None], taps_part]
    sums = jnp.concatenate(sums, axis=0)
    def sum_ctx(parts):
        total = lax.dynamic_index_in_dim(parts, rank, axis=0, keepdims=False).astype(F32)
        for k in range(1, ranks):
            sent = lax.dynamic_index_in_dim(parts, (rank + k) % ranks, axis=0, keepdims=False)
            got = lax.ppermute(sent, "ctx", [(i, (i + k) % ranks) for i in range(ranks)])
            total = total + got.astype(F32)
        return total

    d_wout = sum_ctx(d_wout.reshape(ranks, share, columns)).T
    d_one, sums, result = lax.optimization_barrier((d_one, sums, result))
    total = sum_ctx(d_one)
    sums = sum_over(sums, sum_steps[:1])
    hidden_parts = by_shard(hidden_sum)
    d_one, result, sums, d_w, hidden_parts, d_wout = lax.optimization_barrier(
        (total, result, sums, d_w, hidden_parts, d_wout)
    )
    sums = sum_over(sums, sum_steps[1:])
    every = sum_over(sums[:7], tp_steps)

    d_w = d_w.reshape(ranks, share, 4 * width)
    w_blocks = [lax.dynamic_index_in_dim(d_w, rank, axis=0, keepdims=False)]
    for k in range(1, ranks):
        sent = lax.dynamic_index_in_dim(d_w, (rank + k) % ranks, axis=0, keepdims=False)
        pairs_k = [(i, (i + k) % ranks) for i in range(heads)]
        w_blocks.append(lax.ppermute(sent, "ctx", pairs_k))
    d_wgate, d_wup, d_wdown = unpack_hidden(order_s[None], hidden_parts)
    d_wdown = d_wdown.T
    inv_one = lax.rsqrt(jnp.mean(x_own * x_own, axis=1, keepdims=True) + EPS)
    d_input = d_middle + norm_back(x_own, inv_one, gain_one, d_one)
    both = jnp.concatenate([d_input.astype(BF), result.astype(BF)], axis=1)
    both = spread_rows(both, tp_steps)
    both, w_blocks = lax.optimization_barrier((both, w_blocks))
    both = both.reshape(lanes, small, 2 * depth)
    both = jnp.take(both, natural, axis=0).reshape(span, 2 * depth)
    d_tokens, output = both[:, :depth], both[:, depth:]
    totals, one_sum, two_sum = jnp.sum(every[:4], axis=1), every[5] / gain_one, every[6]
    beta_sum, taps_sum = sums[7:7 + heads], sums[7 + heads:]
    d_beta = lax.dynamic_slice_in_dim(beta_sum, (shard * ranks + rank) * share, share, axis=1).T
    d_conv = taps_sum[:, :columns]
    d_w = unpack_heads(((rank - turn) % ranks)[None], w_blocks, heads)
    rms_stats = jnp.sqrt(totals / (jnp.maximum(every[4, 0], 1.0) * depth))
    return (
        output, d_tokens, one_sum, d_w[0], d_w[1], d_w[2], d_w[3], d_beta, d_conv,
        d_wout, two_sum, d_wgate, d_wup, d_wdown, rms_stats,
    )


def solution(mesh):
    rows = P(("shard", "ctx"), None)
    tiled = P(("shard", "ctx"), "tp")
    turned = P("tp", ("shard", "ctx"))
    placed = (
        rows, rows, P(("shard", "ctx")), P("shard", None), P("shard", None), P(),
        tiled, tiled, tiled, tiled, tiled, P(None, "tp"), turned, P(), tiled, tiled, turned,
    )
    return jax.shard_map(
        local,
        mesh=mesh,
        in_specs=placed,
        out_specs=(
            rows, rows, P(), tiled, tiled, tiled, tiled, tiled, P(None, "tp"),
            turned, P(), tiled, tiled, turned, P(),
        ),
        check_vma=False,
    )
```

```python
import functools

import jax
import jax.numpy as jnp
from jax import lax
from jax.experimental import pallas as pl
from jax.experimental.pallas import tpu as pltpu
from jax.sharding import PartitionSpec as P

EPS = 1e-06
NEG = -1e30
BF = jnp.bfloat16
F32 = jnp.float32
CHUNK = 128


def dg(left, right, cl, cr):
    return lax.dot_general(left, right, (((cl,), (cr,)), ((), ())), preferred_element_type=F32)


def halves(value):
    high = value.astype(BF)
    return high, (value - high.astype(F32)).astype(BF)


def joined(pairs, cl=1, cr=0):
    lefts, rights = [], []
    for left, right in pairs:
        if left.dtype == BF and right.dtype == BF:
            lefts += [left]
            rights += [right]
        elif left.dtype == BF:
            lefts += [left, left]
            rights += halves(right)
        elif right.dtype == BF:
            lefts += halves(left)
            rights += [right, right]
        else:
            lh, ll = halves(left)
            rh, rl = halves(right)
            lefts += [lh, lh, ll]
            rights += [rh, rl, rh]
    return dg(jnp.concatenate(lefts, axis=cl), jnp.concatenate(rights, axis=cr), cl, cr)


def mm(left, right, cl=1, cr=0):
    return joined([(left, right)], cl, cr)


def ml(left, right, cl=1, cr=0):
    return dg(left.astype(BF), right.astype(BF), cl, cr)


def seg_at(position, ends):
    seg = (position >= ends[0]).astype(jnp.int32)
    for end in ends[1:]:
        seg = seg + (position >= end).astype(jnp.int32)
    return seg


def seq_ends(len_ref):
    ends = [len_ref[0, 0]]
    for index in range(1, len_ref.shape[1] - 1):
        ends.append(ends[-1] + len_ref[0, index])
    return ends


def shifted_mask(rows, width, shift, ends):
    here = lax.broadcasted_iota(jnp.int32, (rows, width), 0)
    back = here - shift
    return (back >= 0) & (seg_at(here, ends) == seg_at(back, ends))


def tile_iota():
    row = lax.broadcasted_iota(jnp.int32, (CHUNK, CHUNK), 0)
    col = lax.broadcasted_iota(jnp.int32, (CHUNK, CHUNK), 1)
    return row, col


def forward_kernel(x_count, w_count, *refs):
    deal_ref, spot_ref, slot_ref, len_ref = refs[:4]
    here_ref, refs = refs[4], refs[5:]
    x_refs, refs = refs[:x_count], refs[x_count:]
    gain_ref, refs = refs[0], refs[1:]
    w_refs, refs = refs[:w_count], refs[w_count:]
    taps_ref, o_ref, refs = refs[0], refs[1], refs[2:]
    kept, refs = refs[:SAVED], refs[SAVED:]
    held, (proj_ref, score_ref, sems) = refs[:SAVED], refs[SAVED:]
    (
        w_ref, wb_ref, h1_ref, q_ref, k_ref, v_ref, house_ref, raw_ref, logit_ref, prob_ref,
        u_ref, kt_ref, tr_ref, tinv_ref, xq_ref, yk_ref, z_ref,
    ) = held
    depth = here_ref.shape[1]
    pieces = deal_ref.shape[1]
    small = h1_ref.shape[0] // spot_ref.shape[1]
    rows = h1_ref.shape[0]
    piece = rows // pieces
    chunks = rows // CHUNK
    width = o_ref.shape[1]
    share = depth // w_count
    scale = width ** (-0.5)
    ends = seq_ends(len_ref)
    gain = gain_ref[...].astype(F32)

    def keep(first, last):
        for index in range(first, last):
            pltpu.make_async_copy(held[index], kept[index], sems.at[index]).start()

    pick = jnp.where(
        (lax.broadcasted_iota(jnp.int32, (16, width), 0) == 0)
        & (lax.broadcasted_iota(jnp.int32, (16, width), 1) == 0),
        1.0,
        0.0,
    ).astype(BF)
    for index, ref in enumerate(w_refs):
        base = pl.multiple_of(slot_ref[0, index] * share, share)
        w_ref[pl.ds(base, share), :] = ref[:share, :]
        wb_ref[pl.ds(base, share), :] = dg(ref[share:, :share], pick, 0, 0).astype(BF)

    def settle(x, index):
        x = x.astype(F32)
        inv = lax.rsqrt(jnp.mean(x * x, axis=1, keepdims=True) + EPS)
        base = pl.multiple_of(spot_ref[0, index] * small, small)
        h1_ref[pl.ds(base, small), :] = (x * inv * gain).astype(BF)

    local_count = here_ref.shape[0] // small
    for index in range(local_count):
        settle(here_ref[index * small:(index + 1) * small, :], index)
    for ref in x_refs:
        for index in range(ref.shape[0] // small):
            settle(ref[index * small:(index + 1) * small, :], local_count + index)
        local_count += ref.shape[0] // small
    keep(0, 3)

    for step in range(4):
        at = slice(step * width, (step + 1) * width)
        proj_ref[:, at] = dg(h1_ref[...], w_ref[:, at], 1, 0)
    logit_ref[...] = dg(h1_ref[...], wb_ref[...], 1, 0)
    q_ref[...] = proj_ref[:, :width].astype(BF)
    k_ref[...] = proj_ref[:, width:2 * width].astype(BF)
    v_ref[...] = proj_ref[:, 2 * width:3 * width].astype(BF)
    raw = proj_ref[:, 3 * width:4 * width]
    raw_ref[...] = raw
    taps = taps_ref[...].astype(F32)
    mixed = taps[0:1, :] * raw
    for shift in range(1, taps.shape[0]):
        moved = pltpu.roll(raw, shift, 0)
        mixed = mixed + taps[shift:shift + 1, :] * jnp.where(
            shifted_mask(rows, width, shift, ends), moved, 0.0
        )
    unit = mixed * lax.rsqrt(jnp.sum(mixed * mixed, axis=1, keepdims=True) + EPS)
    house_ref[...] = unit.astype(BF)
    keep(3, 9)

    row, col = tile_iota()
    strict = row > col
    eye = jnp.where(row == col, 1.0, 0.0)
    spans = [slice(n * CHUNK, (n + 1) * CHUNK) for n in range(chunks)]
    strength = [2.0 * jax.nn.sigmoid(logit_ref[s, 0:1]) for s in spans]
    system = []
    for n, s in enumerate(spans):
        house = house_ref[s, :]
        system.append(jnp.where(strict, strength[n] * dg(house, house, 1, 1), 0.0))
    inverse = [eye - jnp.where((row ^ col) == 1, a, 0.0) for a in system]
    level = 1
    while (1 << level) < CHUNK:
        block = ((row ^ col) >> level) == 1
        inner = [mm(jnp.where(block, a, 0.0), t) for a, t in zip(system, inverse)]
        inverse = [t - mm(t, i) for t, i in zip(inverse, inner)]
        level += 1
    for n, s in enumerate(spans):
        query, key, house = q_ref[s, :], k_ref[s, :], house_ref[s, :]
        tinv = inverse[n]
        tinv_ref[s, :] = tinv
        across = jnp.transpose(jnp.broadcast_to(strength[n], (CHUNK, CHUNK)))
        merged = tinv * across
        a_qw = jnp.where(row >= col, dg(query, house, 1, 1), 0.0)
        a_wk = jnp.where(strict, dg(house, key, 1, 1), 0.0)
        xq = mm(a_qw, merged)
        yk = mm(merged, a_wk)
        zz = mm(merged, house)
        xq_ref[s, :] = xq
        yk_ref[s, :] = yk
        z_ref[s, :] = zz
        score_ref[s, s] = (dg(query, key, 1, 1) - mm(xq, a_wk)) * scale
        proj_ref[s, :width] = query.astype(F32) - mm(xq, house)
        kt_ref[s, :] = key.astype(F32) - mm(yk, house, 0, 0)
        tr_ref[s, :] = eye - mm(house, zz, 0, 0)
    keep(11, SAVED)
    offset = 0
    for n in range(chunks - 2, -1, -1):
        later = slice((n + 1) * CHUNK, rows)
        count = rows - (n + 1) * CHUNK
        carried = proj_ref[later, :width]
        u_ref[offset:offset + count, :] = carried
        offset += count
        score_ref[later, spans[n]] = mm(carried, kt_ref[spans[n], :], 1, 1) * scale
        if n > 0:
            proj_ref[later, :width] = mm(carried, tr_ref[spans[n], :])
    keep(10, 11)
    for m, s in enumerate(spans):
        reach = (m + 1) * CHUNK
        at_row = lax.broadcasted_iota(jnp.int32, (CHUNK, reach), 0) + m * CHUNK
        at_col = lax.broadcasted_iota(jnp.int32, (CHUNK, reach), 1)
        seen = (at_row >= at_col) & (seg_at(at_row, ends) == seg_at(at_col, ends))
        logits = jnp.where(seen, score_ref[s, :reach], NEG)
        top = jnp.max(logits, axis=1, keepdims=True)
        grown = jnp.exp(logits - top)
        prob = grown / jnp.sum(grown, axis=1, keepdims=True)
        prob_ref[s, :reach] = prob
        proj_ref[s, :width] = dg(prob.astype(BF), v_ref[:reach, :], 1, 0)

    def give(step, carry):
        base = pl.multiple_of(step * piece, piece)
        given = pl.multiple_of(deal_ref[0, step] * piece, piece)
        o_ref[pl.ds(given, piece), :] = proj_ref[pl.ds(base, piece), :width].astype(BF)
        return carry

    keep(9, 10)
    lax.fori_loop(0, pieces, give, 0)
    for index in range(SAVED):
        pltpu.make_async_copy(held[index], kept[index], sems.at[index]).wait()


def backward_kernel(*refs):
    deal_ref, place_ref, source_ref, from_ref, len_ref, live_ref = refs[:6]
    ranks = from_ref.shape[1]
    parts, taps_ref, refs = refs[6:6 + ranks], refs[6 + ranks], refs[7 + ranks:]
    kept, refs = refs[:SAVED], refs[SAVED:]
    (near_ref, far_ref, dproj_ref, small_ref, dtaps_ref), refs = refs[:5], refs[5:]
    held, refs = refs[:SAVED], refs[SAVED:]
    ds_ref, dout_ref, du_ref, dkt_ref, dtr_ref, dhouse_ref, do_ref, sems = refs
    (
        w_ref, wb_ref, h1_ref, q_ref, k_ref, v_ref, house_ref, raw_ref, logit_ref, prob_ref,
        u_ref, kt_ref, tr_ref, tinv_ref, xq_ref, yk_ref, z_ref,
    ) = held

    def fetch(index):
        return pltpu.make_async_copy(kept[index], held[index], sems.at[index])

    needed = (5, 9), (10, 11, 12), (3, 4, 6, 8, 13, 14, 15, 16), (7,), (0, 1, 2)
    for index in sum(needed, ()):
        fetch(index).start()
    for k, ref in enumerate(parts):
        span = ref.shape[0]
        do_ref[pl.ds(pl.multiple_of(from_ref[0, k] * span, span), span), :] = ref[...]

    def ready(stage):
        for index in needed[stage]:
            fetch(index).wait()

    rows = do_ref.shape[0]
    pieces = deal_ref.shape[1]
    piece = rows // pieces
    small = rows // place_ref.shape[1]
    chunks = rows // CHUNK
    width = do_ref.shape[1]
    scale = width ** (-0.5)
    ends = seq_ends(len_ref)
    spans = [slice(n * CHUNK, (n + 1) * CHUNK) for n in range(chunks)]
    row, col = tile_iota()
    strict = row > col

    def take(step, carry):
        base = pl.multiple_of(step * piece, piece)
        for part in range(piece // small):
            there = source_ref[0, deal_ref[0, step] * (piece // small) + part]
            dout_ref[pl.ds(base + part * small, small), :] = do_ref[
                pl.ds(pl.multiple_of(there * small, small), small), :
            ]
        return carry

    lax.fori_loop(0, pieces, take, 0)
    ready(0)
    for m, s in enumerate(spans):
        reach = (m + 1) * CHUNK
        prob = prob_ref[s, :reach]
        dprob = dg(dout_ref[s, :], v_ref[:reach, :], 1, 1)
        dot = jnp.sum(prob * dprob, axis=1, keepdims=True)
        ds_ref[s, :reach] = prob * (dprob - dot) * scale
    for n, s in enumerate(spans):
        dproj_ref[s, 2 * width:3 * width] = dg(
            prob_ref[n * CHUNK:, s].astype(BF), dout_ref[n * CHUNK:, :], 0, 0
        ).astype(BF)
    starts = {}
    offset = 0
    for n in range(chunks - 2, -1, -1):
        starts[n] = offset
        offset += rows - (n + 1) * CHUNK
    ready(1)
    for n in range(chunks - 1):
        later = slice((n + 1) * CHUNK, rows)
        count = rows - (n + 1) * CHUNK
        grad = ds_ref[later, spans[n]]
        carried = u_ref[starts[n]:starts[n] + count, :]
        dkt_ref[spans[n], :] = mm(grad, carried, 0, 0)
        fresh = mm(grad, kt_ref[spans[n], :])
        if n > 0:
            before = du_ref[later, :]
            dtr_ref[spans[n], :] = mm(carried, before, 0, 0)
            fresh = fresh + mm(before, tr_ref[spans[n], :], 1, 1)
        du_ref[later, :] = fresh
    ready(2)
    for n, s in enumerate(spans):
        query, key, house = q_ref[s, :], k_ref[s, :], house_ref[s, :]
        strength = 2.0 * jax.nn.sigmoid(logit_ref[s, 0:1])
        tinv = tinv_ref[s, :]
        merged = tinv * jnp.transpose(jnp.broadcast_to(strength, (CHUNK, CHUNK)))
        a_qw = jnp.where(row >= col, dg(query, house, 1, 1), 0.0)
        a_wk = jnp.where(strict, dg(house, key, 1, 1), 0.0)
        gram = jnp.where(strict, dg(house, house, 1, 1), 0.0)
        xq, yk, zz = xq_ref[s, :], yk_ref[s, :], z_ref[s, :]
        di = ds_ref[s, s]
        first, final = n == 0, n == chunks - 1
        if first:
            dxq = mm(di, a_wk, 1, 1)
            da_qw = mm(di, yk, 1, 1)
        else:
            dqt = du_ref[s, :]
            dxq = joined([(di, a_wk), (dqt, house)], 1, 1)
            da_qw = joined([(di, yk), (dqt, zz)], 1, 1)
        da_qw = jnp.where(row >= col, da_qw, 0.0)
        dm = mm(a_qw, dxq, 0, 0)
        cross = [(xq, di)]
        if not final:
            dkt = dkt_ref[s, :]
            dyk = mm(house, dkt, 1, 1)
            cross.append((merged, dyk))
            outer = [(dyk, a_wk)]
            if not first:
                dtr = dtr_ref[s, :]
                wd = mm(house, dtr)
                outer.append((wd, house))
            dm = dm + joined(outer, 1, 1)
        da_wk = jnp.where(strict, joined(cross, 0, 0), 0.0)
        ee = mm(tinv, dm, 0, 0)
        rest = jnp.where(row == col, 1.0, 0.0) - mm(gram, merged)
        dstrength = -jnp.sum(ee * rest, axis=1, keepdims=True)
        dgram = jnp.where(strict, mm(strength * ee, merged, 1, 1), 0.0)
        dq = joined([(di, key), (-da_qw, house)])
        dk = joined([(di, query), (-da_wk, house)], 0, 0)
        tall = [(da_qw, query), (-dgram, house)]
        wide = [(da_wk, key), (-dgram, house)]
        if not first:
            dq = dq + dqt
            tall.append((xq, dqt))
        if not final:
            dk = dk + dkt
            wide.append((yk, dkt))
            if not first:
                tall.append((merged, wd))
        dw = joined(tall, 0, 0) + joined(wide)
        if not first and not final:
            dw = dw + mm(zz, dtr, 1, 1)
        dw = -dw
        dproj_ref[s, :width] = dq.astype(BF)
        dproj_ref[s, width:2 * width] = dk.astype(BF)
        dhouse_ref[s, :] = dw
        gate = 0.5 * strength
        dlogit = dstrength * 2.0 * gate * (1.0 - gate)
        lane = lax.broadcasted_iota(jnp.int32, (CHUNK, width), 1)
        dproj_ref[s, 4 * width:] = jnp.where(lane == 0, dlogit, 0.0).astype(BF)
    ready(3)
    raw = raw_ref[...]
    taps = taps_ref[...].astype(F32)
    count = taps.shape[0]
    mixed = taps[0:1, :] * raw
    earlier = [raw]
    masks = [None]
    for shift in range(1, count):
        masks.append(shifted_mask(rows, width, shift, ends))
        earlier.append(jnp.where(masks[shift], pltpu.roll(raw, shift, 0), 0.0))
        mixed = mixed + taps[shift:shift + 1, :] * earlier[shift]
    inv = lax.rsqrt(jnp.sum(mixed * mixed, axis=1, keepdims=True) + EPS)
    dunit = dhouse_ref[...]
    dmixed = inv * dunit - mixed * (
        inv * inv * inv * jnp.sum(dunit * mixed, axis=1, keepdims=True)
    )
    live = live_ref[0, 0].astype(F32)
    draw = taps[0:1, :] * dmixed
    dtaps_ref[0:1, :] = jnp.sum(dmixed * raw, axis=0, keepdims=True) * live
    for shift in range(1, count):
        dtaps_ref[shift:shift + 1, :] = (
            jnp.sum(dmixed * earlier[shift], axis=0, keepdims=True) * live
        )
        later = jnp.where(masks[shift], dmixed, 0.0)
        draw = draw + taps[shift:shift + 1, :] * pltpu.roll(later, rows - shift, 0)
    dproj_ref[:, 3 * width:4 * width] = draw.astype(BF)

    ready(4)

    small_ref[...] = jnp.zeros_like(small_ref)
    count = near_ref.shape[0] // small
    tile = 256

    def send(step, carry):
        at = pl.ds(pl.multiple_of(step * tile, tile), tile)
        dh1 = dg(dproj_ref[:, :4 * width], w_ref[at, :], 1, 1)
        dh1 = (dh1 + dg(dproj_ref[:, 4 * width:], wb_ref[at, :], 1, 1)) * live
        small_ref[0:1, at] = jnp.sum(dh1 * h1_ref[:, at].astype(F32), axis=0, keepdims=True)
        for block in range(rows // small):
            given = deal_ref[0, block * small // piece] * (piece // small)
            there = place_ref[0, given + block % (piece // small)]
            values = dh1[block * small:(block + 1) * small]

            @pl.when(there < count)
            def _():
                near_ref[pl.ds(pl.multiple_of(there * small, small), small), at] = values

            @pl.when(there >= count)
            def _():
                to = pl.ds(pl.multiple_of((there - count) * small, small), small)
                far_ref[to, at] = values.astype(BF)

        return carry

    lax.fori_loop(0, h1_ref.shape[1] // tile, send, 0)
    beta = dg(dproj_ref[:, 4 * width:], h1_ref[...], 0, 0)
    small_ref[1:2, :] = beta[0:1, :] * live


SAVED = 17


def saved_shapes(rows, depth, width):
    chunks = rows // CHUNK
    carried = CHUNK * chunks * (chunks - 1) // 2
    slim = ((rows, width), BF)
    tall = ((rows, width), F32)
    return (
        ((depth, 4 * width), BF), ((depth, width), BF), ((rows, depth), BF), slim, slim, slim, slim,
        tall, tall, ((rows, rows), F32), ((carried, width), F32), tall, tall, tall, tall, tall, tall,
    )


VMEM = pl.BlockSpec(memory_space=pltpu.VMEM)
SMEM = pl.BlockSpec(memory_space=pltpu.SMEM)
AWAY = pl.BlockSpec(memory_space=pl.ANY)
LIMIT = pltpu.CompilerParams(vmem_limit_bytes=56 * 1024 * 1024)


def attend_forward(deal, spot, slot, lengths, here, x_parts, gain, w_parts, taps):
    depth = here.shape[1]
    rows = here.shape[0] + sum(part_.shape[0] for part_ in x_parts)
    width = taps.shape[1]
    saved = saved_shapes(rows, depth, width)
    return pl.pallas_call(
        functools.partial(forward_kernel, len(x_parts), len(w_parts)),
        out_shape=(jax.ShapeDtypeStruct((rows, width), BF),)
        + tuple(jax.ShapeDtypeStruct(*entry) for entry in saved),
        in_specs=[SMEM] * 4 + [VMEM] * (len(x_parts) + len(w_parts) + 3),
        out_specs=(VMEM,) + (AWAY,) * SAVED,
        scratch_shapes=[pltpu.VMEM(*entry) for entry in saved]
        + [
            pltpu.VMEM((rows, 4 * width), F32),
            pltpu.VMEM((rows, rows), F32),
            pltpu.SemaphoreType.DMA((SAVED,)),
        ],
        compiler_params=LIMIT,
        cost_estimate=pl.CostEstimate(flops=16 * 10**9, bytes_accessed=10**7, transcendentals=0),
        name="attend_forward",
    )(deal, spot, slot, lengths, here, *x_parts, gain, *w_parts, taps)


def attend_backward(deal, place, source, origin, lengths, live, d_out, taps, depth, kept):
    rows, width = d_out[0].shape[0] * len(d_out), d_out[0].shape[1]
    saved = saved_shapes(rows, depth, width)
    return pl.pallas_call(
        backward_kernel,
        out_shape=(
            jax.ShapeDtypeStruct((rows // 2, depth), F32),
            jax.ShapeDtypeStruct((rows // 2, depth), BF),
            jax.ShapeDtypeStruct((rows, 5 * width), BF),
            jax.ShapeDtypeStruct((8, depth), F32),
            jax.ShapeDtypeStruct((taps.shape[0], width), F32),
        ),
        in_specs=[SMEM] * 6 + [VMEM] * (len(d_out) + 1) + [AWAY] * SAVED,
        out_specs=(VMEM,) * 5,
        scratch_shapes=[pltpu.VMEM(*entry) for entry in saved]
        + [
            pltpu.VMEM((rows, rows), F32),
            pltpu.VMEM((rows, width), BF),
            pltpu.VMEM((rows, width), F32),
            pltpu.VMEM((rows, width), F32),
            pltpu.VMEM((rows, width), F32),
            pltpu.VMEM((rows, width), F32),
            pltpu.VMEM((rows, width), BF),
            pltpu.SemaphoreType.DMA((SAVED,)),
        ],
        compiler_params=LIMIT,
        cost_estimate=pl.CostEstimate(flops=20 * 10**9, bytes_accessed=10**7, transcendentals=0),
        name="attend_backward",
    )(deal, place, source, origin, lengths, live, *d_out, taps, *kept)


def head_kernel(head_ref, left_ref, right_ref, *outs):
    width = outs[0].shape[1]
    every = dg(left_ref[...], right_ref[...], 1, 0).astype(BF)
    for k, out in enumerate(outs):
        for head in range(right_ref.shape[1] // width):

            @pl.when(head_ref[0, k] == head)
            def _():
                out[...] = every[:, head * width:(head + 1) * width]


def by_head(head, left, right, width):
    ranks = head.shape[1]
    return pl.pallas_call(
        head_kernel,
        out_shape=(jax.ShapeDtypeStruct((left.shape[0], width), BF),) * ranks,
        in_specs=[SMEM, VMEM, VMEM],
        out_specs=(VMEM,) * ranks,
        compiler_params=LIMIT,
        cost_estimate=pl.CostEstimate(flops=3 * 10**9, bytes_accessed=10**6, transcendentals=0),
        name="by_head",
    )(head, left, right)


def pack_kernel(heads, ranks, shards, *refs):
    head_ref, order_ref = refs[:2]
    projections = refs[2:6]
    beta_ref, gate_ref, up_ref, down_ref = refs[6:10]
    blocks, parts = refs[10:10 + ranks], refs[10 + ranks:]
    share, columns = projections[0].shape
    width = columns // heads
    part = gate_ref.shape[1] // shards
    beta = beta_ref[...].astype(F32)
    for k, block in enumerate(blocks):
        head = head_ref[0, k]
        at = pl.multiple_of(head * width, width)
        for index, ref in enumerate(projections):
            block[:share, index * width:(index + 1) * width] = ref[:, pl.ds(at, width)]
        row = beta[0:1, :]
        for other in range(1, heads):
            row = jnp.where(head == other, beta[other:other + 1, :], row)
        block[share:, :] = jnp.zeros((block.shape[0] - share, block.shape[1]), BF)
        block[share:, :share] = jnp.broadcast_to(row, (block.shape[0] - share, share)).astype(BF)
    for index, ref in enumerate(parts):
        at = pl.multiple_of(order_ref[0, index] * part, part)
        ref[:, :part] = gate_ref[:, pl.ds(at, part)]
        ref[:, part:2 * part] = up_ref[:, pl.ds(at, part)]
        ref[:, 2 * part:] = down_ref[:, pl.ds(at, part)]


def pack(head, order, projections, w_beta, w_gate, w_up, w_down, ranks):
    share, columns = projections[0].shape
    heads = w_beta.shape[0]
    shards = order.shape[1]
    width = columns // heads
    part = w_gate.shape[1] // shards
    out = pl.pallas_call(
        functools.partial(pack_kernel, heads, ranks, shards),
        out_shape=(jax.ShapeDtypeStruct((share + 16, 4 * width), BF),) * ranks
        + (jax.ShapeDtypeStruct((share, 3 * part), BF),) * shards,
        in_specs=[SMEM, SMEM] + [VMEM] * 8,
        out_specs=(VMEM,) * (ranks + shards),
        compiler_params=LIMIT,
        cost_estimate=pl.CostEstimate(flops=3 * 10**9, bytes_accessed=10**6, transcendentals=0),
        name="pack",
    )(head, order, *projections, w_beta, w_gate, w_up, w_down)
    return list(out[:ranks]), list(out[ranks:])


def unpack_hidden_kernel(shards, *refs):
    order_ref, blocks = refs[0], refs[1:1 + shards]
    gate_ref, up_ref, down_ref = refs[1 + shards:]
    part = blocks[0].shape[1] // 3
    for index, block in enumerate(blocks):
        at = pl.multiple_of(order_ref[0, index] * part, part)
        gate_ref[:, pl.ds(at, part)] = block[:, :part].astype(F32)
        up_ref[:, pl.ds(at, part)] = block[:, part:2 * part].astype(F32)
        down_ref[:, pl.ds(at, part)] = block[:, 2 * part:].astype(F32)


def unpack_hidden(order, blocks):
    shards = len(blocks)
    share, part = blocks[0].shape[0], blocks[0].shape[1] // 3
    wide = jax.ShapeDtypeStruct((share, shards * part), F32)
    return pl.pallas_call(
        functools.partial(unpack_hidden_kernel, shards),
        out_shape=(wide,) * 3,
        in_specs=[SMEM] + [VMEM] * shards,
        out_specs=(VMEM,) * 3,
        compiler_params=LIMIT,
        cost_estimate=pl.CostEstimate(flops=2 * 10**9, bytes_accessed=10**6, transcendentals=0),
        name="unpack_hidden",
    )(order, *blocks)


def merge_kernel(order_ref, o_ref, w_ref, rows_ref, near_ref, far_ref):
    span, columns = rows_ref.shape
    width = o_ref.shape[2]
    small = span // order_ref.shape[1]
    for slot in range(order_ref.shape[1]):
        at = pl.multiple_of(order_ref[0, slot] * small, small)
        for head in range(columns // width):
            rows_ref[slot * small:(slot + 1) * small, head * width:(head + 1) * width] = o_ref[
                head, pl.ds(at, small), :
            ]
    total = dg(rows_ref[...], w_ref[...], 1, 1)
    near_ref[...] = total[:span // 2]
    far_ref[...] = total[span // 2:].astype(BF)


def merge_heads(order, head_rows, w_out, heads):
    span, width = head_rows.shape[1:]
    depth = w_out.shape[0]
    return pl.pallas_call(
        merge_kernel,
        out_shape=(
            jax.ShapeDtypeStruct((span, heads * width), BF),
            jax.ShapeDtypeStruct((span // 2, depth), F32),
            jax.ShapeDtypeStruct((span // 2, depth), BF),
        ),
        in_specs=[SMEM, VMEM, VMEM],
        out_specs=(VMEM,) * 3,
        compiler_params=LIMIT,
        cost_estimate=pl.CostEstimate(flops=3 * 10**9, bytes_accessed=10**6, transcendentals=0),
        name="merge_heads",
    )(order, head_rows, w_out)


def hidden_kernel(
    near_ref, far_ref, grad_ref, w_ref, h2_ref, act_ref, pair_ref,
    d_near_ref, d_far_ref, m_near_ref, m_far_ref,
):
    half = near_ref.shape[0]
    part = act_ref.shape[1]
    tile = min(part, 256)
    h2_ref[:half, :] = near_ref[...]
    h2_ref[half:, :] = far_ref[...]
    for start in range(0, part, tile):
        gate = dg(h2_ref[...], w_ref[:, start:start + tile], 1, 0)
        up = dg(h2_ref[...], w_ref[:, part + start:part + start + tile], 1, 0)
        d_act = dg(grad_ref[...], w_ref[:, 2 * part + start:2 * part + start + tile], 1, 0)
        sig = jax.nn.sigmoid(gate)
        swish = gate * sig
        act_ref[:, start:start + tile] = (swish * up).astype(BF)
        pair_ref[:, start:start + tile] = (
            d_act * up * sig * (1.0 + gate * (1.0 - sig))
        ).astype(BF)
        pair_ref[:, part + start:part + start + tile] = (d_act * swish).astype(BF)
    d_far_ref[...] = dg(pair_ref[half:, :], w_ref[:, :2 * part], 1, 1).astype(BF)
    d_near_ref[...] = dg(pair_ref[:half, :], w_ref[:, :2 * part], 1, 1)
    m_far_ref[...] = dg(act_ref[half:, :], w_ref[:, 2 * part:], 1, 1).astype(BF)
    m_near_ref[...] = dg(act_ref[:half, :], w_ref[:, 2 * part:], 1, 1)


def hidden_pass(near, far, grad, weights):
    half, depth = near.shape
    part = weights.shape[1] // 3
    keep = jax.ShapeDtypeStruct((half, depth), F32)
    sent = jax.ShapeDtypeStruct((half, depth), BF)
    return pl.pallas_call(
        hidden_kernel,
        out_shape=(
            jax.ShapeDtypeStruct((2 * half, depth), BF),
            jax.ShapeDtypeStruct((2 * half, part), BF),
            jax.ShapeDtypeStruct((2 * half, 2 * part), BF),
            keep, sent, keep, sent,
        ),
        in_specs=[VMEM] * 4,
        out_specs=(VMEM,) * 7,
        compiler_params=LIMIT,
        cost_estimate=pl.CostEstimate(flops=9 * 10**9, bytes_accessed=10**6, transcendentals=0),
        name="hidden_pass",
    )(near, far, grad, weights)


def hidden_grad_kernel(h2_ref, grad_ref, act_ref, pair_ref, out_ref, turned_ref):
    depth, part = out_ref.shape[0], act_ref.shape[1]
    tile = min(part, 256)
    for source, value, start in ((h2_ref, pair_ref, 0), (grad_ref, act_ref, 2 * part)):
        for at in range(0, depth, 256):
            turned_ref[at:at + 256, :] = source[:, at:at + 256].astype(F32).T.astype(BF)
        for at in range(0, value.shape[1], tile):
            out_ref[:, start + at:start + at + tile] = dg(
                turned_ref[...], value[:, at:at + tile], 1, 0
            ).astype(BF)


def hidden_grad(h2, grad, act, pair):
    depth, part = h2.shape[1], act.shape[1]
    return pl.pallas_call(
        hidden_grad_kernel,
        out_shape=jax.ShapeDtypeStruct((depth, 3 * part), BF),
        in_specs=[VMEM] * 4,
        out_specs=VMEM,
        scratch_shapes=[pltpu.VMEM((depth, h2.shape[0]), BF)],
        compiler_params=LIMIT,
        cost_estimate=pl.CostEstimate(flops=8 * 10**9, bytes_accessed=10**6, transcendentals=0),
        name="hidden_grad",
    )(h2, grad, act, pair)


def unpack_heads_kernel(ranks, heads, *refs):
    source_ref, blocks, grads = refs[0], refs[1:1 + ranks], refs[1 + ranks:]
    width = blocks[0].shape[1] // len(grads)
    for k, block in enumerate(blocks):
        source = source_ref[0, k]

        @pl.when(source < heads)
        def _():
            at = pl.multiple_of(source * width, width)
            for index, ref in enumerate(grads):
                ref[:, pl.ds(at, width)] = block[:, index * width:(index + 1) * width].astype(F32)


def unpack_heads(source, blocks, heads):
    ranks = len(blocks)
    share, columns = blocks[0].shape[0], blocks[0].shape[1] // 4 * heads
    return pl.pallas_call(
        functools.partial(unpack_heads_kernel, ranks, heads),
        out_shape=(jax.ShapeDtypeStruct((share, columns), F32),) * 4,
        in_specs=[SMEM] + [VMEM] * ranks,
        out_specs=(VMEM,) * 4,
        compiler_params=LIMIT,
        cost_estimate=pl.CostEstimate(flops=2 * 10**9, bytes_accessed=10**6, transcendentals=0),
        name="unpack_heads",
    )(source, *blocks)


def steps_of(axis, descending):
    size = lax.axis_size(axis)
    bits = []
    bit = 1
    while bit < size:
        bits.append((axis, bit))
        bit *= 2
    return bits[::-1] if descending else bits


def swap(value, axis, bit):
    size = lax.axis_size(axis)
    return lax.ppermute(value, axis, [(i, i ^ bit) for i in range(size)])


def spread_rows(value, steps):
    for axis, bit in steps:
        value = jnp.concatenate([value, swap(value, axis, bit)], axis=0)
    return value


def gather_rows(value, steps):
    for axis, bit in steps[::-1]:
        half = value.shape[0] // 2
        value = value[:half] + swap(value[half:].astype(BF), axis, bit).astype(F32)
    return value


def fold(kept, got, steps):
    for axis, bit in steps[::-1]:
        half = kept.shape[0] // 2
        sent = (kept[half:] + got[half:].astype(F32)).astype(BF)
        kept, got = kept[:half] + got[:half].astype(F32), swap(sent, axis, bit)
    return kept + got.astype(F32)


def in_order(mine, other):
    first = lax.axis_index("shard") == 0
    return jnp.stack([jnp.where(first, mine, other), jnp.where(first, other, mine)])


def over_shard(value):
    if lax.axis_size("shard") == 2:
        return in_order(value, swap(value, "shard", 1))
    return lax.all_gather(value, "shard", axis=0, tiled=False)


def across_shard(parts):
    if lax.axis_size("shard") == 2:
        shard = lax.axis_index("shard")
        mine = lax.dynamic_index_in_dim(parts, shard, axis=0, keepdims=False)
        sent = lax.dynamic_index_in_dim(parts, 1 - shard, axis=0, keepdims=False)
        return in_order(mine, swap(sent, "shard", 1))
    return deal_out(parts, "shard")


def sum_shard(parts):
    if lax.axis_size("shard") == 2:
        shard = lax.axis_index("shard")
        mine = lax.dynamic_index_in_dim(parts, shard, axis=0, keepdims=False)
        sent = lax.dynamic_index_in_dim(parts, 1 - shard, axis=0, keepdims=False)
        return mine.astype(F32) + swap(sent, "shard", 1).astype(F32)
    return jnp.sum(deal_out(parts, "shard").astype(F32), axis=0)


def over_ctx(value):
    ranks = lax.axis_size("ctx")
    got = [value] + [
        lax.ppermute(value, "ctx", [(i, (i + k) % ranks) for i in range(ranks)])
        for k in range(1, ranks)
    ]
    return got


def sum_over(value, steps):
    for axis, bit in steps:
        value = value + swap(value, axis, bit)
    return value


def deal_out(value, axis):
    return lax.all_to_all(value, axis, split_axis=0, concat_axis=0, tiled=True)


def norm_back(value, inverse, gain, grad):
    scaled = grad * gain
    return inverse * scaled - value * inverse**3 * jnp.mean(scaled * value, axis=1, keepdims=True)


def local(
    tokens, cotangent, valid_mask, lengths, deal, attn_gain,
    w_query, w_key, w_value, w_house, w_beta, conv_taps, w_out,
    mlp_gain, w_gate, w_up, w_down,
):
    shards, ranks, lanes = (lax.axis_size(a) for a in ("shard", "ctx", "tp"))
    shard, rank, lane = (lax.axis_index(a) for a in ("shard", "ctx", "tp"))
    span, depth = tokens.shape
    share, columns = w_query.shape
    heads = w_beta.shape[1]
    width = columns // heads
    piece = span // 2
    group = ranks * span
    small = span // lanes
    part = w_gate.shape[1] // shards
    spare = ranks - heads
    tp_steps = steps_of("tp", True)
    plane_steps = steps_of("shard", False) + tp_steps
    live = (rank < heads).astype(jnp.int32).reshape(1, 1)
    head_at = jnp.minimum(rank, heads - 1)

    shifted = over_ctx(lax.dynamic_slice_in_dim(tokens, lane * small, small, axis=0))[1:]

    turn = jnp.arange(ranks, dtype=jnp.int32)
    order_s = jnp.arange(shards, dtype=jnp.int32)
    if shards == 2:
        order_s = order_s ^ shard
    head_of = jnp.minimum((rank + turn) % ranks, heads - 1)[None]
    blocks, hidden = pack(
        head_of, order_s[None],
        (w_query, w_key, w_value, w_house), w_beta.T, w_gate, w_up, w_down.T, ranks,
    )
    crossed = [blocks[0]]
    for k in range(1, ranks):
        pairs = [(i, (i + k) % ranks) for i in range(ranks) if (i + k) % ranks < heads]
        crossed.append(lax.ppermute(blocks[k], "ctx", pairs))
    slots_of = []
    taps = lax.dynamic_slice_in_dim(conv_taps, head_at * width, width, axis=1)

    x_parts, apart_of = list(shifted), [0]
    x_parts = [jnp.concatenate(shifted, axis=0)]
    for axis, bit in tp_steps:
        joined_parts = jnp.concatenate(x_parts, axis=0) if len(x_parts) > 1 else x_parts[0]
        x_parts = x_parts + [swap(joined_parts, axis, bit)]
        apart_of = apart_of + [other ^ bit for other in apart_of]
    owners = (rank - jnp.arange(1, ranks, dtype=jnp.int32)) % ranks
    blocks_of = [rank * lanes + jnp.arange(lanes, dtype=jnp.int32)]
    blocks_of += [owners * lanes + (lane ^ apart) for apart in apart_of]
    blocks_of = jnp.concatenate(blocks_of)
    labels = jnp.arange(2 * ranks, dtype=jnp.int32)
    per_piece = lanes // 2
    at_piece = jnp.sum(
        jnp.where(deal[0][None, :] == (blocks_of // per_piece)[:, None], labels[None, :], 0), axis=1
    )
    spot = (at_piece * per_piece + blocks_of % per_piece)[None]
    w_parts = []
    for k, block in enumerate(crossed):
        source = (rank - k) % ranks
        if shards == 2:
            w_parts += [block, swap(block, "shard", 1)]
            slots_of += [shard * ranks + source, (1 - shard) * ranks + source]
        else:
            every = lax.all_gather(block, "shard", axis=0, tiled=False)
            w_parts += [every[i] for i in range(shards)]
            slots_of += [i * ranks + source for i in range(shards)]
    slot = jnp.stack(slots_of)[None]

    wo_t = over_shard(w_out.T).reshape(shards * share, columns)
    wo_t = lax.all_gather(wo_t, "ctx", axis=0, tiled=False)
    wo_t = wo_t.reshape(ranks, shards, share, columns).transpose(1, 0, 2, 3).reshape(depth, columns)
    grad_own = lax.dynamic_slice_in_dim(cotangent, lane * small, small, axis=0)
    hidden, grad_start, _ = lax.optimization_barrier((hidden, grad_own, shifted))
    if shards == 2:
        hidden = [hidden[0], swap(hidden[1], "shard", 1)]
    else:
        hidden = list(deal_out(jnp.stack(hidden), "shard"))
    def to_plane(value):
        value = value.reshape(-1, shards, ranks, share).transpose(0, 2, 1, 3)
        return value.reshape(-1, depth)

    def from_plane(value):
        value = value.reshape(-1, ranks, shards, share).transpose(0, 2, 1, 3)
        return value.reshape(-1, depth)

    def my_rows(value):
        return lax.dynamic_slice_in_dim(value, lane * small, small, axis=0)

    grad_plane = spread_rows(to_plane(grad_start), plane_steps)
    hidden, _, _ = lax.optimization_barrier((hidden, shifted, crossed))
    hidden = in_order(*hidden) if shards == 2 else jnp.stack(hidden)
    hidden = hidden.reshape(shards * share, 3 * part)
    hidden = lax.all_gather(hidden, "ctx", axis=0, tiled=True)
    fwd = attend_forward(deal, spot, slot, lengths, tokens, x_parts, attn_gain[None], w_parts, taps)
    head_out, saved = fwd[0], fwd[1:]
    h1 = saved[2]
    slots = jnp.arange(lanes, dtype=jnp.int32)
    order = jnp.full_like(slots, lane)
    for index, (_, bit) in enumerate(tp_steps):
        order = order ^ jnp.where((slots >> index) % 2 == 1, bit, 0)
    natural = jnp.zeros_like(slots)
    for index, (_, bit) in enumerate(tp_steps):
        natural = natural + jnp.where(((slots ^ lane) & bit) != 0, 1 << index, 0)
    head_out, grad_plane = lax.optimization_barrier((head_out, grad_plane))
    o_all = deal_out(head_out.reshape(ranks, span, width), "ctx")
    o_rows, near, far = merge_heads(order[None], o_all, wo_t, heads)
    attn = fold(near, swap(far, *tp_steps[-1]), tp_steps[:-1])
    x_own = my_rows(tokens).astype(F32)
    middle = x_own + attn
    gain_two = mlp_gain.astype(F32)
    inv_two = lax.rsqrt(jnp.mean(middle * middle, axis=1, keepdims=True) + EPS)
    normed = (middle * inv_two * gain_two).astype(BF)
    near = spread_rows(to_plane(normed), plane_steps[:-1])
    far = swap(near, *tp_steps[-1])

    h2, act, pair, near, far, mlp, m_far = hidden_pass(near, far, grad_plane, hidden)
    far, act, pair = lax.optimization_barrier((swap(far, *tp_steps[-1]), act, pair))
    mlp = mlp + swap(m_far, *tp_steps[-1]).astype(F32)
    middle_steps = plane_steps[len(plane_steps) - len(tp_steps):-1]
    shard_steps = plane_steps[:-len(tp_steps)]
    d_two = fold(near, far, middle_steps)
    hidden_sum = hidden_grad(h2, grad_plane, act, pair)
    d_two, hidden_sum, mlp = lax.optimization_barrier((d_two, hidden_sum, mlp))
    hidden_sum = lax.psum_scatter(hidden_sum, "ctx", scatter_dimension=0, tiled=True)
    d_two = from_plane(gather_rows(d_two, shard_steps))

    def by_shard(grad):
        grad = grad.reshape(shards, share, grad.shape[1])
        if shards == 2:
            mine = lax.dynamic_index_in_dim(grad, shard, axis=0, keepdims=False)
            sent = lax.dynamic_index_in_dim(grad, 1 - shard, axis=0, keepdims=False)
            return [mine, swap(sent, "shard", 1)]
        return list(deal_out(grad, "shard"))

    d_gain_two = jnp.sum(d_two * middle * inv_two, axis=0)
    d_middle = grad_own.astype(F32) + norm_back(middle, inv_two, gain_two, d_two)
    d_attn = spread_rows(d_middle.astype(BF), tp_steps[:-1])
    d_attn = spread_rows(d_attn, tp_steps[-1:])
    d_heads = by_head(head_of, d_attn, wo_t, width)
    d_heads, d_attn, mlp = lax.optimization_barrier((d_heads, d_attn, mlp))
    d_heads = [d_heads[0]] + [
        lax.ppermute(
            d_heads[k], "ctx",
            [(i, (i + k) % ranks) for i in range(ranks) if (i + k) % ranks < heads],
        )
        for k in range(1, ranks)
    ]
    d_wout = dg(d_attn, o_rows, 0, 0).astype(BF)
    d_wout = sum_shard(d_wout.reshape(shards, ranks * share, columns)).astype(BF)
    mlp = gather_rows(mlp, middle_steps)
    d_heads, d_wout, mlp = lax.optimization_barrier((d_heads, d_wout, mlp))

    given = jnp.arange(group // small, dtype=jnp.int32)
    apart = (given % lanes) ^ lane
    turned = jnp.zeros_like(apart)
    for index, (_, bit) in enumerate(tp_steps):
        turned = turned + jnp.where((apart & bit) != 0, 1 << index, 0)
    place = (turned * ranks + given // lanes)[None]
    source = (given // lanes * lanes + turned)[None]
    near, far, d_proj, d_small, d_taps = attend_backward(
        deal, place, source, ((rank - turn) % ranks)[None], lengths, live, d_heads, taps, depth, saved
    )
    gain_one = attn_gain.astype(F32)
    mine = (jnp.arange(heads) == rank).astype(F32)
    taps_part = (mine[None, :, None] * d_taps[:, None]).reshape(conv_taps.shape)
    taps_part = jnp.pad(taps_part, ((0, 0), (0, depth - columns)))
    sum_steps = steps_of("ctx", False) + steps_of("shard", False)

    got = swap(far, *tp_steps[-1])
    mlp = from_plane(gather_rows(mlp, shard_steps))
    for axis, bit in tp_steps[:-1][::-1]:
        count, wide = near.shape[0] // 2, depth // 2
        sent = (near[count:] + got[count:].astype(F32)).astype(BF)
        first, last = swap(sent[:, :wide], axis, bit), swap(sent[:, wide:], axis, bit)
        near = near[:count] + got[:count].astype(F32)
        first, d_proj, mlp, d_wout = lax.optimization_barrier((first, d_proj, mlp, d_wout))

    d_one = jnp.concatenate(
        [near[:, :wide] + first.astype(F32), near[:, wide:] + last.astype(F32)], axis=1
    ).astype(BF).reshape(ranks, small, depth)
    d_w = dg(h1, d_proj[:, :4 * width], 0, 0).astype(BF)
    d_w = sum_shard(d_w.reshape(shards, ranks * share, 4 * width)).astype(BF)
    result = middle + mlp
    mask = my_rows(valid_mask).astype(F32)[:, None]
    branches = [x_own, attn, mlp, result]
    sums = [jnp.sum(mask * b * b, axis=0, keepdims=True) for b in branches]
    sums += [jnp.broadcast_to(jnp.sum(mask, axis=0, keepdims=True), (1, depth))]
    sums += [d_small[:1], d_gain_two[None], mine[:, None] * d_small[1][None], taps_part]
    sums = jnp.concatenate(sums, axis=0)
    def sum_ctx(parts):
        total = lax.dynamic_index_in_dim(parts, rank, axis=0, keepdims=False).astype(F32)
        for k in range(1, ranks):
            sent = lax.dynamic_index_in_dim(parts, (rank + k) % ranks, axis=0, keepdims=False)
            got = lax.ppermute(sent, "ctx", [(i, (i + k) % ranks) for i in range(ranks)])
            total = total + got.astype(F32)
        return total

    d_wout = sum_ctx(d_wout.reshape(ranks, share, columns)).T
    d_one, sums, result = lax.optimization_barrier((d_one, sums, result))
    total = sum_ctx(d_one)
    sums = sum_over(sums, sum_steps[:2])
    hidden_parts = by_shard(hidden_sum)
    d_one, result, sums, d_w, hidden_parts, d_wout = lax.optimization_barrier(
        (total, result, sums, d_w, hidden_parts, d_wout)
    )
    sums = sum_over(sums, sum_steps[2:])
    every = sum_over(sums[:7], tp_steps)

    d_w = d_w.reshape(ranks, share, 4 * width)
    w_blocks = [lax.dynamic_index_in_dim(d_w, rank, axis=0, keepdims=False)]
    for k in range(1, ranks):
        sent = lax.dynamic_index_in_dim(d_w, (rank + k) % ranks, axis=0, keepdims=False)
        pairs_k = [(i, (i + k) % ranks) for i in range(heads)]
        w_blocks.append(lax.ppermute(sent, "ctx", pairs_k))
    d_wgate, d_wup, d_wdown = unpack_hidden(order_s[None], hidden_parts)
    d_wdown = d_wdown.T
    inv_one = lax.rsqrt(jnp.mean(x_own * x_own, axis=1, keepdims=True) + EPS)
    d_input = d_middle + norm_back(x_own, inv_one, gain_one, d_one)
    both = jnp.concatenate([d_input.astype(BF), result.astype(BF)], axis=1)
    both = spread_rows(both, tp_steps)
    both, w_blocks = lax.optimization_barrier((both, w_blocks))
    both = both.reshape(lanes, small, 2 * depth)
    both = jnp.take(both, natural, axis=0).reshape(span, 2 * depth)
    d_tokens, output = both[:, :depth], both[:, depth:]
    totals, one_sum, two_sum = jnp.sum(every[:4], axis=1), every[5] / gain_one, every[6]
    beta_sum, taps_sum = sums[7:7 + heads], sums[7 + heads:]
    d_beta = lax.dynamic_slice_in_dim(beta_sum, (shard * ranks + rank) * share, share, axis=1).T
    d_conv = taps_sum[:, :columns]
    d_w = unpack_heads(((rank - turn) % ranks)[None], w_blocks, heads)
    rms_stats = jnp.sqrt(totals / (jnp.maximum(every[4, 0], 1.0) * depth))
    return (
        output, d_tokens, one_sum, d_w[0], d_w[1], d_w[2], d_w[3], d_beta, d_conv,
        d_wout, two_sum, d_wgate, d_wup, d_wdown, rms_stats,
    )


def solution(mesh):
    rows = P(("shard", "ctx"), None)
    tiled = P(("shard", "ctx"), "tp")
    turned = P("tp", ("shard", "ctx"))
    placed = (
        rows, rows, P(("shard", "ctx")), P("shard", None), P("shard", None), P(),
        tiled, tiled, tiled, tiled, tiled, P(None, "tp"), turned, P(), tiled, tiled, turned,
    )
    return jax.shard_map(
        local,
        mesh=mesh,
        in_specs=placed,
        out_specs=(
            rows, rows, P(), tiled, tiled, tiled, tiled, tiled, P(None, "tp"),
            turned, P(), tiled, tiled, turned, P(),
        ),
        check_vma=False,
    )
```

```python
import functools

import jax
import jax.numpy as jnp
from jax import lax
from jax.experimental import pallas as pl
from jax.experimental.pallas import tpu as pltpu
from jax.sharding import PartitionSpec as P

EPS = 1e-06
NEG = -1e30
BF = jnp.bfloat16
F32 = jnp.float32
CHUNK = 128


def dg(left, right, cl, cr):
    return lax.dot_general(left, right, (((cl,), (cr,)), ((), ())), preferred_element_type=F32)


def halves(value):
    high = value.astype(BF)
    return high, (value - high.astype(F32)).astype(BF)


def joined(pairs, cl=1, cr=0):
    lefts, rights = [], []
    for left, right in pairs:
        if left.dtype == BF and right.dtype == BF:
            lefts += [left]
            rights += [right]
        elif left.dtype == BF:
            lefts += [left, left]
            rights += halves(right)
        elif right.dtype == BF:
            lefts += halves(left)
            rights += [right, right]
        else:
            lh, ll = halves(left)
            rh, rl = halves(right)
            lefts += [lh, lh, ll]
            rights += [rh, rl, rh]
    return dg(jnp.concatenate(lefts, axis=cl), jnp.concatenate(rights, axis=cr), cl, cr)


def mm(left, right, cl=1, cr=0):
    return joined([(left, right)], cl, cr)


def ml(left, right, cl=1, cr=0):
    return dg(left.astype(BF), right.astype(BF), cl, cr)


def seg_at(position, ends):
    seg = (position >= ends[0]).astype(jnp.int32)
    for end in ends[1:]:
        seg = seg + (position >= end).astype(jnp.int32)
    return seg


def seq_ends(len_ref):
    ends = [len_ref[0, 0]]
    for index in range(1, len_ref.shape[1] - 1):
        ends.append(ends[-1] + len_ref[0, index])
    return ends


def shifted_mask(rows, width, shift, ends):
    here = lax.broadcasted_iota(jnp.int32, (rows, width), 0)
    back = here - shift
    return (back >= 0) & (seg_at(here, ends) == seg_at(back, ends))


def tile_iota():
    row = lax.broadcasted_iota(jnp.int32, (CHUNK, CHUNK), 0)
    col = lax.broadcasted_iota(jnp.int32, (CHUNK, CHUNK), 1)
    return row, col


def forward_kernel(x_count, w_count, *refs):
    deal_ref, spot_ref, slot_ref, len_ref = refs[:4]
    here_ref, refs = refs[4], refs[5:]
    x_refs, refs = refs[:x_count], refs[x_count:]
    gain_ref, refs = refs[0], refs[1:]
    w_refs, refs = refs[:w_count], refs[w_count:]
    taps_ref, o_ref, refs = refs[0], refs[1], refs[2:]
    kept, refs = refs[:SAVED], refs[SAVED:]
    held, (proj_ref, score_ref, sems) = refs[:SAVED], refs[SAVED:]
    (
        w_ref, wb_ref, h1_ref, q_ref, k_ref, v_ref, house_ref, raw_ref, logit_ref, prob_ref,
        u_ref, kt_ref, tr_ref, tinv_ref, xq_ref, yk_ref, z_ref,
    ) = held
    depth = here_ref.shape[1]
    pieces = deal_ref.shape[1]
    small = h1_ref.shape[0] // spot_ref.shape[1]
    rows = h1_ref.shape[0]
    piece = rows // pieces
    chunks = rows // CHUNK
    width = o_ref.shape[1]
    share = depth // w_count
    scale = width ** (-0.5)
    ends = seq_ends(len_ref)
    gain = gain_ref[...].astype(F32)

    def keep(first, last):
        for index in range(first, last):
            pltpu.make_async_copy(held[index], kept[index], sems.at[index]).start()

    pick = jnp.where(
        (lax.broadcasted_iota(jnp.int32, (16, width), 0) == 0)
        & (lax.broadcasted_iota(jnp.int32, (16, width), 1) == 0),
        1.0,
        0.0,
    ).astype(BF)
    for index, ref in enumerate(w_refs):
        base = pl.multiple_of(slot_ref[0, index] * share, share)
        w_ref[pl.ds(base, share), :] = ref[:share, :]
        wb_ref[pl.ds(base, share), :] = dg(ref[share:, :share], pick, 0, 0).astype(BF)

    def settle(x, index):
        x = x.astype(F32)
        inv = lax.rsqrt(jnp.mean(x * x, axis=1, keepdims=True) + EPS)
        base = pl.multiple_of(spot_ref[0, index] * small, small)
        h1_ref[pl.ds(base, small), :] = (x * inv * gain).astype(BF)

    local_count = here_ref.shape[0] // small
    for index in range(local_count):
        settle(here_ref[index * small:(index + 1) * small, :], index)
    for ref in x_refs:
        for index in range(ref.shape[0] // small):
            settle(ref[index * small:(index + 1) * small, :], local_count + index)
        local_count += ref.shape[0] // small
    keep(0, 3)

    for step in range(4):
        at = slice(step * width, (step + 1) * width)
        proj_ref[:, at] = dg(h1_ref[...], w_ref[:, at], 1, 0)
    logit_ref[...] = dg(h1_ref[...], wb_ref[...], 1, 0)
    q_ref[...] = proj_ref[:, :width].astype(BF)
    k_ref[...] = proj_ref[:, width:2 * width].astype(BF)
    v_ref[...] = proj_ref[:, 2 * width:3 * width].astype(BF)
    raw = proj_ref[:, 3 * width:4 * width]
    raw_ref[...] = raw
    taps = taps_ref[...].astype(F32)
    mixed = taps[0:1, :] * raw
    for shift in range(1, taps.shape[0]):
        moved = pltpu.roll(raw, shift, 0)
        mixed = mixed + taps[shift:shift + 1, :] * jnp.where(
            shifted_mask(rows, width, shift, ends), moved, 0.0
        )
    unit = mixed * lax.rsqrt(jnp.sum(mixed * mixed, axis=1, keepdims=True) + EPS)
    house_ref[...] = unit.astype(BF)
    keep(3, 9)

    row, col = tile_iota()
    strict = row > col
    eye = jnp.where(row == col, 1.0, 0.0)
    spans = [slice(n * CHUNK, (n + 1) * CHUNK) for n in range(chunks)]
    strength = [2.0 * jax.nn.sigmoid(logit_ref[s, 0:1]) for s in spans]
    system = []
    for n, s in enumerate(spans):
        house = house_ref[s, :]
        system.append(jnp.where(strict, strength[n] * dg(house, house, 1, 1), 0.0))
    inverse = [eye - jnp.where((row ^ col) == 1, a, 0.0) for a in system]
    level = 1
    while (1 << level) < CHUNK:
        block = ((row ^ col) >> level) == 1
        inner = [mm(jnp.where(block, a, 0.0), t) for a, t in zip(system, inverse)]
        inverse = [t - mm(t, i) for t, i in zip(inverse, inner)]
        level += 1
    for n, s in enumerate(spans):
        query, key, house = q_ref[s, :], k_ref[s, :], house_ref[s, :]
        tinv = inverse[n]
        tinv_ref[s, :] = tinv
        across = jnp.transpose(jnp.broadcast_to(strength[n], (CHUNK, CHUNK)))
        merged = tinv * across
        a_qw = jnp.where(row >= col, dg(query, house, 1, 1), 0.0)
        a_wk = jnp.where(strict, dg(house, key, 1, 1), 0.0)
        xq = mm(a_qw, merged)
        yk = mm(merged, a_wk)
        zz = mm(merged, house)
        xq_ref[s, :] = xq
        yk_ref[s, :] = yk
        z_ref[s, :] = zz
        score_ref[s, s] = (dg(query, key, 1, 1) - mm(xq, a_wk)) * scale
        proj_ref[s, :width] = query.astype(F32) - mm(xq, house)
        kt_ref[s, :] = key.astype(F32) - mm(yk, house, 0, 0)
        tr_ref[s, :] = eye - mm(house, zz, 0, 0)
    keep(11, SAVED)
    offset = 0
    for n in range(chunks - 2, -1, -1):
        later = slice((n + 1) * CHUNK, rows)
        count = rows - (n + 1) * CHUNK
        carried = proj_ref[later, :width]
        u_ref[offset:offset + count, :] = carried
        offset += count
        score_ref[later, spans[n]] = mm(carried, kt_ref[spans[n], :], 1, 1) * scale
        if n > 0:
            proj_ref[later, :width] = mm(carried, tr_ref[spans[n], :])
    keep(10, 11)
    for m, s in enumerate(spans):
        reach = (m + 1) * CHUNK
        at_row = lax.broadcasted_iota(jnp.int32, (CHUNK, reach), 0) + m * CHUNK
        at_col = lax.broadcasted_iota(jnp.int32, (CHUNK, reach), 1)
        seen = (at_row >= at_col) & (seg_at(at_row, ends) == seg_at(at_col, ends))
        logits = jnp.where(seen, score_ref[s, :reach], NEG)
        top = jnp.max(logits, axis=1, keepdims=True)
        grown = jnp.exp(logits - top)
        prob = grown / jnp.sum(grown, axis=1, keepdims=True)
        prob_ref[s, :reach] = prob
        proj_ref[s, :width] = dg(prob.astype(BF), v_ref[:reach, :], 1, 0)

    def give(step, carry):
        base = pl.multiple_of(step * piece, piece)
        given = pl.multiple_of(deal_ref[0, step] * piece, piece)
        o_ref[pl.ds(given, piece), :] = proj_ref[pl.ds(base, piece), :width].astype(BF)
        return carry

    keep(9, 10)
    lax.fori_loop(0, pieces, give, 0)
    for index in range(SAVED):
        pltpu.make_async_copy(held[index], kept[index], sems.at[index]).wait()


def backward_kernel(*refs):
    deal_ref, place_ref, source_ref, from_ref, len_ref, live_ref = refs[:6]
    ranks = from_ref.shape[1]
    parts, taps_ref, refs = refs[6:6 + ranks], refs[6 + ranks], refs[7 + ranks:]
    kept, refs = refs[:SAVED], refs[SAVED:]
    (near_ref, far_ref, dproj_ref, small_ref, dtaps_ref), refs = refs[:5], refs[5:]
    held, refs = refs[:SAVED], refs[SAVED:]
    ds_ref, dout_ref, du_ref, dkt_ref, dtr_ref, dhouse_ref, do_ref, sems = refs
    (
        w_ref, wb_ref, h1_ref, q_ref, k_ref, v_ref, house_ref, raw_ref, logit_ref, prob_ref,
        u_ref, kt_ref, tr_ref, tinv_ref, xq_ref, yk_ref, z_ref,
    ) = held

    def fetch(index):
        return pltpu.make_async_copy(kept[index], held[index], sems.at[index])

    needed = (5, 9), (10, 11, 12), (3, 4, 6, 8, 13, 14, 15, 16), (7,), (0, 1, 2)
    for index in sum(needed, ()):
        fetch(index).start()
    for k, ref in enumerate(parts):
        span = ref.shape[0]
        do_ref[pl.ds(pl.multiple_of(from_ref[0, k] * span, span), span), :] = ref[...]

    def ready(stage):
        for index in needed[stage]:
            fetch(index).wait()

    rows = do_ref.shape[0]
    pieces = deal_ref.shape[1]
    piece = rows // pieces
    small = rows // place_ref.shape[1]
    chunks = rows // CHUNK
    width = do_ref.shape[1]
    scale = width ** (-0.5)
    ends = seq_ends(len_ref)
    spans = [slice(n * CHUNK, (n + 1) * CHUNK) for n in range(chunks)]
    row, col = tile_iota()
    strict = row > col

    def take(step, carry):
        base = pl.multiple_of(step * piece, piece)
        for part in range(piece // small):
            there = source_ref[0, deal_ref[0, step] * (piece // small) + part]
            dout_ref[pl.ds(base + part * small, small), :] = do_ref[
                pl.ds(pl.multiple_of(there * small, small), small), :
            ]
        return carry

    lax.fori_loop(0, pieces, take, 0)
    ready(0)
    for m, s in enumerate(spans):
        reach = (m + 1) * CHUNK
        prob = prob_ref[s, :reach]
        dprob = dg(dout_ref[s, :], v_ref[:reach, :], 1, 1)
        dot = jnp.sum(prob * dprob, axis=1, keepdims=True)
        ds_ref[s, :reach] = prob * (dprob - dot) * scale
    for n, s in enumerate(spans):
        dproj_ref[s, 2 * width:3 * width] = dg(
            prob_ref[n * CHUNK:, s].astype(BF), dout_ref[n * CHUNK:, :], 0, 0
        ).astype(BF)
    starts = {}
    offset = 0
    for n in range(chunks - 2, -1, -1):
        starts[n] = offset
        offset += rows - (n + 1) * CHUNK
    ready(1)
    for n in range(chunks - 1):
        later = slice((n + 1) * CHUNK, rows)
        count = rows - (n + 1) * CHUNK
        grad = ds_ref[later, spans[n]]
        carried = u_ref[starts[n]:starts[n] + count, :]
        dkt_ref[spans[n], :] = mm(grad, carried, 0, 0)
        fresh = mm(grad, kt_ref[spans[n], :])
        if n > 0:
            before = du_ref[later, :]
            dtr_ref[spans[n], :] = mm(carried, before, 0, 0)
            fresh = fresh + mm(before, tr_ref[spans[n], :], 1, 1)
        du_ref[later, :] = fresh
    ready(2)
    for n, s in enumerate(spans):
        query, key, house = q_ref[s, :], k_ref[s, :], house_ref[s, :]
        strength = 2.0 * jax.nn.sigmoid(logit_ref[s, 0:1])
        tinv = tinv_ref[s, :]
        merged = tinv * jnp.transpose(jnp.broadcast_to(strength, (CHUNK, CHUNK)))
        a_qw = jnp.where(row >= col, dg(query, house, 1, 1), 0.0)
        a_wk = jnp.where(strict, dg(house, key, 1, 1), 0.0)
        gram = jnp.where(strict, dg(house, house, 1, 1), 0.0)
        xq, yk, zz = xq_ref[s, :], yk_ref[s, :], z_ref[s, :]
        di = ds_ref[s, s]
        first, final = n == 0, n == chunks - 1
        if first:
            dxq = mm(di, a_wk, 1, 1)
            da_qw = mm(di, yk, 1, 1)
        else:
            dqt = du_ref[s, :]
            dxq = joined([(di, a_wk), (dqt, house)], 1, 1)
            da_qw = joined([(di, yk), (dqt, zz)], 1, 1)
        da_qw = jnp.where(row >= col, da_qw, 0.0)
        dm = mm(a_qw, dxq, 0, 0)
        cross = [(xq, di)]
        if not final:
            dkt = dkt_ref[s, :]
            dyk = mm(house, dkt, 1, 1)
            cross.append((merged, dyk))
            outer = [(dyk, a_wk)]
            if not first:
                dtr = dtr_ref[s, :]
                wd = mm(house, dtr)
                outer.append((wd, house))
            dm = dm + joined(outer, 1, 1)
        da_wk = jnp.where(strict, joined(cross, 0, 0), 0.0)
        ee = mm(tinv, dm, 0, 0)
        rest = jnp.where(row == col, 1.0, 0.0) - mm(gram, merged)
        dstrength = -jnp.sum(ee * rest, axis=1, keepdims=True)
        dgram = jnp.where(strict, mm(strength * ee, merged, 1, 1), 0.0)
        dq = joined([(di, key), (-da_qw, house)])
        dk = joined([(di, query), (-da_wk, house)], 0, 0)
        tall = [(da_qw, query), (-dgram, house)]
        wide = [(da_wk, key), (-dgram, house)]
        if not first:
            dq = dq + dqt
            tall.append((xq, dqt))
        if not final:
            dk = dk + dkt
            wide.append((yk, dkt))
            if not first:
                tall.append((merged, wd))
        dw = joined(tall, 0, 0) + joined(wide)
        if not first and not final:
            dw = dw + mm(zz, dtr, 1, 1)
        dw = -dw
        dproj_ref[s, :width] = dq.astype(BF)
        dproj_ref[s, width:2 * width] = dk.astype(BF)
        dhouse_ref[s, :] = dw
        gate = 0.5 * strength
        dlogit = dstrength * 2.0 * gate * (1.0 - gate)
        lane = lax.broadcasted_iota(jnp.int32, (CHUNK, width), 1)
        dproj_ref[s, 4 * width:] = jnp.where(lane == 0, dlogit, 0.0).astype(BF)
    ready(3)
    raw = raw_ref[...]
    taps = taps_ref[...].astype(F32)
    count = taps.shape[0]
    mixed = taps[0:1, :] * raw
    earlier = [raw]
    masks = [None]
    for shift in range(1, count):
        masks.append(shifted_mask(rows, width, shift, ends))
        earlier.append(jnp.where(masks[shift], pltpu.roll(raw, shift, 0), 0.0))
        mixed = mixed + taps[shift:shift + 1, :] * earlier[shift]
    inv = lax.rsqrt(jnp.sum(mixed * mixed, axis=1, keepdims=True) + EPS)
    dunit = dhouse_ref[...]
    dmixed = inv * dunit - mixed * (
        inv * inv * inv * jnp.sum(dunit * mixed, axis=1, keepdims=True)
    )
    live = live_ref[0, 0].astype(F32)
    draw = taps[0:1, :] * dmixed
    dtaps_ref[0:1, :] = jnp.sum(dmixed * raw, axis=0, keepdims=True) * live
    for shift in range(1, count):
        dtaps_ref[shift:shift + 1, :] = (
            jnp.sum(dmixed * earlier[shift], axis=0, keepdims=True) * live
        )
        later = jnp.where(masks[shift], dmixed, 0.0)
        draw = draw + taps[shift:shift + 1, :] * pltpu.roll(later, rows - shift, 0)
    dproj_ref[:, 3 * width:4 * width] = draw.astype(BF)

    ready(4)

    small_ref[...] = jnp.zeros_like(small_ref)
    count = near_ref.shape[0] // small
    tile = 256

    def send(step, carry):
        at = pl.ds(pl.multiple_of(step * tile, tile), tile)
        dh1 = dg(dproj_ref[:, :4 * width], w_ref[at, :], 1, 1)
        dh1 = (dh1 + dg(dproj_ref[:, 4 * width:], wb_ref[at, :], 1, 1)) * live
        small_ref[0:1, at] = jnp.sum(dh1 * h1_ref[:, at].astype(F32), axis=0, keepdims=True)
        for block in range(rows // small):
            given = deal_ref[0, block * small // piece] * (piece // small)
            there = place_ref[0, given + block % (piece // small)]
            values = dh1[block * small:(block + 1) * small]

            @pl.when(there < count)
            def _():
                near_ref[pl.ds(pl.multiple_of(there * small, small), small), at] = values

            @pl.when(there >= count)
            def _():
                to = pl.ds(pl.multiple_of((there - count) * small, small), small)
                far_ref[to, at] = values.astype(BF)

        return carry

    lax.fori_loop(0, h1_ref.shape[1] // tile, send, 0)
    beta = dg(dproj_ref[:, 4 * width:], h1_ref[...], 0, 0)
    small_ref[1:2, :] = beta[0:1, :] * live


SAVED = 17


def saved_shapes(rows, depth, width):
    chunks = rows // CHUNK
    carried = CHUNK * chunks * (chunks - 1) // 2
    slim = ((rows, width), BF)
    tall = ((rows, width), F32)
    return (
        ((depth, 4 * width), BF), ((depth, width), BF), ((rows, depth), BF), slim, slim, slim, slim,
        tall, tall, ((rows, rows), F32), ((carried, width), F32), tall, tall, tall, tall, tall, tall,
    )


VMEM = pl.BlockSpec(memory_space=pltpu.VMEM)
SMEM = pl.BlockSpec(memory_space=pltpu.SMEM)
AWAY = pl.BlockSpec(memory_space=pl.ANY)
LIMIT = pltpu.CompilerParams(vmem_limit_bytes=56 * 1024 * 1024)


def attend_forward(deal, spot, slot, lengths, here, x_parts, gain, w_parts, taps):
    depth = here.shape[1]
    rows = here.shape[0] + sum(part_.shape[0] for part_ in x_parts)
    width = taps.shape[1]
    saved = saved_shapes(rows, depth, width)
    return pl.pallas_call(
        functools.partial(forward_kernel, len(x_parts), len(w_parts)),
        out_shape=(jax.ShapeDtypeStruct((rows, width), BF),)
        + tuple(jax.ShapeDtypeStruct(*entry) for entry in saved),
        in_specs=[SMEM] * 4 + [VMEM] * (len(x_parts) + len(w_parts) + 3),
        out_specs=(VMEM,) + (AWAY,) * SAVED,
        scratch_shapes=[pltpu.VMEM(*entry) for entry in saved]
        + [
            pltpu.VMEM((rows, 4 * width), F32),
            pltpu.VMEM((rows, rows), F32),
            pltpu.SemaphoreType.DMA((SAVED,)),
        ],
        compiler_params=LIMIT,
        cost_estimate=pl.CostEstimate(flops=16 * 10**9, bytes_accessed=10**7, transcendentals=0),
        name="attend_forward",
    )(deal, spot, slot, lengths, here, *x_parts, gain, *w_parts, taps)


def attend_backward(deal, place, source, origin, lengths, live, d_out, taps, depth, kept):
    rows, width = d_out[0].shape[0] * len(d_out), d_out[0].shape[1]
    saved = saved_shapes(rows, depth, width)
    return pl.pallas_call(
        backward_kernel,
        out_shape=(
            jax.ShapeDtypeStruct((rows // 2, depth), F32),
            jax.ShapeDtypeStruct((rows // 2, depth), BF),
            jax.ShapeDtypeStruct((rows, 5 * width), BF),
            jax.ShapeDtypeStruct((8, depth), F32),
            jax.ShapeDtypeStruct((taps.shape[0], width), F32),
        ),
        in_specs=[SMEM] * 6 + [VMEM] * (len(d_out) + 1) + [AWAY] * SAVED,
        out_specs=(VMEM,) * 5,
        scratch_shapes=[pltpu.VMEM(*entry) for entry in saved]
        + [
            pltpu.VMEM((rows, rows), F32),
            pltpu.VMEM((rows, width), BF),
            pltpu.VMEM((rows, width), F32),
            pltpu.VMEM((rows, width), F32),
            pltpu.VMEM((rows, width), F32),
            pltpu.VMEM((rows, width), F32),
            pltpu.VMEM((rows, width), BF),
            pltpu.SemaphoreType.DMA((SAVED,)),
        ],
        compiler_params=LIMIT,
        cost_estimate=pl.CostEstimate(flops=20 * 10**9, bytes_accessed=10**7, transcendentals=0),
        name="attend_backward",
    )(deal, place, source, origin, lengths, live, *d_out, taps, *kept)


def head_kernel(head_ref, left_ref, right_ref, *outs):
    width = outs[0].shape[1]
    every = dg(left_ref[...], right_ref[...], 1, 0).astype(BF)
    for k, out in enumerate(outs):
        for head in range(right_ref.shape[1] // width):

            @pl.when(head_ref[0, k] == head)
            def _():
                out[...] = every[:, head * width:(head + 1) * width]


def by_head(head, left, right, width):
    ranks = head.shape[1]
    return pl.pallas_call(
        head_kernel,
        out_shape=(jax.ShapeDtypeStruct((left.shape[0], width), BF),) * ranks,
        in_specs=[SMEM, VMEM, VMEM],
        out_specs=(VMEM,) * ranks,
        compiler_params=LIMIT,
        cost_estimate=pl.CostEstimate(flops=3 * 10**9, bytes_accessed=10**6, transcendentals=0),
        name="by_head",
    )(head, left, right)


def pack_kernel(heads, ranks, shards, *refs):
    head_ref, order_ref = refs[:2]
    projections = refs[2:6]
    beta_ref, gate_ref, up_ref, down_ref = refs[6:10]
    blocks, parts = refs[10:10 + ranks], refs[10 + ranks:]
    share, columns = projections[0].shape
    width = columns // heads
    part = gate_ref.shape[1] // shards
    beta = beta_ref[...].astype(F32)
    for k, block in enumerate(blocks):
        head = head_ref[0, k]
        at = pl.multiple_of(head * width, width)
        for index, ref in enumerate(projections):
            block[:share, index * width:(index + 1) * width] = ref[:, pl.ds(at, width)]
        row = beta[0:1, :]
        for other in range(1, heads):
            row = jnp.where(head == other, beta[other:other + 1, :], row)
        block[share:, :] = jnp.zeros((block.shape[0] - share, block.shape[1]), BF)
        block[share:, :share] = jnp.broadcast_to(row, (block.shape[0] - share, share)).astype(BF)
    for index, ref in enumerate(parts):
        at = pl.multiple_of(order_ref[0, index] * part, part)
        ref[:, :part] = gate_ref[:, pl.ds(at, part)]
        ref[:, part:2 * part] = up_ref[:, pl.ds(at, part)]
        ref[:, 2 * part:] = down_ref[:, pl.ds(at, part)]


def pack(head, order, projections, w_beta, w_gate, w_up, w_down, ranks):
    share, columns = projections[0].shape
    heads = w_beta.shape[0]
    shards = order.shape[1]
    width = columns // heads
    part = w_gate.shape[1] // shards
    out = pl.pallas_call(
        functools.partial(pack_kernel, heads, ranks, shards),
        out_shape=(jax.ShapeDtypeStruct((share + 16, 4 * width), BF),) * ranks
        + (jax.ShapeDtypeStruct((share, 3 * part), BF),) * shards,
        in_specs=[SMEM, SMEM] + [VMEM] * 8,
        out_specs=(VMEM,) * (ranks + shards),
        compiler_params=LIMIT,
        cost_estimate=pl.CostEstimate(flops=3 * 10**9, bytes_accessed=10**6, transcendentals=0),
        name="pack",
    )(head, order, *projections, w_beta, w_gate, w_up, w_down)
    return list(out[:ranks]), list(out[ranks:])


def unpack_hidden_kernel(shards, *refs):
    order_ref, blocks = refs[0], refs[1:1 + shards]
    gate_ref, up_ref, down_ref = refs[1 + shards:]
    part = blocks[0].shape[1] // 3
    for index, block in enumerate(blocks):
        at = pl.multiple_of(order_ref[0, index] * part, part)
        gate_ref[:, pl.ds(at, part)] = block[:, :part].astype(F32)
        up_ref[:, pl.ds(at, part)] = block[:, part:2 * part].astype(F32)
        down_ref[:, pl.ds(at, part)] = block[:, 2 * part:].astype(F32)


def unpack_hidden(order, blocks):
    shards = len(blocks)
    share, part = blocks[0].shape[0], blocks[0].shape[1] // 3
    wide = jax.ShapeDtypeStruct((share, shards * part), F32)
    return pl.pallas_call(
        functools.partial(unpack_hidden_kernel, shards),
        out_shape=(wide,) * 3,
        in_specs=[SMEM] + [VMEM] * shards,
        out_specs=(VMEM,) * 3,
        compiler_params=LIMIT,
        cost_estimate=pl.CostEstimate(flops=2 * 10**9, bytes_accessed=10**6, transcendentals=0),
        name="unpack_hidden",
    )(order, *blocks)


def merge_kernel(order_ref, o_ref, w_ref, rows_ref, near_ref, far_ref):
    span, columns = rows_ref.shape
    width = o_ref.shape[2]
    small = span // order_ref.shape[1]
    for slot in range(order_ref.shape[1]):
        at = pl.multiple_of(order_ref[0, slot] * small, small)
        for head in range(columns // width):
            rows_ref[slot * small:(slot + 1) * small, head * width:(head + 1) * width] = o_ref[
                head, pl.ds(at, small), :
            ]
    total = dg(rows_ref[...], w_ref[...], 1, 1)
    near_ref[...] = total[:span // 2]
    far_ref[...] = total[span // 2:].astype(BF)


def merge_heads(order, head_rows, w_out, heads):
    span, width = head_rows.shape[1:]
    depth = w_out.shape[0]
    return pl.pallas_call(
        merge_kernel,
        out_shape=(
            jax.ShapeDtypeStruct((span, heads * width), BF),
            jax.ShapeDtypeStruct((span // 2, depth), F32),
            jax.ShapeDtypeStruct((span // 2, depth), BF),
        ),
        in_specs=[SMEM, VMEM, VMEM],
        out_specs=(VMEM,) * 3,
        compiler_params=LIMIT,
        cost_estimate=pl.CostEstimate(flops=3 * 10**9, bytes_accessed=10**6, transcendentals=0),
        name="merge_heads",
    )(order, head_rows, w_out)


def hidden_kernel(
    near_ref, far_ref, grad_ref, w_ref, h2_ref, act_ref, pair_ref,
    d_near_ref, d_far_ref, m_near_ref, m_far_ref,
):
    half = near_ref.shape[0]
    part = act_ref.shape[1]
    tile = min(part, 256)
    h2_ref[:half, :] = near_ref[...]
    h2_ref[half:, :] = far_ref[...]
    for start in range(0, part, tile):
        gate = dg(h2_ref[...], w_ref[:, start:start + tile], 1, 0)
        up = dg(h2_ref[...], w_ref[:, part + start:part + start + tile], 1, 0)
        d_act = dg(grad_ref[...], w_ref[:, 2 * part + start:2 * part + start + tile], 1, 0)
        sig = jax.nn.sigmoid(gate)
        swish = gate * sig
        act_ref[:, start:start + tile] = (swish * up).astype(BF)
        pair_ref[:, start:start + tile] = (
            d_act * up * sig * (1.0 + gate * (1.0 - sig))
        ).astype(BF)
        pair_ref[:, part + start:part + start + tile] = (d_act * swish).astype(BF)
    d_far_ref[...] = dg(pair_ref[half:, :], w_ref[:, :2 * part], 1, 1).astype(BF)
    d_near_ref[...] = dg(pair_ref[:half, :], w_ref[:, :2 * part], 1, 1)
    m_far_ref[...] = dg(act_ref[half:, :], w_ref[:, 2 * part:], 1, 1).astype(BF)
    m_near_ref[...] = dg(act_ref[:half, :], w_ref[:, 2 * part:], 1, 1)


def hidden_pass(near, far, grad, weights):
    half, depth = near.shape
    part = weights.shape[1] // 3
    keep = jax.ShapeDtypeStruct((half, depth), F32)
    sent = jax.ShapeDtypeStruct((half, depth), BF)
    return pl.pallas_call(
        hidden_kernel,
        out_shape=(
            jax.ShapeDtypeStruct((2 * half, depth), BF),
            jax.ShapeDtypeStruct((2 * half, part), BF),
            jax.ShapeDtypeStruct((2 * half, 2 * part), BF),
            keep, sent, keep, sent,
        ),
        in_specs=[VMEM] * 4,
        out_specs=(VMEM,) * 7,
        compiler_params=LIMIT,
        cost_estimate=pl.CostEstimate(flops=9 * 10**9, bytes_accessed=10**6, transcendentals=0),
        name="hidden_pass",
    )(near, far, grad, weights)


def hidden_grad_kernel(h2_ref, grad_ref, act_ref, pair_ref, out_ref, turned_ref):
    depth, part = out_ref.shape[0], act_ref.shape[1]
    tile = min(part, 256)
    for source, value, start in ((h2_ref, pair_ref, 0), (grad_ref, act_ref, 2 * part)):
        for at in range(0, depth, 256):
            turned_ref[at:at + 256, :] = source[:, at:at + 256].astype(F32).T.astype(BF)
        for at in range(0, value.shape[1], tile):
            out_ref[:, start + at:start + at + tile] = dg(
                turned_ref[...], value[:, at:at + tile], 1, 0
            ).astype(BF)


def hidden_grad(h2, grad, act, pair):
    depth, part = h2.shape[1], act.shape[1]
    return pl.pallas_call(
        hidden_grad_kernel,
        out_shape=jax.ShapeDtypeStruct((depth, 3 * part), BF),
        in_specs=[VMEM] * 4,
        out_specs=VMEM,
        scratch_shapes=[pltpu.VMEM((depth, h2.shape[0]), BF)],
        compiler_params=LIMIT,
        cost_estimate=pl.CostEstimate(flops=8 * 10**9, bytes_accessed=10**6, transcendentals=0),
        name="hidden_grad",
    )(h2, grad, act, pair)


def unpack_heads_kernel(ranks, heads, *refs):
    source_ref, blocks, grads = refs[0], refs[1:1 + ranks], refs[1 + ranks:]
    width = blocks[0].shape[1] // len(grads)
    for k, block in enumerate(blocks):
        source = source_ref[0, k]

        @pl.when(source < heads)
        def _():
            at = pl.multiple_of(source * width, width)
            for index, ref in enumerate(grads):
                ref[:, pl.ds(at, width)] = block[:, index * width:(index + 1) * width].astype(F32)


def unpack_heads(source, blocks, heads):
    ranks = len(blocks)
    share, columns = blocks[0].shape[0], blocks[0].shape[1] // 4 * heads
    return pl.pallas_call(
        functools.partial(unpack_heads_kernel, ranks, heads),
        out_shape=(jax.ShapeDtypeStruct((share, columns), F32),) * 4,
        in_specs=[SMEM] + [VMEM] * ranks,
        out_specs=(VMEM,) * 4,
        compiler_params=LIMIT,
        cost_estimate=pl.CostEstimate(flops=2 * 10**9, bytes_accessed=10**6, transcendentals=0),
        name="unpack_heads",
    )(source, *blocks)


def steps_of(axis, descending):
    size = lax.axis_size(axis)
    bits = []
    bit = 1
    while bit < size:
        bits.append((axis, bit))
        bit *= 2
    return bits[::-1] if descending else bits


def swap(value, axis, bit):
    size = lax.axis_size(axis)
    return lax.ppermute(value, axis, [(i, i ^ bit) for i in range(size)])


def spread_rows(value, steps):
    for axis, bit in steps:
        value = jnp.concatenate([value, swap(value, axis, bit)], axis=0)
    return value


def gather_rows(value, steps):
    for axis, bit in steps[::-1]:
        half = value.shape[0] // 2
        value = value[:half] + swap(value[half:].astype(BF), axis, bit).astype(F32)
    return value


def fold(kept, got, steps):
    for axis, bit in steps[::-1]:
        half = kept.shape[0] // 2
        sent = (kept[half:] + got[half:].astype(F32)).astype(BF)
        kept, got = kept[:half] + got[:half].astype(F32), swap(sent, axis, bit)
    return kept + got.astype(F32)


def in_order(mine, other):
    first = lax.axis_index("shard") == 0
    return jnp.stack([jnp.where(first, mine, other), jnp.where(first, other, mine)])


def over_shard(value):
    if lax.axis_size("shard") == 2:
        return in_order(value, swap(value, "shard", 1))
    return lax.all_gather(value, "shard", axis=0, tiled=False)


def across_shard(parts):
    if lax.axis_size("shard") == 2:
        shard = lax.axis_index("shard")
        mine = lax.dynamic_index_in_dim(parts, shard, axis=0, keepdims=False)
        sent = lax.dynamic_index_in_dim(parts, 1 - shard, axis=0, keepdims=False)
        return in_order(mine, swap(sent, "shard", 1))
    return deal_out(parts, "shard")


def sum_shard(parts):
    if lax.axis_size("shard") == 2:
        shard = lax.axis_index("shard")
        mine = lax.dynamic_index_in_dim(parts, shard, axis=0, keepdims=False)
        sent = lax.dynamic_index_in_dim(parts, 1 - shard, axis=0, keepdims=False)
        return mine.astype(F32) + swap(sent, "shard", 1).astype(F32)
    return jnp.sum(deal_out(parts, "shard").astype(F32), axis=0)


def over_ctx(value):
    ranks = lax.axis_size("ctx")
    got = [value] + [
        lax.ppermute(value, "ctx", [(i, (i + k) % ranks) for i in range(ranks)])
        for k in range(1, ranks)
    ]
    return got


def sum_over(value, steps):
    for axis, bit in steps:
        value = value + swap(value, axis, bit)
    return value


def deal_out(value, axis):
    return lax.all_to_all(value, axis, split_axis=0, concat_axis=0, tiled=True)


def norm_back(value, inverse, gain, grad):
    scaled = grad * gain
    return inverse * scaled - value * inverse**3 * jnp.mean(scaled * value, axis=1, keepdims=True)


def local(
    tokens, cotangent, valid_mask, lengths, deal, attn_gain,
    w_query, w_key, w_value, w_house, w_beta, conv_taps, w_out,
    mlp_gain, w_gate, w_up, w_down,
):
    shards, ranks, lanes = (lax.axis_size(a) for a in ("shard", "ctx", "tp"))
    shard, rank, lane = (lax.axis_index(a) for a in ("shard", "ctx", "tp"))
    span, depth = tokens.shape
    share, columns = w_query.shape
    heads = w_beta.shape[1]
    width = columns // heads
    piece = span // 2
    group = ranks * span
    small = span // lanes
    part = w_gate.shape[1] // shards
    spare = ranks - heads
    tp_steps = steps_of("tp", True)
    plane_steps = steps_of("shard", False) + tp_steps
    live = (rank < heads).astype(jnp.int32).reshape(1, 1)
    head_at = jnp.minimum(rank, heads - 1)

    shifted = over_ctx(lax.dynamic_slice_in_dim(tokens, lane * small, small, axis=0))[1:]

    turn = jnp.arange(ranks, dtype=jnp.int32)
    order_s = jnp.arange(shards, dtype=jnp.int32)
    if shards == 2:
        order_s = order_s ^ shard
    head_of = jnp.minimum((rank + turn) % ranks, heads - 1)[None]
    blocks, hidden = pack(
        head_of, order_s[None],
        (w_query, w_key, w_value, w_house), w_beta.T, w_gate, w_up, w_down.T, ranks,
    )
    crossed = [blocks[0]]
    for k in range(1, ranks):
        pairs = [(i, (i + k) % ranks) for i in range(ranks) if (i + k) % ranks < heads]
        crossed.append(lax.ppermute(blocks[k], "ctx", pairs))
    slots_of = []
    taps = lax.dynamic_slice_in_dim(conv_taps, head_at * width, width, axis=1)

    x_parts, apart_of = list(shifted), [0]
    x_parts = [jnp.concatenate(shifted, axis=0)]
    for axis, bit in tp_steps:
        joined_parts = jnp.concatenate(x_parts, axis=0) if len(x_parts) > 1 else x_parts[0]
        x_parts = x_parts + [swap(joined_parts, axis, bit)]
        apart_of = apart_of + [other ^ bit for other in apart_of]
    owners = (rank - jnp.arange(1, ranks, dtype=jnp.int32)) % ranks
    blocks_of = [rank * lanes + jnp.arange(lanes, dtype=jnp.int32)]
    blocks_of += [owners * lanes + (lane ^ apart) for apart in apart_of]
    blocks_of = jnp.concatenate(blocks_of)
    labels = jnp.arange(2 * ranks, dtype=jnp.int32)
    per_piece = lanes // 2
    at_piece = jnp.sum(
        jnp.where(deal[0][None, :] == (blocks_of // per_piece)[:, None], labels[None, :], 0), axis=1
    )
    spot = (at_piece * per_piece + blocks_of % per_piece)[None]
    w_parts = []
    for k, block in enumerate(crossed):
        source = (rank - k) % ranks
        if shards == 2:
            w_parts += [block, swap(block, "shard", 1)]
            slots_of += [shard * ranks + source, (1 - shard) * ranks + source]
        else:
            every = lax.all_gather(block, "shard", axis=0, tiled=False)
            w_parts += [every[i] for i in range(shards)]
            slots_of += [i * ranks + source for i in range(shards)]
    slot = jnp.stack(slots_of)[None]

    wo_t = over_shard(w_out.T).reshape(shards * share, columns)
    wo_t = lax.all_gather(wo_t, "ctx", axis=0, tiled=False)
    wo_t = wo_t.reshape(ranks, shards, share, columns).transpose(1, 0, 2, 3).reshape(depth, columns)
    grad_own = lax.dynamic_slice_in_dim(cotangent, lane * small, small, axis=0)
    hidden, grad_start, _ = lax.optimization_barrier((hidden, grad_own, shifted))
    if shards == 2:
        hidden = [hidden[0], swap(hidden[1], "shard", 1)]
    else:
        hidden = list(deal_out(jnp.stack(hidden), "shard"))
    def to_plane(value):
        value = value.reshape(-1, shards, ranks, share).transpose(0, 2, 1, 3)
        return value.reshape(-1, depth)

    def from_plane(value):
        value = value.reshape(-1, ranks, shards, share).transpose(0, 2, 1, 3)
        return value.reshape(-1, depth)

    def my_rows(value):
        return lax.dynamic_slice_in_dim(value, lane * small, small, axis=0)

    grad_plane = spread_rows(to_plane(grad_start), plane_steps)
    hidden, _, _ = lax.optimization_barrier((hidden, shifted, crossed))
    hidden = in_order(*hidden) if shards == 2 else jnp.stack(hidden)
    hidden = hidden.reshape(shards * share, 3 * part)
    hidden = lax.all_gather(hidden, "ctx", axis=0, tiled=True)
    fwd = attend_forward(deal, spot, slot, lengths, tokens, x_parts, attn_gain[None], w_parts, taps)
    head_out, saved = fwd[0], fwd[1:]
    h1 = saved[2]
    slots = jnp.arange(lanes, dtype=jnp.int32)
    order = jnp.full_like(slots, lane)
    for index, (_, bit) in enumerate(tp_steps):
        order = order ^ jnp.where((slots >> index) % 2 == 1, bit, 0)
    natural = jnp.zeros_like(slots)
    for index, (_, bit) in enumerate(tp_steps):
        natural = natural + jnp.where(((slots ^ lane) & bit) != 0, 1 << index, 0)
    head_out, grad_plane = lax.optimization_barrier((head_out, grad_plane))
    o_all = deal_out(head_out.reshape(ranks, span, width), "ctx")
    o_rows, near, far = merge_heads(order[None], o_all, wo_t, heads)
    attn = fold(near, swap(far, *tp_steps[-1]), tp_steps[:-1])
    x_own = my_rows(tokens).astype(F32)
    middle = x_own + attn
    gain_two = mlp_gain.astype(F32)
    inv_two = lax.rsqrt(jnp.mean(middle * middle, axis=1, keepdims=True) + EPS)
    normed = (middle * inv_two * gain_two).astype(BF)
    near = spread_rows(to_plane(normed), plane_steps[:-1])
    far = swap(near, *tp_steps[-1])

    h2, act, pair, near, far, mlp, m_far = hidden_pass(near, far, grad_plane, hidden)
    far, act, pair = lax.optimization_barrier((swap(far, *tp_steps[-1]), act, pair))
    mlp = mlp + swap(m_far, *tp_steps[-1]).astype(F32)
    middle_steps = plane_steps[len(plane_steps) - len(tp_steps):-1]
    shard_steps = plane_steps[:-len(tp_steps)]
    d_two = fold(near, far, middle_steps)
    hidden_sum = hidden_grad(h2, grad_plane, act, pair)
    d_two, hidden_sum, mlp = lax.optimization_barrier((d_two, hidden_sum, mlp))
    hidden_sum = lax.psum_scatter(hidden_sum, "ctx", scatter_dimension=0, tiled=True)
    d_two = from_plane(gather_rows(d_two, shard_steps))

    def by_shard(grad):
        grad = grad.reshape(shards, share, grad.shape[1])
        if shards == 2:
            mine = lax.dynamic_index_in_dim(grad, shard, axis=0, keepdims=False)
            sent = lax.dynamic_index_in_dim(grad, 1 - shard, axis=0, keepdims=False)
            return [mine, swap(sent, "shard", 1)]
        return list(deal_out(grad, "shard"))

    d_gain_two = jnp.sum(d_two * middle * inv_two, axis=0)
    d_middle = grad_own.astype(F32) + norm_back(middle, inv_two, gain_two, d_two)
    d_attn = spread_rows(d_middle.astype(BF), tp_steps[:-1])
    d_attn = spread_rows(d_attn, tp_steps[-1:])
    d_heads = by_head(head_of, d_attn, wo_t, width)
    d_heads, d_attn, mlp = lax.optimization_barrier((d_heads, d_attn, mlp))
    d_heads = [d_heads[0]] + [
        lax.ppermute(
            d_heads[k], "ctx",
            [(i, (i + k) % ranks) for i in range(ranks) if (i + k) % ranks < heads],
        )
        for k in range(1, ranks)
    ]
    d_wout = dg(d_attn, o_rows, 0, 0).astype(BF)
    d_wout = sum_shard(d_wout.reshape(shards, ranks * share, columns)).astype(BF)
    mlp = gather_rows(mlp, middle_steps)
    d_heads, d_wout, mlp = lax.optimization_barrier((d_heads, d_wout, mlp))

    given = jnp.arange(group // small, dtype=jnp.int32)
    apart = (given % lanes) ^ lane
    turned = jnp.zeros_like(apart)
    for index, (_, bit) in enumerate(tp_steps):
        turned = turned + jnp.where((apart & bit) != 0, 1 << index, 0)
    place = (turned * ranks + given // lanes)[None]
    source = (given // lanes * lanes + turned)[None]
    near, far, d_proj, d_small, d_taps = attend_backward(
        deal, place, source, ((rank - turn) % ranks)[None], lengths, live, d_heads, taps, depth, saved
    )
    gain_one = attn_gain.astype(F32)
    mine = (jnp.arange(heads) == rank).astype(F32)
    taps_part = (mine[None, :, None] * d_taps[:, None]).reshape(conv_taps.shape)
    taps_part = jnp.pad(taps_part, ((0, 0), (0, depth - columns)))
    sum_steps = steps_of("ctx", False) + steps_of("shard", False)

    got = swap(far, *tp_steps[-1])
    mlp = from_plane(gather_rows(mlp, shard_steps))
    for axis, bit in tp_steps[:-1][::-1]:
        count, wide = near.shape[0] // 2, depth // 4
        sent = (near[count:] + got[count:].astype(F32)).astype(BF)
        first, last = swap(sent[:, :wide], axis, bit), swap(sent[:, wide:], axis, bit)
        near = near[:count] + got[:count].astype(F32)
        first, d_proj, mlp, d_wout = lax.optimization_barrier((first, d_proj, mlp, d_wout))

    d_one = jnp.concatenate(
        [near[:, :wide] + first.astype(F32), near[:, wide:] + last.astype(F32)], axis=1
    ).astype(BF).reshape(ranks, small, depth)
    d_w = dg(h1, d_proj[:, :4 * width], 0, 0).astype(BF)
    d_w = sum_shard(d_w.reshape(shards, ranks * share, 4 * width)).astype(BF)
    result = middle + mlp
    mask = my_rows(valid_mask).astype(F32)[:, None]
    branches = [x_own, attn, mlp, result]
    sums = [jnp.sum(mask * b * b, axis=0, keepdims=True) for b in branches]
    sums += [jnp.broadcast_to(jnp.sum(mask, axis=0, keepdims=True), (1, depth))]
    sums += [d_small[:1], d_gain_two[None], mine[:, None] * d_small[1][None], taps_part]
    sums = jnp.concatenate(sums, axis=0)
    def sum_ctx(parts):
        total = lax.dynamic_index_in_dim(parts, rank, axis=0, keepdims=False).astype(F32)
        for k in range(1, ranks):
            sent = lax.dynamic_index_in_dim(parts, (rank + k) % ranks, axis=0, keepdims=False)
            got = lax.ppermute(sent, "ctx", [(i, (i + k) % ranks) for i in range(ranks)])
            total = total + got.astype(F32)
        return total

    d_wout = sum_ctx(d_wout.reshape(ranks, share, columns)).T
    d_one, sums, result = lax.optimization_barrier((d_one, sums, result))
    total = sum_ctx(d_one)
    sums = sum_over(sums, sum_steps[:2])
    hidden_parts = by_shard(hidden_sum)
    d_one, result, sums, d_w, hidden_parts, d_wout = lax.optimization_barrier(
        (total, result, sums, d_w, hidden_parts, d_wout)
    )
    sums = sum_over(sums, sum_steps[2:])
    every = sum_over(sums[:7], tp_steps)

    d_w = d_w.reshape(ranks, share, 4 * width)
    w_blocks = [lax.dynamic_index_in_dim(d_w, rank, axis=0, keepdims=False)]
    for k in range(1, ranks):
        sent = lax.dynamic_index_in_dim(d_w, (rank + k) % ranks, axis=0, keepdims=False)
        pairs_k = [(i, (i + k) % ranks) for i in range(heads)]
        w_blocks.append(lax.ppermute(sent, "ctx", pairs_k))
    d_wgate, d_wup, d_wdown = unpack_hidden(order_s[None], hidden_parts)
    d_wdown = d_wdown.T
    inv_one = lax.rsqrt(jnp.mean(x_own * x_own, axis=1, keepdims=True) + EPS)
    d_input = d_middle + norm_back(x_own, inv_one, gain_one, d_one)
    both = jnp.concatenate([d_input.astype(BF), result.astype(BF)], axis=1)
    both = spread_rows(both, tp_steps)
    both, w_blocks = lax.optimization_barrier((both, w_blocks))
    both = both.reshape(lanes, small, 2 * depth)
    both = jnp.take(both, natural, axis=0).reshape(span, 2 * depth)
    d_tokens, output = both[:, :depth], both[:, depth:]
    totals, one_sum, two_sum = jnp.sum(every[:4], axis=1), every[5] / gain_one, every[6]
    beta_sum, taps_sum = sums[7:7 + heads], sums[7 + heads:]
    d_beta = lax.dynamic_slice_in_dim(beta_sum, (shard * ranks + rank) * share, share, axis=1).T
    d_conv = taps_sum[:, :columns]
    d_w = unpack_heads(((rank - turn) % ranks)[None], w_blocks, heads)
    rms_stats = jnp.sqrt(totals / (jnp.maximum(every[4, 0], 1.0) * depth))
    return (
        output, d_tokens, one_sum, d_w[0], d_w[1], d_w[2], d_w[3], d_beta, d_conv,
        d_wout, two_sum, d_wgate, d_wup, d_wdown, rms_stats,
    )


def solution(mesh):
    rows = P(("shard", "ctx"), None)
    tiled = P(("shard", "ctx"), "tp")
    turned = P("tp", ("shard", "ctx"))
    placed = (
        rows, rows, P(("shard", "ctx")), P("shard", None), P("shard", None), P(),
        tiled, tiled, tiled, tiled, tiled, P(None, "tp"), turned, P(), tiled, tiled, turned,
    )
    return jax.shard_map(
        local,
        mesh=mesh,
        in_specs=placed,
        out_specs=(
            rows, rows, P(), tiled, tiled, tiled, tiled, tiled, P(None, "tp"),
            turned, P(), tiled, tiled, turned, P(),
        ),
        check_vma=False,
    )
```
